32 devices in a mesh: groups: 2 (over x), tile: 16 (over z, y, core).
Axes of the slice: x: 2, y: 2, z: 4, core: 2. Of those that a mesh axis runs over, the one named last changes fastest.
Arguments:
- coarse_solution: bfloat16 [32, 2, 4096], P(('groups', 'tile')), parts along dimension 0, may hold values from -6 to 6
- geometry: int32 [32, 4096], P(('groups', 'tile')), parts along dimension 0, may hold values 0 or 1
- fine_fields: bfloat16 [32, 3, 2, 2, 256, 256], P('groups', None, None, None, 'tile'), parts along dimension 0, may hold values from -6 to 6
- cotangent: bfloat16 [32, 3, 2, 2, 256, 256], P('groups', None, None, None, 'tile'), parts along dimension 0, may hold values from -0.046875 to 0.046875
- sample_ids: int32 [32], P('groups'), parts along dimension 0, may hold values from 0 to 15, each once
- first_weight: bfloat16 [3, 3, 3, 128], replicated, may hold values from -1.25 to 1.25
- dilated_weight: bfloat16 [3, 3, 128, 128], replicated, may hold values from -0.1875 to 0.1875
- project_weight: bfloat16 [128, 128], replicated, may hold values from -0.5 to 0.5
- down_weight: bfloat16 [3, 4, 4, 128], replicated, may hold values from -0.875 to 0.875
- up_weight: bfloat16 [4, 4, 6, 128], replicated, may hold values from -0.25 to 0.25
Outputs:
- prediction: bfloat16 [32, 3, 2, 2, 256, 256], P('groups', None, None, None, 'tile'), parts along dimension 0
- first_grad: float32 [6, 3, 3, 128], P('groups'), parts along dimension 0
- dilated_grad: float32 [6, 3, 128, 128], P('groups'), parts along dimension 0
- project_grad: float32 [256, 128], P('groups'), parts along dimension 0
- down_grad: float32 [6, 4, 4, 128], P('groups'), parts along dimension 0
- up_grad: float32 [8, 4, 6, 128], P('groups'), parts along dimension 0
The draws below stay inside these ranges and needn't reach their ends.
There are 2 independent parts, one for each index of `groups`. The reference program is written for one: setup_inputs(seed, part) draws one part's arguments, and reference() takes and returns one part's arrays. A program takes and returns all parts, laid end to end along the dimension named above; an argument that names none is the same for every part. Nothing has to cross between parts.
Inputs may be any that keep to these rules, and one draw needn't show every extreme that they name: `sample_ids`: every sample is named by exactly one of the 16 slots.
All inputs are finite; a program needn't handle non-finite values. No bound on the sum of `geometry` on one device may be relied on, other than what follows from the above.
Results may differ from the reference program's by a relative error of at most 0.0064.
Values may be sent and summed in bfloat16 or wider, within the bound.
No kernel may reach another device: no remote copies, remote signals or barrier semaphores. Data moves between devices by JAX's collectives and lax.ppermute only.
A program may use at most 256 MiB of HBM per device.

```python
import math
import jax
import jax.numpy as jnp
from jax import lax

CIN = 2
FIN = 3
CC = 128
FC = 128
CG = 64
SAMPLES = 16
FG = 512


def set_ends(values, rng, smallest, largest):
    index_at = [jax.random.randint(jax.random.fold_in(rng, axis), (), 0, length) for axis, length in enumerate(values.shape)]
    longest = values.shape.index(max(values.shape))
    beside = index_at[:longest] + [(index_at[longest] + 1) % values.shape[longest]] + index_at[longest + 1:]
    return values.at[tuple(index_at)].set(smallest).at[tuple(beside)].set(largest)


def steps_of(rng, dims, cuts, smallest, largest):
    level = 1.0
    for position, parts in cuts:
        draws = jax.random.uniform(jax.random.fold_in(jax.random.fold_in(rng, 6), position), (parts,), jnp.float32, smallest / len(cuts), largest / len(cuts))
        level = level * jnp.repeat(jnp.exp(draws), dims[position] // parts).reshape((-1,) + (1,) * (len(dims) - 1 - position))
    return level


def scatter_about(key, dims, scale, bound, shards=(), held_as=jnp.bfloat16):
    result = jax.random.normal(key, dims, jnp.float32) * scale
    if len(shards) > 0:
        result = steps_of(key, dims, shards, -0.22, 0.18) * result
    return jnp.clip(result, min=-bound, max=bound).astype(held_as)


def setup_inputs(seed: int = 0, part: int = 0) -> dict:
    arg_keys = jax.random.split(jax.random.key(seed), 11)
    own_keys = jax.random.split(jax.random.fold_in(arg_keys[10], part), 11)
    coarse_solution = scatter_about(own_keys[0], (SAMPLES, CIN, CG * CG), 1.0, 6.0, ((0, 16),))
    geometry = set_ends((jax.random.randint(own_keys[1], (SAMPLES, CG * CG), 0, 3) < 1).astype(jnp.int32), jax.random.fold_in(own_keys[1], 1), 0, 1)
    fine_fields = scatter_about(own_keys[2], (SAMPLES, FIN, 2, 2, FG // 2, FG // 2), 1.0, 6.0, ((4, 16),))
    cotangent = scatter_about(own_keys[3], (SAMPLES, FIN, 2, 2, FG // 2, FG // 2), (4 * FG ** -1), 0.046875, ((4, 16),))
    sample_ids = jax.random.permutation(own_keys[4], SAMPLES).astype(jnp.int32)
    first_weight = scatter_about(arg_keys[5], (CIN + 1, 3, 3, CC), (9 * (CIN + 1)) ** -0.5, 1.25)
    dilated_weight = scatter_about(arg_keys[6], (3, 3, CC, CC), (9 * CC) ** -0.5, 0.1875)
    project_weight = scatter_about(arg_keys[7], (CC, FC), CC ** -0.5, 0.5)
    down_weight = scatter_about(arg_keys[8], (FIN, 4, 4, FC), (16 * FIN) ** -0.5, 0.875)
    up_weight = scatter_about(arg_keys[9], (4, 4, 2 * FIN, FC), (4 * FC) ** -0.5, 0.25)
    return {"coarse_solution": coarse_solution, "geometry": geometry, "fine_fields": fine_fields, "cotangent": cotangent, "sample_ids": sample_ids, "first_weight": first_weight, "dilated_weight": dilated_weight, "project_weight": project_weight, "down_weight": down_weight, "up_weight": up_weight}


tap_table = ((-1, 1), (0, 0), (0, 1), (1, 0))

def gelu_slope(pre_act, upstream):
    unused, pull_back = jax.vjp(jax.nn.gelu, pre_act)
    return pull_back(upstream)[0]

def coarse_inputs(coarse_solution, geometry):
    samples = coarse_solution.shape[0]
    fields = coarse_solution.reshape(samples, CIN, CG, CG)
    metal = geometry.reshape(samples, 1, CG, CG).astype(jnp.bfloat16)
    return jnp.concatenate([fields, metal], axis=1)

def first_conv(inputs, first_weight):
    samples, channels = (inputs.shape[0], inputs.shape[1])
    padded = jnp.pad(inputs, ((0, 0), (0, 0), (2, 2), (2, 2)))
    pieces = [padded[:, :, 2 * row_tap:2 * row_tap + CG, 2 * col_tap:2 * col_tap + CG] for row_tap in range(3) for col_tap in range(3)]
    patches = jnp.swapaxes(jnp.stack(pieces, 0), 1, 2).reshape(9 * channels, samples, CG * CG)
    weight_mat = jnp.transpose(first_weight, (1, 2, 0, 3)).reshape(9 * channels, first_weight.shape[3])
    first_pre = lax.dot_general(patches, weight_mat, (((0,), (0,)), ((), ())), preferred_element_type=jnp.float32)
    return (first_pre.reshape(samples, CG, CG, first_weight.shape[3]), patches)

def first_back(patches, d_first, first_weight):
    samples = d_first.shape[0]
    flat = d_first.reshape(samples, CG * CG, d_first.shape[3])
    matrix = lax.dot_general(patches, flat, (((1, 2), (0, 1)), ((), ())), preferred_element_type=jnp.float32)
    return jnp.transpose(matrix.reshape(3, 3, first_weight.shape[0], first_weight.shape[3]), (2, 0, 1, 3))

def second_conv(first_hidden, dilated_weight):
    padded = jnp.pad(first_hidden, ((0, 0), (4, 4), (4, 4), (0, 0)))
    summed = jnp.zeros(first_hidden.shape[:3] + (dilated_weight.shape[3],), jnp.float32)
    for row_tap in range(3):
        for col_tap in range(3):
            window = padded[:, 4 * row_tap:4 * row_tap + CG, 4 * col_tap:4 * col_tap + CG, :]
            summed = summed + lax.dot_general(window, dilated_weight[row_tap, col_tap], (((3,), (0,)), ((), ())), preferred_element_type=jnp.float32)
    return summed

def second_back(first_hidden, d_second, dilated_weight):
    padded = jnp.pad(first_hidden, ((0, 0), (4, 4), (4, 4), (0, 0)))
    d_padded = jnp.zeros(padded.shape, jnp.float32)
    gradients = []
    for row_tap in range(3):
        for col_tap in range(3):
            window = padded[:, 4 * row_tap:4 * row_tap + CG, 4 * col_tap:4 * col_tap + CG, :]
            gradients.append(lax.dot_general(window, d_second, (((0, 1, 2), (0, 1, 2)), ((), ())), preferred_element_type=jnp.float32))
            back_term = lax.dot_general(d_second, dilated_weight[row_tap, col_tap], (((3,), (1,)), ((), ())), preferred_element_type=jnp.float32)
            d_padded = d_padded.at[:, 4 * row_tap:4 * row_tap + CG, 4 * col_tap:4 * col_tap + CG, :].add(back_term)
    dilated_grad = jnp.stack(gradients, 0).reshape(dilated_weight.shape)
    return (dilated_grad, d_padded[:, 4:4 + CG, 4:4 + CG, :])

def column_shift(array, shift):
    if shift == 0:
        return array
    width = array.shape[-1]
    edges = [(0, 0)] * (array.ndim - 1)
    if shift > 0:
        return jnp.pad(array[..., shift:], edges + [(0, shift)])
    return jnp.pad(array[..., :width + shift], edges + [(-shift, 0)])

def phase_patches(wide):
    rows = wide.shape[4] - 2
    pieces = []
    for row_tap in range(4):
        row_move, row_phase = tap_table[row_tap]
        for col_tap in range(4):
            col_move, col_phase = tap_table[col_tap]
            block = column_shift(wide[:, :, row_phase, col_phase, 1 + row_move:1 + row_move + rows, :], col_move)
            for channel in range(wide.shape[1]):
                pieces.append(block[:, channel])
    return jnp.stack(pieces, 0)

def down_conv(wide, down_weight):
    patches = phase_patches(wide)
    weight_mat = jnp.transpose(down_weight, (1, 2, 0, 3)).reshape(patches.shape[0], down_weight.shape[3])
    down_pre = lax.dot_general(patches, weight_mat, (((0,), (0,)), ((), ())), preferred_element_type=jnp.float32)
    return (down_pre, patches)

def down_layout(matrix, down_weight):
    shaped = matrix.reshape(4, 4, down_weight.shape[0], down_weight.shape[3])
    return jnp.transpose(shaped, (2, 0, 1, 3))

def add_coarse(down_pre, coarse_part):
    samples, fine_rows, fine_cols, channels = down_pre.shape
    coarse_rows, coarse_cols = (coarse_part.shape[1], coarse_part.shape[2])
    shaped = down_pre.reshape(samples, coarse_rows, fine_rows // coarse_rows, coarse_cols, fine_cols // coarse_cols, channels)
    return (shaped + coarse_part[:, :, None, :, None, :]).reshape(down_pre.shape)

def pool_cells(grad_pre, coarse_rows, coarse_cols):
    samples, fine_rows, fine_cols, channels = grad_pre.shape
    shaped = grad_pre.reshape(samples, coarse_rows, fine_rows // coarse_rows, coarse_cols, fine_cols // coarse_cols, channels)
    return lax.optimization_barrier(jnp.sum(shaped, axis=(2, 4), dtype=jnp.float32))

def up_phase(hidden, up_weight):
    samples, rows_in, cols_in, channels = hidden.shape
    outputs = up_weight.shape[2]
    weight_mat = up_weight.reshape(16 * outputs, channels)
    taps = lax.dot_general(weight_mat, hidden, (((1,), (3,)), ((), ())), preferred_element_type=jnp.float32)
    taps = taps.reshape(4, 4, outputs, samples, rows_in, cols_in)
    row_groups = []
    for row_phase in range(2):
        col_groups = []
        for col_phase in range(2):
            summed = jnp.zeros((outputs, samples, rows_in + 2, cols_in), jnp.float32)
            for row_tap in range(4):
                row_move, tap_row_phase = tap_table[row_tap]
                for col_tap in range(4):
                    col_move, tap_col_phase = tap_table[col_tap]
                    if tap_row_phase == row_phase and tap_col_phase == col_phase:
                        piece = column_shift(taps[row_tap, col_tap], -col_move)
                        summed = summed + jnp.pad(piece, ((0, 0), (0, 0), (1 + row_move, 1 - row_move), (0, 0)))
            col_groups.append(summed)
        row_groups.append(jnp.stack(col_groups, 0))
    layout = jnp.stack(row_groups, 0)
    return jnp.transpose(layout, (3, 2, 0, 1, 4, 5))

def earlier_rows(flux):
    paired = flux[:, :, 0] + flux[:, :, 1]
    inclusive = jnp.cumsum(paired, axis=3)
    exclusive = inclusive - paired
    return (jnp.stack([exclusive + flux[:, :, 0], inclusive], axis=2), inclusive[:, :, :, -1])

def later_rows(upstream):
    paired = upstream[:, :, 0] + upstream[:, :, 1]
    inclusive = jnp.flip(jnp.cumsum(jnp.flip(paired, 3), axis=3), 3)
    exclusive = inclusive - paired
    return (jnp.stack([inclusive, exclusive + upstream[:, :, 1]], axis=2), inclusive[:, :, :, 0])

def reference(coarse_solution, geometry, fine_fields, cotangent, sample_ids, first_weight, dilated_weight, project_weight, down_weight, up_weight):
    root_scale = 1.0 / math.sqrt(FG)
    half = FG // 2
    row_pad = ((0, 0), (0, 0), (0, 0), (0, 0), (1, 1), (0, 0))

    def one_slot(carry, slot_index):
        source = sample_ids[slot_index].astype(jnp.int32)
        inputs = coarse_inputs(lax.dynamic_slice_in_dim(coarse_solution, source, 1, 0), lax.dynamic_slice_in_dim(geometry, source, 1, 0))
        first_pre, first_patches = first_conv(inputs, first_weight)
        first_hidden = jax.nn.gelu(first_pre).astype(jnp.bfloat16)
        second_pre = second_conv(first_hidden, dilated_weight)
        feature = jax.nn.gelu(second_pre).astype(jnp.bfloat16)
        projected = lax.dot_general(feature, project_weight, (((3,), (0,)), ((), ())), preferred_element_type=jnp.float32)
        fine_one = lax.dynamic_slice_in_dim(fine_fields, slot_index, 1, 0)
        fine_wide = jnp.pad(fine_one, row_pad)
        down_pre, patches = down_conv(fine_wide, down_weight)
        third_pre = add_coarse(down_pre, projected)
        hidden = jax.nn.gelu(third_pre).astype(jnp.bfloat16)
        out_field = up_phase(hidden, up_weight)[:, :, :, :, 1:half + 1]
        running, unused_total = earlier_rows(out_field[:, FIN:])
        predicted = (out_field[:, :FIN] + running * root_scale).astype(jnp.bfloat16)
        upstream = lax.dynamic_slice_in_dim(cotangent, slot_index, 1, 0).astype(jnp.float32)
        behind, unused_lead = later_rows(upstream)
        slope_rows = jnp.concatenate([upstream, behind * root_scale], axis=1).astype(jnp.bfloat16)
        slope_patches = phase_patches(jnp.pad(slope_rows, row_pad))
        up_mat = up_weight.reshape(slope_patches.shape[0], up_weight.shape[3])
        d_hidden = lax.dot_general(slope_patches, up_mat, (((0,), (0,)), ((), ())), preferred_element_type=jnp.float32)
        up_part = lax.dot_general(slope_patches, hidden, (((1, 2, 3), (0, 1, 2)), ((), ())), preferred_element_type=jnp.float32).reshape(up_weight.shape)
        d_third = gelu_slope(third_pre, d_hidden).astype(jnp.bfloat16)
        down_part = down_layout(lax.dot_general(patches, d_third, (((1, 2, 3), (0, 1, 2)), ((), ())), preferred_element_type=jnp.float32), down_weight)
        d_project = pool_cells(d_third, CG, CG).astype(jnp.bfloat16)
        project_part = lax.dot_general(feature, d_project, (((0, 1, 2), (0, 1, 2)), ((), ())), preferred_element_type=jnp.float32)
        d_feature = lax.dot_general(d_project, project_weight, (((3,), (1,)), ((), ())), preferred_element_type=jnp.float32).astype(jnp.bfloat16)
        d_second = gelu_slope(second_pre, d_feature.astype(jnp.float32)).astype(jnp.bfloat16)
        dilated_part, d_first_hidden = second_back(first_hidden, d_second, dilated_weight)
        d_first = gelu_slope(first_pre, d_first_hidden).astype(jnp.bfloat16)
        first_part = first_back(first_patches, d_first, first_weight)
        updated = (carry[0] + first_part, carry[1] + dilated_part, carry[2] + project_part, carry[3] + down_part, carry[4] + up_part)
        return (updated, predicted[0])
    initial = (jnp.zeros(first_weight.shape, jnp.float32), jnp.zeros(dilated_weight.shape, jnp.float32), jnp.zeros(project_weight.shape, jnp.float32), jnp.zeros(down_weight.shape, jnp.float32), jnp.zeros(up_weight.shape, jnp.float32))
    sums, prediction = lax.scan(one_slot, initial, jnp.arange(SAMPLES, dtype=jnp.int32))
    return (prediction, sums[0], sums[1], sums[2], sums[3], sums[4])
```

```python
import math

import jax
import jax.numpy as jnp
import numpy as np
from jax import lax
from jax.experimental import pallas as pl
from jax.experimental.pallas import tpu as pltpu
from jax.sharding import PartitionSpec as P

CG = 64
FG = 512
HALF = FG // 2
SCALE = 1.0 / math.sqrt(FG)
GELU_A = math.sqrt(2.0 / math.pi)
GELU_B = GELU_A * 0.044715
BF = jnp.bfloat16
F32 = jnp.float32

AUX = 48
GRAD_ROWS = 1536
UP_AT, DOWN_AT, FIRST_AT, PROJECT_AT = 1280, 1376, 1424, 1152


def nn(a, b):
    return lax.dot_general(a, b, (((1,), (0,)), ((), ())), preferred_element_type=F32)


def nt(a, b):
    return lax.dot_general(a, b, (((1,), (1,)), ((), ())), preferred_element_type=F32)


def exact(a, b):
    return lax.dot_general(
        a, b, (((1,), (0,)), ((), ())), precision=lax.Precision.HIGHEST, preferred_element_type=F32
    )


def row_at(tap, r):
    if tap == 0:
        return 8 if r == 0 else 4 + r - 1
    if tap == 1:
        return r
    if tap == 2:
        return 4 + r
    return 9 if r == 3 else r + 1


def fine_row(block, index):
    if index == 8:
        return 8 * block - 1
    if index == 9:
        return 8 * block + 8
    return 8 * block + 2 * (index % 4) + index // 4


COL_GROUP = (2, 0, 1, 3)


def constants(rows):
    blocks = rows // 4
    last = 2 * rows
    width = 12 * rows + AUX

    def held(ch, q, o):
        return ((ch * 2 + o % 2) * 2 + q) * rows + o // 2

    sel_x = np.zeros((blocks, 2, 32, width), np.float32)
    sel_s = np.zeros((blocks, 2, 64, width), np.float32)
    sel_o = np.zeros((12 * rows + 32, blocks, 2, 64), np.float32)
    base = 12 * rows
    for b in range(blocks):
        for q in range(2):
            for ch in range(3):
                for index in range(10):
                    o = fine_row(b, index)
                    at = ch * 10 + index
                    if o == -1:
                        sel_x[b, q, at, base + ch * 2 + q] = 1
                        sel_s[b, q, at, base + 6 + ch * 2 + q] = 1
                        sel_s[b, q, 32 + at, base + 6 + ch * 2 + q] = 1
                    elif o == last:
                        sel_x[b, q, at, base + 16 + ch * 2 + q] = 1
                        sel_s[b, q, at, base + 22 + ch * 2 + q] = 1
                    else:
                        sel_x[b, q, at, held(ch, q, o)] = 1
                        sel_s[b, q, at, held(ch, q, o)] = 1
                    for later in range(max(o, 0), last):
                        sel_s[b, q, 32 + at, held(ch, q, later)] = 1
                    sel_s[b, q, 32 + at, base + 32 + ch * 2 + q] = 1
                    sel_s[b, q, 32 + at, base + 40 + ch * 2 + q] = 1
                    for target in range(max(o, 0), last):
                        if target == o:
                            sel_o[held(ch, q, target), b, q, at] = 1
                        if o >= 0:
                            sel_o[held(ch, q, target), b, q, 32 + at] = 1
                    if o == -1:
                        sel_o[base + ch * 2 + q, b, q, at] = 1
                        sel_o[base + 6 + ch * 2 + q, b, q, 32 + at] = 1
                    else:
                        sel_o[base + 18 + ch * 2 + q, b, q, 32 + at] = 1
                    if o == last:
                        sel_o[base + 12 + ch * 2 + q, b, q, at] = 1
    sel_s_first = sel_s.copy()
    for q in range(2):
        for ch in range(3):
            sel_s_first[0, q, 32 + ch * 10 + 8] = 0
    ex = np.zeros((4, 128, 48), np.float32)
    eu = np.zeros((4, 256, 96), np.float32)
    for r in range(4):
        for i in range(4):
            for j in range(4):
                for ch in range(3):
                    ex[r, COL_GROUP[j] * 32 + ch * 10 + row_at(i, r), (ch * 4 + i) * 4 + j] = 1
                for k in range(6):
                    at = COL_GROUP[j] * 64 + (k // 3) * 32 + (k % 3) * 10 + row_at(i, r)
                    eu[r, at, (i * 4 + j) * 6 + k] = 1
    ef = np.zeros((80, 32), np.float32)
    for ch in range(3):
        for tap in range(9):
            ef[tap * 8 + ch, ch * 9 + tap] = 1
    pool = np.zeros((CG, HALF), np.float32)
    for c in range(HALF):
        pool[c // 4, c] = 1
    spread = np.zeros((blocks, CG, blocks, HALF), np.float32)
    for a in range(blocks):
        spread[a, :, a, :] = pool
    return dict(
        sel_x=sel_x.reshape(blocks * 64, width),
        sel_s=sel_s.reshape(blocks * 128, width),
        sel_s_first=sel_s_first.reshape(blocks * 128, width),
        sel_o=sel_o.reshape(12 * rows + 32, blocks * 128),
        ex=ex.reshape(512, 48),
        eu=eu.reshape(1024, 96),
        ext=np.concatenate(list(np.swapaxes(ex, 1, 2)), 0),
        eut=np.concatenate(list(np.swapaxes(eu, 1, 2)), 0),
        ef=ef,
        eft=ef.T,
        pool=pool,
        spread=spread.reshape(blocks * CG, blocks * HALF),
    )


def gelu_both(pre):
    square = pre * pre
    t = jnp.tanh(pre * (GELU_B * square + GELU_A))
    gate = 0.5 + 0.5 * t
    value = pre * gate
    slope = gate + (value * (1.0 - gate)) * (6.0 * GELU_B * square + 2.0 * GELU_A)
    return value, slope


def moved(value, shift, lane, keep):
    width = value.shape[1]
    return jnp.where(keep(lane), pltpu.roll(value, shift % width, 1), 0.0)


def slot_kernel(
    blocks,
    ids_ref,
    tile_ref,
    coarse_ref,
    fine_ref,
    cot_ref,
    before_ref,
    after_ref,
    later_ref,
    sel_x_ref,
    sel_s_ref,
    sel_o_ref,
    ex_ref,
    eu_ref,
    ext_ref,
    eut_ref,
    ef_ref,
    eft_ref,
    pool_ref,
    spread_ref,
    first_t_ref,
    second_t_ref,
    second_ref,
    project_ref,
    project_t_ref,
    down_t_ref,
    up_t_ref,
    up_ref,
    pred_ref,
    edge_ref,
    out_ref,
    grad_ref,
    w_ref,
    u_ref,
    ut_ref,
    w1_ref,
    gu_ref,
    gd_ref,
    fg_ref,
):
    step = pl.program_id(0)
    cells = blocks * CG
    tile = tile_ref[0]

    @pl.when(step == 0)
    def _():
        for r in range(4):
            rows = slice(r * 128, (r + 1) * 128)
            w_ref[rows, 0:128] = nt(down_t_ref[...], ex_ref[rows, :]).astype(BF)
            w_ref[rows, 128:256] = project_t_ref[...]
            taps = eu_ref[r * 256 : (r + 1) * 256, :]
            u_ref[rows, :] = nt(up_t_ref[...], taps).astype(BF)
            ut_ref[:, rows] = nn(taps, up_ref[...]).astype(BF)
        w1_ref[...] = nt(first_t_ref[...], ef_ref[...]).astype(BF)
        gu_ref[...] = jnp.zeros_like(gu_ref)
        gd_ref[...] = jnp.zeros_like(gd_ref)
        fg_ref[...] = jnp.zeros_like(fg_ref)
        grad_ref[...] = jnp.zeros_like(grad_ref)

    inputs = jnp.concatenate([coarse_ref[0], jnp.zeros((5, coarse_ref.shape[2]), F32)], axis=0)
    lane_in = lax.broadcasted_iota(jnp.int32, inputs.shape, 1) % CG
    by_col = (
        moved(inputs, 2, lane_in, lambda x: x >= 2),
        inputs,
        moved(inputs, -2, lane_in, lambda x: x < CG - 2),
    )
    above = jnp.where(tile * blocks >= 4, 1.0, 0.0)
    below = jnp.where(tile * blocks + 4 <= CG - blocks, 1.0, 0.0)
    windows = []
    for window in range(3):
        pieces = []
        for row_tap in range(3):
            for col_tap in range(3):
                start = (4 * window + 2 * row_tap) * CG
                pieces.append(by_col[col_tap][:, start : start + cells])
        pieces.append(jnp.zeros((8, cells), F32))
        stacked = jnp.concatenate(pieces, axis=0)
        if window == 0:
            stacked = stacked * above
        if window == 2:
            stacked = stacked * below
        windows.append(stacked)
    patches = jnp.concatenate(windows, axis=1).astype(BF)
    first_value, first_slope = gelu_both(nn(w1_ref[...], patches))
    lane_h = lax.broadcasted_iota(jnp.int32, first_value.shape, 1) % CG
    first_value = first_value.astype(BF).astype(F32)
    hidden_by_col = (
        moved(first_value, 4, lane_h, lambda x: x >= 4).astype(BF),
        first_value.astype(BF),
        moved(first_value, -4, lane_h, lambda x: x < CG - 4).astype(BF),
    )
    columns = jnp.concatenate(
        [
            hidden_by_col[col_tap][:, window * cells : (window + 1) * cells]
            for window in range(3)
            for col_tap in range(3)
        ],
        axis=0,
    )
    second_value, second_slope = gelu_both(nn(second_t_ref[...], columns))
    feature = second_value.astype(BF)
    feature_wide = nn(feature, spread_ref[...]).astype(BF)

    later = later_ref[0]
    later_high = later.astype(BF).astype(F32)
    later_both = jnp.concatenate([later_high, later - later_high], axis=0).astype(BF)
    aux = [before_ref[0], after_ref[0], later_both]
    fine_all = nn(sel_x_ref[...], jnp.concatenate([fine_ref[0]] + aux, axis=0))
    slope_all = nn(sel_s_ref[...], jnp.concatenate([cot_ref[0]] + aux, axis=0))
    row = lax.broadcasted_iota(jnp.int32, (64, HALF), 0)
    flux_scale = jnp.where(row >= 32, SCALE, 1.0)
    lane32 = lax.broadcasted_iota(jnp.int32, (32, HALF), 1)
    lane64 = lax.broadcasted_iota(jnp.int32, (64, HALF), 1)
    not_first = lambda x: x >= 1
    not_last = lambda x: x < HALF - 1

    def enter(b):
        x0 = fine_all[b * 64 : b * 64 + 32]
        x1 = fine_all[b * 64 + 32 : b * 64 + 64]
        x_taps = jnp.concatenate(
            [x0, x1, moved(x1, 1, lane32, not_first), moved(x0, -1, lane32, not_last)], axis=0
        ).astype(BF)
        s0 = slope_all[b * 128 : b * 128 + 64] * flux_scale
        s1 = slope_all[b * 128 + 64 : b * 128 + 128] * flux_scale
        s_taps = jnp.concatenate(
            [s0, s1, moved(s1, 1, lane64, not_first), moved(s0, -1, lane64, not_last)], axis=0
        ).astype(BF)
        third = nn(
            w_ref[...],
            jnp.concatenate([x_taps, feature_wide[:, b * HALF : (b + 1) * HALF]], axis=0),
        )
        return x_taps, s_taps, third, nn(u_ref[...], s_taps)

    def middle(entered):
        x_taps, s_taps, third, d_hidden = entered
        value, slope = gelu_both(third)
        return x_taps, s_taps, value.astype(BF), (d_hidden * slope).astype(BF)

    def leave(held):
        x_taps, s_taps, hidden, d_third = held
        taps = nn(ut_ref[...], hidden)
        c0 = taps[0:64] + moved(taps[192:256], 1, lane64, not_first)
        c1 = taps[64:128] + moved(taps[128:192], -1, lane64, not_last)
        gu_ref[...] += nt(s_taps, hidden)
        both = nt(jnp.concatenate([x_taps, pool_ref[...]], axis=0), d_third)
        gd_ref[...] += both[0:128]
        per_row = both[128:192]
        cells_sum = (per_row[:, 0:128] + per_row[:, 128:256]) + (
            per_row[:, 256:384] + per_row[:, 384:512]
        )
        return [c0 * flux_scale, c1 * flux_scale], cells_sum

    combined = []
    pooled = []
    entered = {}
    held = {}
    for turn in range(blocks + 2):
        if turn < blocks:
            entered[turn] = enter(turn)
        if 0 <= turn - 1 < blocks:
            held[turn - 1] = middle(entered.pop(turn - 1))
        if turn - 2 >= 0:
            pair, cells_sum = leave(held.pop(turn - 2))
            combined += pair
            pooled.append(cells_sum)

    out = jnp.concatenate(combined, axis=0)
    out_high = out.astype(BF)
    out_low = (out - out_high.astype(F32)).astype(BF)
    placed = nn(sel_o_ref[...], out_high) + nn(sel_o_ref[...], out_low)
    main = pred_ref.shape[1]
    pred_ref[0] = placed[0:main]
    edge_ref[0] = placed[main : main + 32]

    d_project = jnp.concatenate(pooled, axis=0).astype(BF)
    grad_ref[PROJECT_AT : PROJECT_AT + 128, :] += nn(feature, d_project)
    d_feature = nt(project_ref[...], d_project).astype(BF).astype(F32)
    d_second = (d_feature * second_slope).astype(BF)
    grad_ref[0:1152, :] += nt(columns, d_second)
    back = nn(second_ref[...], d_second)
    lane_c = lax.broadcasted_iota(jnp.int32, (128, cells), 1) % CG
    parts = []
    for window in range(3):
        at = window * 384
        parts.append(
            back[at + 128 : at + 256]
            + moved(back[at : at + 128], -4, lane_c, lambda x: x < CG - 4)
            + moved(back[at + 256 : at + 384], 4, lane_c, lambda x: x >= 4)
        )
    d_first = (jnp.concatenate(parts, axis=1) * first_slope).astype(BF)
    fg_ref[...] += nt(patches, d_first)

    @pl.when(step == pl.num_programs(0) - 1)
    def _():
        up = jnp.zeros((96, 128), F32)
        down = jnp.zeros((48, 128), F32)
        for r in range(4):
            lanes = slice(r * 128, (r + 1) * 128)
            up = up + exact(eut_ref[r * 96 : (r + 1) * 96, :], gu_ref[:, lanes])
            down = down + exact(ext_ref[r * 48 : (r + 1) * 48, :], gd_ref[:, lanes])
        grad_ref[UP_AT : UP_AT + 96, :] = up
        grad_ref[DOWN_AT : DOWN_AT + 48, :] = down
        grad_ref[FIRST_AT : FIRST_AT + 32, :] = exact(eft_ref[...], fg_ref[...])
        out_ref[...] = grad_ref[...].astype(BF)


def run_slots(ids, tile, coarse, fine, cot, before, after, later, fixed, weights):
    slots, main, width = fine.shape
    blocks = main // 48

    def whole(array):
        return pl.BlockSpec(array.shape, lambda n, ids, tile: (0,) * array.ndim)

    def per_slot(array):
        return pl.BlockSpec((1,) + array.shape[1:], lambda n, ids, tile: (n, 0, 0))

    in_specs = [
        pl.BlockSpec((1,) + coarse.shape[1:], lambda n, ids, tile: (ids[n], 0, 0)),
        per_slot(fine),
        per_slot(cot),
        per_slot(before),
        per_slot(after),
        per_slot(later),
    ] + [whole(a) for a in fixed + weights]
    grid_spec = pltpu.PrefetchScalarGridSpec(
        num_scalar_prefetch=2,
        grid=(slots,),
        in_specs=in_specs,
        out_specs=[
            pl.BlockSpec((1, main, width), lambda n, ids, tile: (n, 0, 0)),
            pl.BlockSpec((1, 32, width), lambda n, ids, tile: (n, 0, 0)),
            pl.BlockSpec((GRAD_ROWS, 128), lambda n, ids, tile: (0, 0)),
        ],
        scratch_shapes=[
            pltpu.VMEM((GRAD_ROWS, 128), F32),
            pltpu.VMEM((512, 256), BF),
            pltpu.VMEM((512, 256), BF),
            pltpu.VMEM((256, 512), BF),
            pltpu.VMEM((128, 80), BF),
            pltpu.VMEM((256, 512), F32),
            pltpu.VMEM((128, 512), F32),
            pltpu.VMEM((80, 128), F32),
        ],
    )

    def body(*refs):
        slot_kernel(blocks, *refs)

    return pl.pallas_call(
        body,
        grid_spec=grid_spec,
        out_shape=[
            jax.ShapeDtypeStruct((slots, main, width), F32),
            jax.ShapeDtypeStruct((slots, 32, width), F32),
            jax.ShapeDtypeStruct((GRAD_ROWS, 128), BF),
        ],
        compiler_params=pltpu.CompilerParams(vmem_limit_bytes=52 * 1024 * 1024),
        cost_estimate=pl.CostEstimate(
            flops=slots * blocks * 500_000_000, bytes_accessed=16_000_000, transcendentals=0
        ),
    )(ids, tile, coarse, fine, cot, before, after, later, *fixed, *weights)


def exchanged(value):
    return lax.all_to_all(value, "tile", split_axis=0, concat_axis=0, tiled=True)


def local(
    coarse_solution,
    geometry,
    fine_fields,
    cotangent,
    sample_ids,
    first_weight,
    dilated_weight,
    project_weight,
    down_weight,
    up_weight,
):
    peers = lax.axis_size("tile")
    position = lax.axis_index("tile")
    slots, rows = fine_fields.shape[0], fine_fields.shape[4]
    blocks = rows // 4
    up = [(i, i + 1) for i in range(peers - 1)]
    down = [(i + 1, i) for i in range(peers - 1)]

    totals = jnp.sum(cotangent.astype(F32), axis=(2, 4)).reshape(slots, 6, HALF)
    totals = jnp.pad(totals, ((0, 0), (0, 2), (0, 0)))
    mine = coarse_solution.shape[0]
    inputs = jnp.concatenate([coarse_solution.astype(F32), geometry.astype(F32)[:, None]], axis=1)
    padded = jnp.pad(inputs, ((0, 0), (0, 0), (6 * CG, 6 * CG)))
    span = (blocks + 12) * CG
    windows = jnp.stack(
        [padded[:, :, t * blocks * CG : t * blocks * CG + span] for t in range(peers)], 0
    )
    sent = jnp.concatenate(
        [
            windows.reshape(peers, mine * 3 * span),
            totals.reshape(peers, (slots // peers) * 8 * HALF),
        ],
        axis=1,
    )
    got = exchanged(sent)
    coarse = got[:, : mine * 3 * span].reshape(peers * mine, 3, span)
    sums = got[:, mine * 3 * span :]
    order = lax.broadcasted_iota(jnp.int32, (peers, peers), 0)
    other = lax.broadcasted_iota(jnp.int32, (peers, peers), 1)
    behind = jnp.sum(jnp.where((other > order)[:, :, None], sums[None], 0.0), axis=1)
    later = exchanged(behind).reshape(slots, 8, HALF)

    blank = jnp.zeros((slots, 4, HALF), BF)
    edge_last = jnp.concatenate(
        [
            fine_fields[:, :, 1, :, -1].reshape(slots, 6, HALF),
            cotangent[:, :, 1, :, -1].reshape(slots, 6, HALF),
            blank,
        ],
        axis=1,
    )
    edge_first = jnp.concatenate(
        [
            fine_fields[:, :, 0, :, 0].reshape(slots, 6, HALF),
            cotangent[:, :, 0, :, 0].reshape(slots, 6, HALF),
            blank,
        ],
        axis=1,
    )
    from_before = lax.ppermute(edge_last, "tile", up)
    from_after = lax.ppermute(edge_first, "tile", down)

    made = constants(rows)
    sel_s = jnp.where(
        position == 0, jnp.asarray(made["sel_s_first"], BF), jnp.asarray(made["sel_s"], BF)
    )
    fixed = [
        jnp.asarray(made["sel_x"], BF),
        sel_s,
        jnp.asarray(made["sel_o"], BF),
        jnp.asarray(made["ex"], BF),
        jnp.asarray(made["eu"], BF),
        jnp.asarray(made["ext"], F32),
        jnp.asarray(made["eut"], F32),
        jnp.asarray(made["ef"], BF),
        jnp.asarray(made["eft"], F32),
        jnp.asarray(made["pool"], BF),
        jnp.asarray(made["spread"], BF),
    ]
    second = dilated_weight.reshape(1152, 128)
    up_flat = up_weight.reshape(96, 128)
    weights = [
        jnp.pad(first_weight.reshape(27, 128), ((0, 5), (0, 0))).T,
        second.T,
        second,
        project_weight,
        project_weight.T,
        down_weight.reshape(48, 128).T,
        up_flat.T,
        up_flat,
    ]
    pred_local, edges, grads = run_slots(
        sample_ids,
        position.reshape(1).astype(jnp.int32),
        coarse,
        fine_fields.reshape(slots, 12 * rows, HALF),
        cotangent.reshape(slots, 12 * rows, HALF),
        from_before,
        from_after,
        later,
        fixed,
        weights,
    )

    before_flux = jnp.where(position >= 1, edges[:, 6:12], 0.0)
    flux = edges[:, 18:24] + before_flux
    chunk = GRAD_ROWS // peers
    extra = (slots // peers) * 12

    def halves(value):
        high = lax.reduce_precision(value, 8, 7)
        return [high.astype(BF), (value - high).astype(BF)]

    sent = jnp.concatenate(
        [grads.reshape(peers, chunk, 128)] + halves(flux.reshape(peers, extra, 128)), axis=1
    )
    got = exchanged(sent).astype(F32)
    to_first = lax.ppermute(edges[:, 12:18], "tile", up)
    to_last = lax.ppermute(edges[:, 0:6] + edges[:, 6:12], "tile", down)
    reduced = jnp.sum(got[:, :chunk], axis=0).astype(BF)
    sums = got[:, chunk : chunk + extra] + got[:, chunk + extra :]
    ahead = jnp.sum(jnp.where((other < order)[:, :, None, None], sums[None], 0.0), axis=1)
    reduced, to_first, to_last = lax.optimization_barrier((reduced, to_first, to_last))
    back = exchanged(
        jnp.concatenate(
            [jnp.broadcast_to(reduced, (peers, chunk, 128))] + halves(ahead), axis=1
        )
    )
    total = back[:, :chunk].reshape(GRAD_ROWS, 128).astype(F32)
    ahead = back[:, chunk : chunk + extra].astype(F32) + back[:, chunk + extra :].astype(F32)
    base = ahead.reshape(slots, 6, HALF) + before_flux

    shape = (slots, 3, 2, 2, rows, HALF)
    half_row = lax.broadcasted_iota(jnp.int32, shape, 2)
    fine_row_at = lax.broadcasted_iota(jnp.int32, shape, 4)

    def over_rows(value):
        return value.reshape(slots, 3, 1, 2, 1, HALF)

    prediction = (
        pred_local.reshape(shape)
        + over_rows(base)
        + jnp.where((half_row == 0) & (fine_row_at == 0), over_rows(to_first), 0.0)
        + jnp.where((half_row == 1) & (fine_row_at == rows - 1), over_rows(to_last), 0.0)
    ).astype(BF)
    return (
        prediction,
        total[FIRST_AT : FIRST_AT + 27].reshape(first_weight.shape),
        total[0:1152].reshape(dilated_weight.shape),
        total[PROJECT_AT : PROJECT_AT + 128],
        total[DOWN_AT : DOWN_AT + 48].reshape(down_weight.shape),
        total[UP_AT : UP_AT + 96].reshape(up_weight.shape),
    )


def solution(mesh):
    in_specs = (
        P(("groups", "tile"), None, None),
        P(("groups", "tile"), None),
        P("groups", None, None, None, "tile", None),
        P("groups", None, None, None, "tile", None),
        P("groups"),
        P(),
        P(),
        P(),
        P(),
        P(),
    )
    out_specs = (
        P("groups", None, None, None, "tile", None),
        P("groups", None, None, None),
        P("groups", None, None, None),
        P("groups", None),
        P("groups", None, None, None),
        P("groups", None, None, None),
    )
    return jax.shard_map(local, mesh=mesh, in_specs=in_specs, out_specs=out_specs, check_vma=False)
```

```python
import math

import jax
import jax.numpy as jnp
import numpy as np
from jax import lax
from jax.experimental import pallas as pl
from jax.experimental.pallas import tpu as pltpu
from jax.sharding import PartitionSpec as P

CG = 64
FG = 512
HALF = FG // 2
SCALE = 1.0 / math.sqrt(FG)
GELU_A = math.sqrt(2.0 / math.pi)
GELU_B = GELU_A * 0.044715
BF = jnp.bfloat16
F32 = jnp.float32

AUX = 48
GRAD_ROWS = 1536
UP_AT, DOWN_AT, FIRST_AT, PROJECT_AT = 1280, 1376, 1424, 1152


def nn(a, b):
    return lax.dot_general(a, b, (((1,), (0,)), ((), ())), preferred_element_type=F32)


def nt(a, b):
    return lax.dot_general(a, b, (((1,), (1,)), ((), ())), preferred_element_type=F32)


def exact(a, b):
    return lax.dot_general(
        a, b, (((1,), (0,)), ((), ())), precision=lax.Precision.HIGHEST, preferred_element_type=F32
    )


def row_at(tap, r):
    if tap == 0:
        return 8 if r == 0 else 4 + r - 1
    if tap == 1:
        return r
    if tap == 2:
        return 4 + r
    return 9 if r == 3 else r + 1


def fine_row(block, index):
    if index == 8:
        return 8 * block - 1
    if index == 9:
        return 8 * block + 8
    return 8 * block + 2 * (index % 4) + index // 4


COL_GROUP = (2, 0, 1, 3)


def constants(rows):
    blocks = rows // 4
    last = 2 * rows
    width = 12 * rows + AUX

    def held(ch, q, o):
        return ((ch * 2 + o % 2) * 2 + q) * rows + o // 2

    sel_x = np.zeros((blocks, 2, 32, width), np.float32)
    sel_s = np.zeros((blocks, 2, 64, width), np.float32)
    sel_o = np.zeros((12 * rows + 32, blocks, 2, 64), np.float32)
    base = 12 * rows
    for b in range(blocks):
        for q in range(2):
            for ch in range(3):
                for index in range(10):
                    o = fine_row(b, index)
                    at = ch * 10 + index
                    if o == -1:
                        sel_x[b, q, at, base + ch * 2 + q] = 1
                        sel_s[b, q, at, base + 6 + ch * 2 + q] = 1
                        sel_s[b, q, 32 + at, base + 6 + ch * 2 + q] = 1
                    elif o == last:
                        sel_x[b, q, at, base + 16 + ch * 2 + q] = 1
                        sel_s[b, q, at, base + 22 + ch * 2 + q] = 1
                    else:
                        sel_x[b, q, at, held(ch, q, o)] = 1
                        sel_s[b, q, at, held(ch, q, o)] = 1
                    for later in range(max(o, 0), last):
                        sel_s[b, q, 32 + at, held(ch, q, later)] = 1
                    sel_s[b, q, 32 + at, base + 32 + ch * 2 + q] = 1
                    sel_s[b, q, 32 + at, base + 40 + ch * 2 + q] = 1
                    for target in range(max(o, 0), last):
                        if target == o:
                            sel_o[held(ch, q, target), b, q, at] = 1
                        if o >= 0:
                            sel_o[held(ch, q, target), b, q, 32 + at] = 1
                    if o == -1:
                        sel_o[base + ch * 2 + q, b, q, at] = 1
                        sel_o[base + 8 + ch * 2 + q, b, q, 32 + at] = 1
                    else:
                        sel_o[base + 24 + ch * 2 + q, b, q, 32 + at] = 1
                    if o == last:
                        sel_o[base + 16 + ch * 2 + q, b, q, at] = 1
    sel_s_first = sel_s.copy()
    for q in range(2):
        for ch in range(3):
            sel_s_first[0, q, 32 + ch * 10 + 8] = 0
    ex = np.zeros((4, 128, 48), np.float32)
    eu = np.zeros((4, 256, 96), np.float32)
    for r in range(4):
        for i in range(4):
            for j in range(4):
                for ch in range(3):
                    ex[r, COL_GROUP[j] * 32 + ch * 10 + row_at(i, r), (ch * 4 + i) * 4 + j] = 1
                for k in range(6):
                    at = COL_GROUP[j] * 64 + (k // 3) * 32 + (k % 3) * 10 + row_at(i, r)
                    eu[r, at, (i * 4 + j) * 6 + k] = 1
    ef = np.zeros((80, 32), np.float32)
    for ch in range(3):
        for tap in range(9):
            ef[tap * 8 + ch, ch * 9 + tap] = 1
    pool = np.zeros((CG, HALF), np.float32)
    for c in range(HALF):
        pool[c // 4, c] = 1
    spread = np.zeros((blocks, CG, blocks, HALF), np.float32)
    for a in range(blocks):
        spread[a, :, a, :] = pool
    return dict(
        sel_x=sel_x.reshape(blocks * 64, width),
        sel_s=sel_s.reshape(blocks * 128, width),
        sel_s_first=sel_s_first.reshape(blocks * 128, width),
        sel_o=sel_o.reshape(12 * rows + 32, blocks * 128),
        ex=ex.reshape(512, 48),
        eu=eu.reshape(1024, 96),
        ext=np.concatenate(list(np.swapaxes(ex, 1, 2)), 0),
        eut=np.concatenate(list(np.swapaxes(eu, 1, 2)), 0),
        ef=ef,
        eft=ef.T,
        pool=pool,
        spread=spread.reshape(blocks * CG, blocks * HALF),
    )


def gelu_both(pre):
    square = pre * pre
    t = jnp.tanh(pre * (GELU_B * square + GELU_A))
    gate = 0.5 + 0.5 * t
    value = pre * gate
    slope = gate + (value * (1.0 - gate)) * (6.0 * GELU_B * square + 2.0 * GELU_A)
    return value, slope


def moved(value, shift, lane, keep):
    width = value.shape[1]
    return jnp.where(keep(lane), pltpu.roll(value, shift % width, 1), 0.0)


def coarse_forward(blocks, tile, coarse_ref, w1_ref, second_t_ref, spread_ref, store, place):
    patches_s, columns_s, first_slope_s, second_slope_s, feature_s, wide_s = store
    cells = blocks * CG
    inputs = jnp.concatenate([coarse_ref[0], jnp.zeros((5, coarse_ref.shape[2]), F32)], axis=0)
    lane_in = lax.broadcasted_iota(jnp.int32, inputs.shape, 1) % CG
    by_col = (
        moved(inputs, 2, lane_in, lambda x: x >= 2),
        inputs,
        moved(inputs, -2, lane_in, lambda x: x < CG - 2),
    )
    above = jnp.where(tile * blocks >= 4, 1.0, 0.0)
    below = jnp.where(tile * blocks + 4 <= CG - blocks, 1.0, 0.0)
    windows = []
    for window in range(3):
        pieces = []
        for row_tap in range(3):
            for col_tap in range(3):
                start = (4 * window + 2 * row_tap) * CG
                pieces.append(by_col[col_tap][:, start : start + cells])
        pieces.append(jnp.zeros((8, cells), F32))
        stacked = jnp.concatenate(pieces, axis=0)
        if window == 0:
            stacked = stacked * above
        if window == 2:
            stacked = stacked * below
        windows.append(stacked)
    patches = jnp.concatenate(windows, axis=1).astype(BF)
    first_value, first_slope = gelu_both(nn(w1_ref[...], patches))
    yield
    lane_h = lax.broadcasted_iota(jnp.int32, first_value.shape, 1) % CG
    first_value = first_value.astype(BF).astype(F32)
    hidden_by_col = (
        moved(first_value, 4, lane_h, lambda x: x >= 4).astype(BF),
        first_value.astype(BF),
        moved(first_value, -4, lane_h, lambda x: x < CG - 4).astype(BF),
    )
    columns = jnp.concatenate(
        [
            hidden_by_col[col_tap][:, window * cells : (window + 1) * cells]
            for window in range(3)
            for col_tap in range(3)
        ],
        axis=0,
    )
    second_value, second_slope = gelu_both(nn(second_t_ref[...], columns))
    yield
    feature = second_value.astype(BF)
    patches_s[place] = patches
    columns_s[place] = columns
    first_slope_s[place] = first_slope
    second_slope_s[place] = second_slope
    feature_s[place] = feature
    wide_s[place] = nn(feature, spread_ref[...]).astype(BF)


def coarse_backward(blocks, d_project, project_ref, second_ref, store, place, grad_ref, fg_ref):
    patches_s, columns_s, first_slope_s, second_slope_s, feature_s, _ = store
    cells = blocks * CG
    grad_ref[PROJECT_AT : PROJECT_AT + 128, :] += nn(feature_s[place], d_project)
    d_feature = nt(project_ref[...], d_project).astype(BF).astype(F32)
    d_second = (d_feature * second_slope_s[place]).astype(BF)
    yield
    grad_ref[0:1152, :] += nt(columns_s[place], d_second)
    back = nn(second_ref[...], d_second)
    yield
    lane_c = lax.broadcasted_iota(jnp.int32, (128, cells), 1) % CG
    parts = []
    for window in range(3):
        at = window * 384
        parts.append(
            back[at + 128 : at + 256]
            + moved(back[at : at + 128], -4, lane_c, lambda x: x < CG - 4)
            + moved(back[at + 256 : at + 384], 4, lane_c, lambda x: x >= 4)
        )
    d_first = (jnp.concatenate(parts, axis=1) * first_slope_s[place]).astype(BF)
    fg_ref[...] += nt(patches_s[place], d_first)


def advance(stage):
    next(stage, None)


def finish(stage):
    for _ in stage:
        pass


def slot_kernel(
    blocks,
    peers,
    ids_ref,
    tile_ref,
    coarse_first_ref,
    coarse_ref,
    fine_ref,
    cot_ref,
    before_ref,
    after_ref,
    later_ref,
    sel_x_ref,
    sel_s_ref,
    sel_o_ref,
    ex_ref,
    eu_ref,
    ext_ref,
    eut_ref,
    ef_ref,
    eft_ref,
    pool_ref,
    spread_ref,
    first_t_ref,
    second_t_ref,
    second_ref,
    project_ref,
    project_t_ref,
    down_t_ref,
    up_t_ref,
    up_ref,
    pred_ref,
    to_last_ref,
    to_first_ref,
    own_ref,
    sent_ref,
    grad_ref,
    w_ref,
    u_ref,
    ut_ref,
    w1_ref,
    gu_ref,
    gd_ref,
    fg_ref,
    d_project_ref,
    *store,
):
    step = pl.program_id(0)
    tile = tile_ref[0]
    now = lax.rem(step, 3)
    soon = lax.rem(step + 1, 3)
    done = lax.rem(step + 2, 3)

    def forward(source, place):
        return coarse_forward(
            blocks, tile, source, w1_ref, second_t_ref, spread_ref, store, place
        )

    def backward(place):
        return coarse_backward(
            blocks, d_project_ref[...], project_ref, second_ref, store, place, grad_ref, fg_ref
        )

    @pl.when(step == 0)
    def _():
        for r in range(4):
            rows = slice(r * 128, (r + 1) * 128)
            w_ref[rows, 0:128] = nt(down_t_ref[...], ex_ref[rows, :]).astype(BF)
            w_ref[rows, 128:256] = project_t_ref[...]
            taps = eu_ref[r * 256 : (r + 1) * 256, :]
            u_ref[rows, :] = nt(up_t_ref[...], taps).astype(BF)
            ut_ref[:, rows] = nn(taps, up_ref[...]).astype(BF)
        w1_ref[...] = nt(first_t_ref[...], ef_ref[...]).astype(BF)
        gu_ref[...] = jnp.zeros_like(gu_ref)
        gd_ref[...] = jnp.zeros_like(gd_ref)
        fg_ref[...] = jnp.zeros_like(fg_ref)
        grad_ref[...] = jnp.zeros_like(grad_ref)
        d_project_ref[...] = jnp.zeros_like(d_project_ref)
        for buffer in store:
            buffer[2] = jnp.zeros(buffer.shape[1:], buffer.dtype)
        finish(forward(coarse_first_ref, 0))

    back = backward(done)
    ahead = forward(coarse_ref, soon)
    advance(back)
    later = later_ref[0]
    later_high = later.astype(BF).astype(F32)
    later_both = jnp.concatenate([later_high, later - later_high], axis=0).astype(BF)
    aux = [before_ref[0], after_ref[0], later_both]
    fine_all = nn(sel_x_ref[...], jnp.concatenate([fine_ref[0]] + aux, axis=0))
    slope_all = nn(sel_s_ref[...], jnp.concatenate([cot_ref[0]] + aux, axis=0))
    row = lax.broadcasted_iota(jnp.int32, (64, HALF), 0)
    flux_scale = jnp.where(row >= 32, SCALE, 1.0)
    lane32 = lax.broadcasted_iota(jnp.int32, (32, HALF), 1)
    lane64 = lax.broadcasted_iota(jnp.int32, (64, HALF), 1)
    not_first = lambda x: x >= 1
    not_last = lambda x: x < HALF - 1

    def enter(b):
        x0 = fine_all[b * 64 : b * 64 + 32]
        x1 = fine_all[b * 64 + 32 : b * 64 + 64]
        x_taps = jnp.concatenate(
            [x0, x1, moved(x1, 1, lane32, not_first), moved(x0, -1, lane32, not_last)], axis=0
        ).astype(BF)
        s0 = slope_all[b * 128 : b * 128 + 64] * flux_scale
        s1 = slope_all[b * 128 + 64 : b * 128 + 128] * flux_scale
        s_taps = jnp.concatenate(
            [s0, s1, moved(s1, 1, lane64, not_first), moved(s0, -1, lane64, not_last)], axis=0
        ).astype(BF)
        wide = store[5][now, :, b * HALF : (b + 1) * HALF]
        third = nn(w_ref[...], jnp.concatenate([x_taps, wide], axis=0))
        return x_taps, s_taps, third, nn(u_ref[...], s_taps)

    def middle(entered):
        x_taps, s_taps, third, d_hidden = entered
        value, slope = gelu_both(third)
        return x_taps, s_taps, value.astype(BF), (d_hidden * slope).astype(BF)

    def leave(held):
        x_taps, s_taps, hidden, d_third = held
        taps = nn(ut_ref[...], hidden)
        c0 = taps[0:64] + moved(taps[192:256], 1, lane64, not_first)
        c1 = taps[64:128] + moved(taps[128:192], -1, lane64, not_last)
        gu_ref[...] += nt(s_taps, hidden)
        both = nt(jnp.concatenate([x_taps, pool_ref[...]], axis=0), d_third)
        gd_ref[...] += both[0:128]
        per_row = both[128:192]
        cells_sum = (per_row[:, 0:128] + per_row[:, 128:256]) + (
            per_row[:, 256:384] + per_row[:, 384:512]
        )
        return [c0 * flux_scale, c1 * flux_scale], cells_sum

    combined = []
    pooled = []
    entered = {}
    held = {}
    for turn in range(blocks + 2):
        if turn < blocks:
            entered[turn] = enter(turn)
        if turn == 1:
            advance(back)
        if turn == 2:
            finish(back)
        if 0 <= turn - 1 < blocks:
            held[turn - 1] = middle(entered.pop(turn - 1))
        if turn >= 3:
            advance(ahead)
        if turn - 2 >= 0:
            pair, cells_sum = leave(held.pop(turn - 2))
            combined += pair
            pooled.append(cells_sum)

    out = jnp.concatenate(combined, axis=0)
    out_high = out.astype(BF)
    out_low = (out - out_high.astype(F32)).astype(BF)
    finish(ahead)
    placed = nn(sel_o_ref[...], out_high) + nn(sel_o_ref[...], out_low)
    main = pred_ref.shape[1]
    pred_ref[0] = placed[0:main]
    before_flux = placed[main + 8 : main + 16]
    own = before_flux * jnp.where(tile >= 1, 1.0, 0.0)
    flux = placed[main + 24 : main + 32] + own
    to_last_ref[0] = placed[main : main + 8] + before_flux
    to_first_ref[0] = placed[main + 16 : main + 24]
    own_ref[0] = own
    flux = jnp.concatenate([flux[:, 0:128], flux[:, 128:256]], axis=0)
    flux_high = flux.astype(BF)
    chunk = GRAD_ROWS // peers
    sent_ref[step, chunk : chunk + 16, :] = flux_high
    sent_ref[step, chunk + 16 : chunk + 32, :] = (flux - flux_high.astype(F32)).astype(BF)
    d_project_ref[...] = jnp.concatenate(pooled, axis=0).astype(BF)

    @pl.when(step == pl.num_programs(0) - 1)
    def _():
        finish(backward(now))
        up = jnp.zeros((96, 128), F32)
        down = jnp.zeros((48, 128), F32)
        for r in range(4):
            lanes = slice(r * 128, (r + 1) * 128)
            up = up + exact(eut_ref[r * 96 : (r + 1) * 96, :], gu_ref[:, lanes])
            down = down + exact(ext_ref[r * 48 : (r + 1) * 48, :], gd_ref[:, lanes])
        grad_ref[UP_AT : UP_AT + 96, :] = up
        grad_ref[DOWN_AT : DOWN_AT + 48, :] = down
        grad_ref[FIRST_AT : FIRST_AT + 32, :] = exact(eft_ref[...], fg_ref[...])
        for t in range(peers):
            sent_ref[t, 0:chunk, :] = grad_ref[t * chunk : (t + 1) * chunk, :].astype(BF)


def run_slots(peers, ids, tile, coarse, fine, cot, before, after, later, fixed, weights):
    slots, main, width = fine.shape
    blocks = main // 48
    cells = blocks * CG
    chunk = GRAD_ROWS // peers

    def whole(array):
        return pl.BlockSpec(array.shape, lambda n, ids, tile: (0,) * array.ndim)

    def per_slot(array):
        return pl.BlockSpec((1,) + array.shape[1:], lambda n, ids, tile: (n, 0, 0))

    one = (1,) + coarse.shape[1:]
    in_specs = [
        pl.BlockSpec(one, lambda n, ids, tile: (ids[0], 0, 0)),
        pl.BlockSpec(one, lambda n, ids, tile: (ids[jnp.minimum(n + 1, slots - 1)], 0, 0)),
        per_slot(fine),
        per_slot(cot),
        per_slot(before),
        per_slot(after),
        per_slot(later),
    ] + [whole(a) for a in fixed + weights]
    edge = jax.ShapeDtypeStruct((slots, 8, width), F32)
    out_shape = [
        jax.ShapeDtypeStruct((slots, main, width), F32),
        edge,
        edge,
        edge,
        jax.ShapeDtypeStruct((peers, chunk + 32, 128), BF),
    ]
    grid_spec = pltpu.PrefetchScalarGridSpec(
        num_scalar_prefetch=2,
        grid=(slots,),
        in_specs=in_specs,
        out_specs=[per_slot(a) for a in out_shape[:4]] + [whole(out_shape[4])],
        scratch_shapes=[
            pltpu.VMEM((GRAD_ROWS, 128), F32),
            pltpu.VMEM((512, 256), BF),
            pltpu.VMEM((512, 256), BF),
            pltpu.VMEM((256, 512), BF),
            pltpu.VMEM((128, 80), BF),
            pltpu.VMEM((256, 512), F32),
            pltpu.VMEM((128, 512), F32),
            pltpu.VMEM((80, 128), F32),
            pltpu.VMEM((cells, 128), BF),
            pltpu.VMEM((3, 80, 3 * cells), BF),
            pltpu.VMEM((3, 1152, cells), BF),
            pltpu.VMEM((3, 128, 3 * cells), F32),
            pltpu.VMEM((3, 128, cells), F32),
            pltpu.VMEM((3, 128, cells), BF),
            pltpu.VMEM((3, 128, blocks * HALF), BF),
        ],
    )

    def body(*refs):
        slot_kernel(blocks, peers, *refs)

    return pl.pallas_call(
        body,
        grid_spec=grid_spec,
        out_shape=out_shape,
        compiler_params=pltpu.CompilerParams(vmem_limit_bytes=52 * 1024 * 1024),
        cost_estimate=pl.CostEstimate(
            flops=slots * blocks * 500_000_000, bytes_accessed=16_000_000, transcendentals=0
        ),
    )(ids, tile, coarse, coarse, fine, cot, before, after, later, *fixed, *weights)


FINAL_SLOTS = 4
PARTS = ((0, 1152), (PROJECT_AT, 128), (UP_AT, 96), (DOWN_AT, 48), (FIRST_AT, 32))


def final_kernel(chunk, rows, back_ref, pred_ref, own_ref, first_ref, last_ref, out_ref, *grads):
    step = pl.program_id(0)

    @pl.when(step == 0)
    def _():
        for (start, size), grad in zip(PARTS, grads):
            at = start
            while at < start + size:
                t = at // chunk
                stop = min((t + 1) * chunk, start + size)
                grad[at - start : stop - start, :] = back_ref[
                    t, at - t * chunk : stop - t * chunk, :
                ].astype(F32)
                at = stop

    row = lax.broadcasted_iota(jnp.int32, (rows, HALF), 0)
    for s in range(out_ref.shape[0]):
        slot = step * out_ref.shape[0] + s
        ahead = back_ref[slot, chunk : chunk + 16, :].astype(F32)
        ahead = ahead + back_ref[slot, chunk + 16 : chunk + 32, :].astype(F32)
        base = jnp.concatenate([ahead[0:8], ahead[8:16]], axis=1) + own_ref[s]
        for k in range(3):
            for p in range(2):
                for q in range(2):
                    at = ((k * 2 + p) * 2 + q) * rows
                    pick = slice(k * 2 + q, k * 2 + q + 1)
                    edge = (first_ref if p == 0 else last_ref)[s, pick, :]
                    reached = row == (0 if p == 0 else rows - 1)
                    out_ref[s, at : at + rows, :] = (
                        pred_ref[s, at : at + rows, :]
                        + base[pick]
                        + jnp.where(reached, edge, 0.0)
                    ).astype(BF)


def run_final(back, pred, own, first, last):
    slots, main, width = pred.shape
    chunk = back.shape[1] - 32
    held = FINAL_SLOTS if main % 192 == 0 else 2 * FINAL_SLOTS

    def per_slots(array):
        return pl.BlockSpec((held,) + array.shape[1:], lambda n: (n, 0, 0))

    def body(*refs):
        final_kernel(chunk, main // 12, *refs)

    return pl.pallas_call(
        body,
        grid=(slots // held,),
        in_specs=[pl.BlockSpec(back.shape, lambda n: (0, 0, 0))]
        + [per_slots(a) for a in (pred, own, first, last)],
        out_specs=[per_slots(pred)]
        + [pl.BlockSpec((size, 128), lambda n: (0, 0)) for _, size in PARTS],
        out_shape=[jax.ShapeDtypeStruct(pred.shape, BF)]
        + [jax.ShapeDtypeStruct((size, 128), F32) for _, size in PARTS],
        compiler_params=pltpu.CompilerParams(vmem_limit_bytes=32 * 1024 * 1024),
    )(back, pred, own, first, last)


def exchanged(value):
    return lax.all_to_all(value, "tile", split_axis=0, concat_axis=0, tiled=True)


def local(
    coarse_solution,
    geometry,
    fine_fields,
    cotangent,
    sample_ids,
    first_weight,
    dilated_weight,
    project_weight,
    down_weight,
    up_weight,
):
    peers = lax.axis_size("tile")
    position = lax.axis_index("tile")
    slots, rows = fine_fields.shape[0], fine_fields.shape[4]
    blocks = rows // 4
    up = [(i, i + 1) for i in range(peers - 1)]
    down = [(i + 1, i) for i in range(peers - 1)]

    totals = jnp.sum(cotangent.astype(F32), axis=(2, 4)).reshape(slots, 6, HALF)
    totals = jnp.pad(totals, ((0, 0), (0, 2), (0, 0)))
    mine = coarse_solution.shape[0]
    inputs = jnp.concatenate([coarse_solution.astype(F32), geometry.astype(F32)[:, None]], axis=1)
    padded = jnp.pad(inputs, ((0, 0), (0, 0), (6 * CG, 6 * CG)))
    span = (blocks + 12) * CG
    windows = jnp.stack(
        [padded[:, :, t * blocks * CG : t * blocks * CG + span] for t in range(peers)], 0
    )
    sent = jnp.concatenate(
        [
            windows.reshape(peers, mine * 3 * span),
            totals.reshape(peers, (slots // peers) * 8 * HALF),
        ],
        axis=1,
    )
    got = exchanged(sent)
    coarse = got[:, : mine * 3 * span].reshape(peers * mine, 3, span)
    sums = got[:, mine * 3 * span :]
    order = lax.broadcasted_iota(jnp.int32, (peers, peers), 0)
    other = lax.broadcasted_iota(jnp.int32, (peers, peers), 1)
    behind = jnp.sum(jnp.where((other > order)[:, :, None], sums[None], 0.0), axis=1)
    later = exchanged(behind).reshape(slots, 8, HALF)

    blank = jnp.zeros((slots, 4, HALF), BF)
    edge_last = jnp.concatenate(
        [
            fine_fields[:, :, 1, :, -1].reshape(slots, 6, HALF),
            cotangent[:, :, 1, :, -1].reshape(slots, 6, HALF),
            blank,
        ],
        axis=1,
    )
    edge_first = jnp.concatenate(
        [
            fine_fields[:, :, 0, :, 0].reshape(slots, 6, HALF),
            cotangent[:, :, 0, :, 0].reshape(slots, 6, HALF),
            blank,
        ],
        axis=1,
    )
    from_before = lax.ppermute(edge_last, "tile", up)
    from_after = lax.ppermute(edge_first, "tile", down)

    made = constants(rows)
    sel_s = jnp.where(
        position == 0, jnp.asarray(made["sel_s_first"], BF), jnp.asarray(made["sel_s"], BF)
    )
    fixed = [
        jnp.asarray(made["sel_x"], BF),
        sel_s,
        jnp.asarray(made["sel_o"], BF),
        jnp.asarray(made["ex"], BF),
        jnp.asarray(made["eu"], BF),
        jnp.asarray(made["ext"], F32),
        jnp.asarray(made["eut"], F32),
        jnp.asarray(made["ef"], BF),
        jnp.asarray(made["eft"], F32),
        jnp.asarray(made["pool"], BF),
        jnp.asarray(made["spread"], BF),
    ]
    second = dilated_weight.reshape(1152, 128)
    up_flat = up_weight.reshape(96, 128)
    weights = [
        jnp.pad(first_weight.reshape(27, 128), ((0, 5), (0, 0))).T,
        second.T,
        second,
        project_weight,
        project_weight.T,
        down_weight.reshape(48, 128).T,
        up_flat.T,
        up_flat,
    ]
    pred_local, last_edge, first_edge, own, sent = run_slots(
        peers,
        sample_ids,
        position.reshape(1).astype(jnp.int32),
        coarse,
        fine_fields.reshape(slots, 12 * rows, HALF),
        cotangent.reshape(slots, 12 * rows, HALF),
        from_before,
        from_after,
        later,
        fixed,
        weights,
    )

    chunk = GRAD_ROWS // peers
    got = exchanged(sent).astype(F32)
    to_first = lax.ppermute(first_edge, "tile", up)
    to_last = lax.ppermute(last_edge, "tile", down)
    reduced = jnp.sum(got[:, :chunk], axis=0).astype(BF)
    sums = got[:, chunk : chunk + 16] + got[:, chunk + 16 :]
    ahead = jnp.sum(jnp.where((other < order)[:, :, None, None], sums[None], 0.0), axis=1)
    high = lax.reduce_precision(ahead, 8, 7)
    reduced, to_first, to_last = lax.optimization_barrier((reduced, to_first, to_last))
    back = exchanged(
        jnp.concatenate(
            [
                jnp.broadcast_to(reduced, (peers, chunk, 128)),
                high.astype(BF),
                (ahead - high).astype(BF),
            ],
            axis=1,
        )
    )
    prediction, dilated, project, up_grad, down_grad, first = run_final(
        back, pred_local, own, to_first, to_last
    )
    return (
        prediction.reshape(fine_fields.shape),
        first[0:27].reshape(first_weight.shape),
        dilated.reshape(dilated_weight.shape),
        project,
        down_grad.reshape(down_weight.shape),
        up_grad.reshape(up_weight.shape),
    )


def solution(mesh):
    in_specs = (
        P(("groups", "tile"), None, None),
        P(("groups", "tile"), None),
        P("groups", None, None, None, "tile", None),
        P("groups", None, None, None, "tile", None),
        P("groups"),
        P(),
        P(),
        P(),
        P(),
        P(),
    )
    out_specs = (
        P("groups", None, None, None, "tile", None),
        P("groups", None, None, None),
        P("groups", None, None, None),
        P("groups", None),
        P("groups", None, None, None),
        P("groups", None, None, None),
    )
    return jax.shard_map(local, mesh=mesh, in_specs=in_specs, out_specs=out_specs, check_vma=False)
```

```python
import math

import jax
import jax.numpy as jnp
import numpy as np
from jax import lax
from jax.experimental import pallas as pl
from jax.experimental.pallas import tpu as pltpu
from jax.sharding import PartitionSpec as P

CG = 64
FG = 512
HALF = FG // 2
SCALE = 1.0 / math.sqrt(FG)
GELU_A = math.sqrt(2.0 / math.pi)
GELU_B = GELU_A * 0.044715
BF = jnp.bfloat16
F32 = jnp.float32

AUX = 48
GRAD_ROWS = 1536
UP_AT, DOWN_AT, FIRST_AT, PROJECT_AT = 1280, 1376, 1424, 1152


def nn(a, b):
    return lax.dot_general(a, b, (((1,), (0,)), ((), ())), preferred_element_type=F32)


def nt(a, b):
    return lax.dot_general(a, b, (((1,), (1,)), ((), ())), preferred_element_type=F32)


def exact(a, b):
    return lax.dot_general(
        a, b, (((1,), (0,)), ((), ())), precision=lax.Precision.HIGHEST, preferred_element_type=F32
    )


def exact_t(a, b):
    return lax.dot_general(
        a, b, (((1,), (1,)), ((), ())), precision=lax.Precision.HIGHEST, preferred_element_type=F32
    )


def row_at(tap, r):
    if tap == 0:
        return 8 if r == 0 else 4 + r - 1
    if tap == 1:
        return r
    if tap == 2:
        return 4 + r
    return 9 if r == 3 else r + 1


def fine_row(block, index):
    if index == 8:
        return 8 * block - 1
    if index == 9:
        return 8 * block + 8
    return 8 * block + 2 * (index % 4) + index // 4


COL_GROUP = (2, 0, 1, 3)


def constants(rows):
    blocks = rows // 4
    last = 2 * rows
    width = 12 * rows + AUX

    def held(ch, q, o):
        return ((ch * 2 + o % 2) * 2 + q) * rows + o // 2

    sel_x = np.zeros((blocks, 2, 32, width), np.float32)
    sel_s = np.zeros((blocks, 2, 64, width), np.float32)
    sel_o = np.zeros((12 * rows + 32, blocks, 2, 64), np.float32)
    base = 12 * rows
    for b in range(blocks):
        for q in range(2):
            for ch in range(3):
                for index in range(10):
                    o = fine_row(b, index)
                    at = ch * 10 + index
                    if o == -1:
                        sel_x[b, q, at, base + ch * 2 + q] = 1
                        sel_s[b, q, at, base + 6 + ch * 2 + q] = 1
                        sel_s[b, q, 32 + at, base + 6 + ch * 2 + q] = 1
                    elif o == last:
                        sel_x[b, q, at, base + 16 + ch * 2 + q] = 1
                        sel_s[b, q, at, base + 22 + ch * 2 + q] = 1
                    else:
                        sel_x[b, q, at, held(ch, q, o)] = 1
                        sel_s[b, q, at, held(ch, q, o)] = 1
                    for later in range(max(o, 0), last):
                        sel_s[b, q, 32 + at, held(ch, q, later)] = 1
                    sel_s[b, q, 32 + at, base + 32 + ch * 2 + q] = 1
                    sel_s[b, q, 32 + at, base + 40 + ch * 2 + q] = 1
                    for target in range(max(o, 0), last):
                        if target == o:
                            sel_o[held(ch, q, target), b, q, at] = 1
                        if o >= 0:
                            sel_o[held(ch, q, target), b, q, 32 + at] = 1
                    if o == -1:
                        sel_o[base + ch * 2 + q, b, q, at] = 1
                        sel_o[base + 8 + ch * 2 + q, b, q, 32 + at] = 1
                    else:
                        sel_o[base + 24 + ch * 2 + q, b, q, 32 + at] = 1
                    if o == last:
                        sel_o[base + 16 + ch * 2 + q, b, q, at] = 1
    sel_s_first = sel_s.copy()
    for q in range(2):
        for ch in range(3):
            sel_s_first[0, q, 32 + ch * 10 + 8] = 0
    ex = np.zeros((4, 128, 48), np.float32)
    eu = np.zeros((4, 256, 96), np.float32)
    for r in range(4):
        for i in range(4):
            for j in range(4):
                for ch in range(3):
                    ex[r, COL_GROUP[j] * 32 + ch * 10 + row_at(i, r), (ch * 4 + i) * 4 + j] = 1
                for k in range(6):
                    at = COL_GROUP[j] * 64 + (k // 3) * 32 + (k % 3) * 10 + row_at(i, r)
                    eu[r, at, (i * 4 + j) * 6 + k] = 1
    ef = np.zeros((80, 32), np.float32)
    for ch in range(3):
        for tap in range(9):
            ef[tap * 8 + ch, ch * 9 + tap] = 1
    pool = np.zeros((CG, HALF), np.float32)
    for c in range(HALF):
        pool[c // 4, c] = 1
    none = np.zeros((CG, HALF), np.float32)
    return dict(
        sel_x=sel_x.reshape(blocks * 64, width),
        sel_s=sel_s.reshape(blocks * 128, width),
        sel_s_first=sel_s_first.reshape(blocks * 128, width),
        sel_o=sel_o.reshape(12 * rows + 32, blocks * 128),
        ex=ex.reshape(512, 48),
        eu=eu.reshape(1024, 96),
        ext=np.concatenate(list(np.swapaxes(ex, 1, 2)), 0),
        eut=np.concatenate(list(np.swapaxes(eu, 1, 2)), 0),
        ef=ef,
        eft=ef.T,
        pool_both=np.concatenate([pool, none, none, pool], 0),
    )


def gelu_both(pre):
    square = pre * pre
    t = jnp.tanh(pre * (GELU_B * square + GELU_A))
    gate = 0.5 + 0.5 * t
    value = pre * gate
    slope = gate + (value * (1.0 - gate)) * (6.0 * GELU_B * square + 2.0 * GELU_A)
    return value, slope


def moved(value, shift, lane, keep):
    width = value.shape[1]
    return jnp.where(keep(lane), pltpu.roll(value, shift % width, 1), 0.0)


def coarse_forward(blocks, tile, coarse_ref, w1_ref, second_t_ref, spread_ref, store, place):
    patches_s, columns_s, first_slope_s, second_slope_s, feature_s, wide_s = store
    cells = blocks * CG
    inputs = jnp.concatenate([coarse_ref[0], jnp.zeros((5, coarse_ref.shape[2]), F32)], axis=0)
    lane_in = lax.broadcasted_iota(jnp.int32, inputs.shape, 1) % CG
    by_col = (
        moved(inputs, 2, lane_in, lambda x: x >= 2),
        inputs,
        moved(inputs, -2, lane_in, lambda x: x < CG - 2),
    )
    above = jnp.where(tile * blocks >= 4, 1.0, 0.0)
    below = jnp.where(tile * blocks + 4 <= CG - blocks, 1.0, 0.0)
    windows = []
    for window in range(3):
        pieces = []
        for row_tap in range(3):
            for col_tap in range(3):
                start = (4 * window + 2 * row_tap) * CG
                pieces.append(by_col[col_tap][:, start : start + cells])
        pieces.append(jnp.zeros((8, cells), F32))
        stacked = jnp.concatenate(pieces, axis=0)
        if window == 0:
            stacked = stacked * above
        if window == 2:
            stacked = stacked * below
        windows.append(stacked)
    patches = jnp.concatenate(windows, axis=1).astype(BF)
    first_value, first_slope = gelu_both(nn(w1_ref[...], patches))
    yield
    hidden = first_value.astype(BF)
    stacked = jnp.concatenate(
        [hidden[:, window * cells : (window + 1) * cells] for window in range(3)], axis=0
    )
    taps = nn(second_t_ref[...], stacked)
    lane_c = lax.broadcasted_iota(jnp.int32, (128, cells), 1) % CG
    second_pre = (
        taps[128:256]
        + moved(taps[0:128], 4, lane_c, lambda x: x >= 4)
        + moved(taps[256:384], -4, lane_c, lambda x: x < CG - 4)
    )
    second_value, second_slope = gelu_both(second_pre)
    yield
    feature = second_value.astype(BF)
    patches_s[place] = patches
    columns_s[place] = stacked
    first_slope_s[place] = first_slope
    second_slope_s[place] = second_slope
    feature_s[place] = feature
    pairs = [feature[:, at * 128 : (at + 1) * 128] for at in range(blocks // 2)]
    pairs = jnp.concatenate(pairs, axis=0) if blocks > 2 else pairs[0]
    for parity in range(2):
        wide = nn(pairs, spread_ref[parity * 128 : (parity + 1) * 128, :]).astype(BF)
        for at in range(blocks // 2):
            b = 2 * at + parity
            wide_s[place, :, b * HALF : (b + 1) * HALF] = wide[at * 128 : (at + 1) * 128]


def coarse_backward(blocks, d_project, project_ref, second_ref, store, place, dil_ref, pg_ref, fg_ref):
    patches_s, columns_s, first_slope_s, second_slope_s, feature_s, _ = store
    cells = blocks * CG
    pg_ref[...] += nt(feature_s[place], d_project)
    d_feature = nn(project_ref[...], d_project).astype(BF).astype(F32)
    d_second = (d_feature * second_slope_s[place]).astype(BF).astype(F32)
    yield
    lane_c = lax.broadcasted_iota(jnp.int32, (128, cells), 1) % CG
    shifted = jnp.concatenate(
        [
            moved(d_second, -4, lane_c, lambda x: x < CG - 4),
            d_second,
            moved(d_second, 4, lane_c, lambda x: x >= 4),
        ],
        axis=0,
    ).astype(BF)
    dil_ref[...] += nt(columns_s[place], shifted)
    back = nn(second_ref[...], shifted)
    yield
    d_first_hidden = jnp.concatenate([back[0:128], back[128:256], back[256:384]], axis=1)
    d_first = (d_first_hidden * first_slope_s[place]).astype(BF)
    fg_ref[...] += nt(patches_s[place], d_first)


def advance(stage):
    next(stage, None)


def finish(stage):
    for _ in stage:
        pass


def slot_kernel(
    blocks,
    peers,
    ids_ref,
    tile_ref,
    coarse_first_ref,
    coarse_ref,
    fine_ref,
    cot_ref,
    before_ref,
    after_ref,
    later_ref,
    sel_x_ref,
    sel_s_ref,
    sel_o_ref,
    ex_ref,
    eu_ref,
    ext_ref,
    eut_ref,
    ef_ref,
    eft_ref,
    spread_ref,
    first_t_ref,
    second_t_ref,
    second_ref,
    project_ref,
    project_t_ref,
    down_t_ref,
    up_t_ref,
    up_ref,
    pred_ref,
    to_last_ref,
    to_first_ref,
    own_ref,
    sent_ref,
    dil_ref,
    pg_ref,
    w_ref,
    u_ref,
    ut_ref,
    w1_ref,
    gu_ref,
    gd_ref,
    fg_ref,
    d_project_ref,
    *store,
):
    step = pl.program_id(0)
    tile = tile_ref[0]
    now = lax.rem(step, 3)
    soon = lax.rem(step + 1, 3)
    done = lax.rem(step + 2, 3)

    def forward(source, place):
        return coarse_forward(
            blocks, tile, source, w1_ref, second_t_ref, spread_ref, store, place
        )

    def backward(place):
        return coarse_backward(
            blocks, d_project_ref[...], project_ref, second_ref, store, place, dil_ref, pg_ref, fg_ref
        )

    @pl.when(step == 0)
    def _():
        for r in range(4):
            rows = slice(r * 128, (r + 1) * 128)
            w_ref[rows, 0:128] = nt(down_t_ref[...], ex_ref[rows, :]).astype(BF)
            w_ref[rows, 128:256] = project_t_ref[...]
            taps = eu_ref[r * 256 : (r + 1) * 256, :]
            u_ref[rows, :] = nt(up_t_ref[...], taps).astype(BF)
            ut_ref[:, rows] = nn(taps, up_ref[...]).astype(BF)
        w1_ref[...] = nt(first_t_ref[...], ef_ref[...]).astype(BF)
        gu_ref[...] = jnp.zeros_like(gu_ref)
        gd_ref[...] = jnp.zeros_like(gd_ref)
        fg_ref[...] = jnp.zeros_like(fg_ref)
        dil_ref[...] = jnp.zeros_like(dil_ref)
        pg_ref[...] = jnp.zeros_like(pg_ref)
        d_project_ref[...] = jnp.zeros_like(d_project_ref)
        for buffer in store:
            buffer[2] = jnp.zeros(buffer.shape[1:], buffer.dtype)
        finish(forward(coarse_first_ref, 0))

    back = backward(done)
    ahead = forward(coarse_ref, soon)
    advance(back)
    later = later_ref[0]
    later_high = later.astype(BF).astype(F32)
    later_both = jnp.concatenate([later_high, later - later_high], axis=0).astype(BF)
    aux = [before_ref[0], after_ref[0], later_both]
    fine_all = nn(sel_x_ref[...], jnp.concatenate([fine_ref[0]] + aux, axis=0))
    slope_all = nn(sel_s_ref[...], jnp.concatenate([cot_ref[0]] + aux, axis=0))
    row = lax.broadcasted_iota(jnp.int32, (64, HALF), 0)
    flux_scale = jnp.where(row >= 32, SCALE, 1.0)
    lane32 = lax.broadcasted_iota(jnp.int32, (32, HALF), 1)
    lane64 = lax.broadcasted_iota(jnp.int32, (64, HALF), 1)
    not_first = lambda x: x >= 1
    not_last = lambda x: x < HALF - 1

    def enter(b):
        x0 = fine_all[b * 64 : b * 64 + 32]
        x1 = fine_all[b * 64 + 32 : b * 64 + 64]
        x_taps = jnp.concatenate(
            [x0, x1, moved(x1, 1, lane32, not_first), moved(x0, -1, lane32, not_last)], axis=0
        ).astype(BF)
        s0 = slope_all[b * 128 : b * 128 + 64] * flux_scale
        s1 = slope_all[b * 128 + 64 : b * 128 + 128] * flux_scale
        s_taps = jnp.concatenate(
            [s0, s1, moved(s1, 1, lane64, not_first), moved(s0, -1, lane64, not_last)], axis=0
        ).astype(BF)
        wide = store[5][now, :, b * HALF : (b + 1) * HALF]
        third = nn(w_ref[...], jnp.concatenate([x_taps, wide], axis=0))
        return x_taps, s_taps, third, nn(u_ref[...], s_taps)

    def middle(entered):
        x_taps, s_taps, third, d_hidden = entered
        value, slope = gelu_both(third)
        return x_taps, s_taps, value.astype(BF), (d_hidden * slope).astype(BF)

    def leave(b, held):
        hidden = held[2]
        taps = nn(ut_ref[...], hidden)
        c0 = taps[0:64] + moved(taps[192:256], 1, lane64, not_first)
        c1 = taps[64:128] + moved(taps[128:192], -1, lane64, not_last)
        return [c0 * flux_scale, c1 * flux_scale]

    def collect(even, odd):
        s_taps = jnp.concatenate([even[1], odd[1]], axis=1)
        hidden = jnp.concatenate([even[2], odd[2]], axis=1)
        gu_ref[...] += nt(hidden, s_taps)
        x_taps = jnp.concatenate(
            [
                jnp.concatenate([even[0], odd[0]], axis=1),
                jnp.concatenate([spread_ref[0:128, :], spread_ref[128:256, :]], axis=1),
            ],
            axis=0,
        )
        both = nt(jnp.concatenate([even[3], odd[3]], axis=1), x_taps)
        gd_ref[...] += both[:, 0:128]
        per_row = both[:, 128:256]
        return (per_row[0:128] + per_row[128:256]) + (per_row[256:384] + per_row[384:512])

    combined = []
    pooled = []
    entered = {}
    held = {}
    for turn in range(blocks + 2):
        if turn < blocks:
            entered[turn] = enter(turn)
        if turn == 1:
            advance(back)
        if turn == 2:
            finish(back)
        if 0 <= turn - 1 < blocks:
            held[turn - 1] = middle(entered.pop(turn - 1))
        if turn >= 3:
            advance(ahead)
        b = turn - 2
        if b >= 0:
            combined += leave(b, held[b])
            if b % 2 == 1:
                pooled.append(collect(held[b - 1], held[b]))

    out = jnp.concatenate(combined, axis=0)
    finish(ahead)
    placed = nn(sel_o_ref[...], out.astype(BF))
    main = pred_ref.shape[1]
    pred_ref[0] = placed[0:main]
    before_flux = placed[main + 8 : main + 16]
    own = before_flux * jnp.where(tile >= 1, 1.0, 0.0)
    flux = placed[main + 24 : main + 32] + own
    to_last_ref[0] = placed[main : main + 8] + before_flux
    to_first_ref[0] = placed[main + 16 : main + 24]
    own_ref[0] = own
    flux = jnp.concatenate([flux[:, 0:128], flux[:, 128:256]], axis=0)
    flux_high = flux.astype(BF)
    chunk = GRAD_ROWS // peers
    sent_ref[step, chunk : chunk + 16, :] = flux_high
    sent_ref[step, chunk + 16 : chunk + 32, :] = (flux - flux_high.astype(F32)).astype(BF)
    d_project_ref[...] = jnp.concatenate(pooled, axis=1).astype(BF)

    @pl.when(step == pl.num_programs(0) - 1)
    def _():
        finish(backward(now))
        up = jnp.zeros((96, 128), F32)
        down = jnp.zeros((48, 128), F32)
        for r in range(4):
            lanes = slice(r * 128, (r + 1) * 128)
            up = up + exact_t(eut_ref[r * 96 : (r + 1) * 96, :], gu_ref[lanes, :])
            down = down + exact_t(ext_ref[r * 48 : (r + 1) * 48, :], gd_ref[lanes, :])
        first = exact(eft_ref[...], fg_ref[...])
        pieces = [
            dil_ref[i * 128 : (i + 1) * 128, j * 128 : (j + 1) * 128]
            for i in range(3)
            for j in range(3)
        ]
        pieces += [pg_ref[...], up, down, first]
        pieces.append(jnp.zeros((GRAD_ROWS - FIRST_AT - 32, 128), F32))
        grads = jnp.concatenate(pieces, axis=0).astype(BF)
        for t in range(peers):
            sent_ref[t, 0:chunk, :] = grads[t * chunk : (t + 1) * chunk, :]


def run_slots(peers, ids, tile, coarse, fine, cot, before, after, later, fixed, weights):
    slots, main, width = fine.shape
    blocks = main // 48
    cells = blocks * CG
    chunk = GRAD_ROWS // peers

    def whole(array):
        return pl.BlockSpec(array.shape, lambda n, ids, tile: (0,) * array.ndim)

    def per_slot(array):
        return pl.BlockSpec((1,) + array.shape[1:], lambda n, ids, tile: (n, 0, 0))

    one = (1,) + coarse.shape[1:]
    in_specs = [
        pl.BlockSpec(one, lambda n, ids, tile: (ids[0], 0, 0)),
        pl.BlockSpec(one, lambda n, ids, tile: (ids[jnp.minimum(n + 1, slots - 1)], 0, 0)),
        per_slot(fine),
        per_slot(cot),
        per_slot(before),
        per_slot(after),
        per_slot(later),
    ] + [whole(a) for a in fixed + weights]
    edge = jax.ShapeDtypeStruct((slots, 8, width), F32)
    out_shape = [
        jax.ShapeDtypeStruct((slots, main, width), F32),
        edge,
        edge,
        edge,
        jax.ShapeDtypeStruct((peers, chunk + 32, 128), BF),
    ]
    grid_spec = pltpu.PrefetchScalarGridSpec(
        num_scalar_prefetch=2,
        grid=(slots,),
        in_specs=in_specs,
        out_specs=[per_slot(a) for a in out_shape[:4]] + [whole(out_shape[4])],
        scratch_shapes=[
            pltpu.VMEM((384, 384), F32),
            pltpu.VMEM((128, 128), F32),
            pltpu.VMEM((512, 256), BF),
            pltpu.VMEM((512, 256), BF),
            pltpu.VMEM((256, 512), BF),
            pltpu.VMEM((128, 80), BF),
            pltpu.VMEM((512, 256), F32),
            pltpu.VMEM((512, 128), F32),
            pltpu.VMEM((80, 128), F32),
            pltpu.VMEM((128, cells), BF),
            pltpu.VMEM((3, 80, 3 * cells), BF),
            pltpu.VMEM((3, 384, cells), BF),
            pltpu.VMEM((3, 128, 3 * cells), F32),
            pltpu.VMEM((3, 128, cells), F32),
            pltpu.VMEM((3, 128, cells), BF),
            pltpu.VMEM((3, 128, blocks * HALF), BF),
        ],
    )

    def body(*refs):
        slot_kernel(blocks, peers, *refs)

    return pl.pallas_call(
        body,
        grid_spec=grid_spec,
        out_shape=out_shape,
        compiler_params=pltpu.CompilerParams(vmem_limit_bytes=52 * 1024 * 1024),
        cost_estimate=pl.CostEstimate(
            flops=slots * blocks * 500_000_000, bytes_accessed=16_000_000, transcendentals=0
        ),
    )(ids, tile, coarse, coarse, fine, cot, before, after, later, *fixed, *weights)


FINAL_SLOTS = 4
PARTS = ((0, 1152), (PROJECT_AT, 128), (UP_AT, 96), (DOWN_AT, 48), (FIRST_AT, 32))


def final_kernel(chunk, rows, back_ref, pred_ref, own_ref, first_ref, last_ref, out_ref, *grads):
    step = pl.program_id(0)

    @pl.when(step == 0)
    def _():
        for (start, size), grad in zip(PARTS, grads):
            at = start
            while at < start + size:
                t = at // chunk
                stop = min((t + 1) * chunk, start + size)
                grad[at - start : stop - start, :] = back_ref[
                    t, at - t * chunk : stop - t * chunk, :
                ].astype(F32)
                at = stop

    row = lax.broadcasted_iota(jnp.int32, (rows, HALF), 0)
    for s in range(out_ref.shape[0]):
        slot = step * out_ref.shape[0] + s
        ahead = back_ref[slot, chunk : chunk + 16, :].astype(F32)
        ahead = ahead + back_ref[slot, chunk + 16 : chunk + 32, :].astype(F32)
        base = jnp.concatenate([ahead[0:8], ahead[8:16]], axis=1) + own_ref[s]
        for k in range(3):
            for p in range(2):
                for q in range(2):
                    at = ((k * 2 + p) * 2 + q) * rows
                    pick = slice(k * 2 + q, k * 2 + q + 1)
                    edge = (first_ref if p == 0 else last_ref)[s, pick, :]
                    reached = row == (0 if p == 0 else rows - 1)
                    out_ref[s, at : at + rows, :] = (
                        pred_ref[s, at : at + rows, :]
                        + base[pick]
                        + jnp.where(reached, edge, 0.0)
                    ).astype(BF)


def run_final(back, pred, own, first, last):
    slots, main, width = pred.shape
    chunk = back.shape[1] - 32
    held = FINAL_SLOTS if main % 192 == 0 else 2 * FINAL_SLOTS

    def per_slots(array):
        return pl.BlockSpec((held,) + array.shape[1:], lambda n: (n, 0, 0))

    def body(*refs):
        final_kernel(chunk, main // 12, *refs)

    return pl.pallas_call(
        body,
        grid=(slots // held,),
        in_specs=[pl.BlockSpec(back.shape, lambda n: (0, 0, 0))]
        + [per_slots(a) for a in (pred, own, first, last)],
        out_specs=[per_slots(pred)]
        + [pl.BlockSpec((size, 128), lambda n: (0, 0)) for _, size in PARTS],
        out_shape=[jax.ShapeDtypeStruct(pred.shape, BF)]
        + [jax.ShapeDtypeStruct((size, 128), F32) for _, size in PARTS],
        compiler_params=pltpu.CompilerParams(vmem_limit_bytes=32 * 1024 * 1024),
    )(back, pred, own, first, last)


def exchanged(value):
    return lax.all_to_all(value, "tile", split_axis=0, concat_axis=0, tiled=True)


def local(
    coarse_solution,
    geometry,
    fine_fields,
    cotangent,
    sample_ids,
    first_weight,
    dilated_weight,
    project_weight,
    down_weight,
    up_weight,
):
    peers = lax.axis_size("tile")
    position = lax.axis_index("tile")
    slots, rows = fine_fields.shape[0], fine_fields.shape[4]
    blocks = rows // 4
    up = [(i, i + 1) for i in range(peers - 1)]
    down = [(i + 1, i) for i in range(peers - 1)]

    totals = jnp.sum(cotangent.astype(F32), axis=(2, 4)).reshape(slots, 6, HALF)
    totals = jnp.pad(totals, ((0, 0), (0, 2), (0, 0)))
    mine = coarse_solution.shape[0]
    inputs = jnp.concatenate([coarse_solution.astype(F32), geometry.astype(F32)[:, None]], axis=1)
    padded = jnp.pad(inputs, ((0, 0), (0, 0), (6 * CG, 6 * CG)))
    span = (blocks + 12) * CG
    windows = jnp.stack(
        [padded[:, :, t * blocks * CG : t * blocks * CG + span] for t in range(peers)], 0
    )
    sent = jnp.concatenate(
        [
            windows.reshape(peers, mine * 3 * span),
            totals.reshape(peers, (slots // peers) * 8 * HALF),
        ],
        axis=1,
    )
    got = exchanged(sent)
    coarse = got[:, : mine * 3 * span].reshape(peers * mine, 3, span)
    sums = got[:, mine * 3 * span :]
    order = lax.broadcasted_iota(jnp.int32, (peers, peers), 0)
    other = lax.broadcasted_iota(jnp.int32, (peers, peers), 1)
    behind = jnp.sum(jnp.where((other > order)[:, :, None], sums[None], 0.0), axis=1)
    later = exchanged(behind).reshape(slots, 8, HALF)

    blank = jnp.zeros((slots, 4, HALF), BF)
    edge_last = jnp.concatenate(
        [
            fine_fields[:, :, 1, :, -1].reshape(slots, 6, HALF),
            cotangent[:, :, 1, :, -1].reshape(slots, 6, HALF),
            blank,
        ],
        axis=1,
    )
    edge_first = jnp.concatenate(
        [
            fine_fields[:, :, 0, :, 0].reshape(slots, 6, HALF),
            cotangent[:, :, 0, :, 0].reshape(slots, 6, HALF),
            blank,
        ],
        axis=1,
    )
    from_before = lax.ppermute(edge_last, "tile", up)
    from_after = lax.ppermute(edge_first, "tile", down)

    made = constants(rows)
    sel_s = jnp.where(
        position == 0, jnp.asarray(made["sel_s_first"], BF), jnp.asarray(made["sel_s"], BF)
    )
    fixed = [
        jnp.asarray(made["sel_x"], BF),
        sel_s,
        jnp.asarray(made["sel_o"], BF),
        jnp.asarray(made["ex"], BF),
        jnp.asarray(made["eu"], BF),
        jnp.asarray(made["ext"], F32),
        jnp.asarray(made["eut"], F32),
        jnp.asarray(made["ef"], BF),
        jnp.asarray(made["eft"], F32),
        jnp.asarray(made["pool_both"], BF),
    ]
    second = dilated_weight
    up_flat = up_weight.reshape(96, 128)
    weights = [
        jnp.pad(first_weight.reshape(27, 128), ((0, 5), (0, 0))).T,
        jnp.transpose(second, (1, 3, 0, 2)).reshape(384, 384),
        jnp.transpose(second, (0, 2, 1, 3)).reshape(384, 384),
        project_weight,
        project_weight.T,
        down_weight.reshape(48, 128).T,
        up_flat.T,
        up_flat,
    ]
    pred_local, last_edge, first_edge, own, sent = run_slots(
        peers,
        sample_ids,
        position.reshape(1).astype(jnp.int32),
        coarse,
        fine_fields.reshape(slots, 12 * rows, HALF),
        cotangent.reshape(slots, 12 * rows, HALF),
        from_before,
        from_after,
        later,
        fixed,
        weights,
    )

    chunk = GRAD_ROWS // peers
    got = exchanged(sent).astype(F32)
    to_first = lax.ppermute(first_edge, "tile", up)
    to_last = lax.ppermute(last_edge, "tile", down)
    reduced = jnp.sum(got[:, :chunk], axis=0).astype(BF)
    sums = got[:, chunk : chunk + 16] + got[:, chunk + 16 :]
    ahead = jnp.sum(jnp.where((other < order)[:, :, None, None], sums[None], 0.0), axis=1)
    high = lax.reduce_precision(ahead, 8, 7)
    reduced, to_first, to_last = lax.optimization_barrier((reduced, to_first, to_last))
    back = exchanged(
        jnp.concatenate(
            [
                jnp.broadcast_to(reduced, (peers, chunk, 128)),
                high.astype(BF),
                (ahead - high).astype(BF),
            ],
            axis=1,
        )
    )
    prediction, dilated, project, up_grad, down_grad, first = run_final(
        back, pred_local, own, to_first, to_last
    )
    return (
        prediction.reshape(fine_fields.shape),
        first[0:27].reshape(first_weight.shape),
        dilated.reshape(dilated_weight.shape),
        project,
        down_grad.reshape(down_weight.shape),
        up_grad.reshape(up_weight.shape),
    )


def solution(mesh):
    in_specs = (
        P(("groups", "tile"), None, None),
        P(("groups", "tile"), None),
        P("groups", None, None, None, "tile", None),
        P("groups", None, None, None, "tile", None),
        P("groups"),
        P(),
        P(),
        P(),
        P(),
        P(),
    )
    out_specs = (
        P("groups", None, None, None, "tile", None),
        P("groups", None, None, None),
        P("groups", None, None, None),
        P("groups", None),
        P("groups", None, None, None),
        P("groups", None, None, None),
    )
    return jax.shard_map(local, mesh=mesh, in_specs=in_specs, out_specs=out_specs, check_vma=False)
```

```python
import math

import jax
import jax.numpy as jnp
import numpy as np
from jax import lax
from jax.experimental import pallas as pl
from jax.experimental.pallas import tpu as pltpu
from jax.sharding import PartitionSpec as P

CG = 64
FG = 512
HALF = FG // 2
SCALE = 1.0 / math.sqrt(FG)
GELU_A = math.sqrt(2.0 / math.pi)
GELU_B = GELU_A * 0.044715
BF = jnp.bfloat16
F32 = jnp.float32

AUX = 48
SENT_INPUT = 64
SENT_EARLY = SENT_INPUT + 32
PER_STEP = 2
GRAD_ROWS = 1536
UP_AT, DOWN_AT, FIRST_AT, PROJECT_AT = 1280, 1376, 1424, 1152


def nn(a, b):
    return lax.dot_general(a, b, (((1,), (0,)), ((), ())), preferred_element_type=F32)


def nt(a, b):
    return lax.dot_general(a, b, (((1,), (1,)), ((), ())), preferred_element_type=F32)


def exact(a, b):
    return lax.dot_general(
        a, b, (((1,), (0,)), ((), ())), precision=lax.Precision.HIGHEST, preferred_element_type=F32
    )


def exact_t(a, b):
    return lax.dot_general(
        a, b, (((1,), (1,)), ((), ())), precision=lax.Precision.HIGHEST, preferred_element_type=F32
    )


def row_at(tap, r):
    if tap == 0:
        return 8 if r == 0 else 4 + r - 1
    if tap == 1:
        return r
    if tap == 2:
        return 4 + r
    return 9 if r == 3 else r + 1


def fine_row(block, index):
    if index == 8:
        return 8 * block - 1
    if index == 9:
        return 8 * block + 8
    return 8 * block + 2 * (index % 4) + index // 4


COL_GROUP = (2, 0, 1, 3)


def constants(rows):
    blocks = rows // 4
    last = 2 * rows
    width = 12 * rows + AUX

    def held(ch, q, o):
        return ((ch * 2 + o % 2) * 2 + q) * rows + o // 2

    sel_x = np.zeros((blocks, 2, 32, width), np.float32)
    sel_s = np.zeros((blocks, 2, 64, width), np.float32)
    sel_o = np.zeros((12 * rows + 32, blocks, 2, 64), np.float32)
    base = 12 * rows
    for b in range(blocks):
        for q in range(2):
            for ch in range(3):
                for index in range(10):
                    o = fine_row(b, index)
                    at = ch * 10 + index
                    if o == -1:
                        sel_x[b, q, at, base + ch * 2 + q] = 1
                        sel_s[b, q, at, base + 6 + ch * 2 + q] = 1
                        sel_s[b, q, 32 + at, base + 6 + ch * 2 + q] = 1
                    elif o == last:
                        sel_x[b, q, at, base + 16 + ch * 2 + q] = 1
                        sel_s[b, q, at, base + 22 + ch * 2 + q] = 1
                    else:
                        sel_x[b, q, at, held(ch, q, o)] = 1
                        sel_s[b, q, at, held(ch, q, o)] = 1
                    for later in range(max(o, 0), last):
                        sel_s[b, q, 32 + at, held(ch, q, later)] = 1
                    sel_s[b, q, 32 + at, base + 32 + ch * 2 + q] = 1
                    sel_s[b, q, 32 + at, base + 40 + ch * 2 + q] = 1
                    for target in range(max(o, 0), last):
                        if target == o:
                            sel_o[held(ch, q, target), b, q, at] = 1
                        if o >= 0:
                            sel_o[held(ch, q, target), b, q, 32 + at] = 1
                    if o == -1:
                        sel_o[base + ch * 2 + q, b, q, at] = 1
                        sel_o[base + 8 + ch * 2 + q, b, q, 32 + at] = 1
                    else:
                        sel_o[base + 24 + ch * 2 + q, b, q, 32 + at] = 1
                    if o == last:
                        sel_o[base + 16 + ch * 2 + q, b, q, at] = 1
    early_x = np.zeros((48, 12 * rows), np.float32)
    early_s = np.zeros((48, 12 * rows), np.float32)
    for ch in range(3):
        for q in range(2):
            at = ch * 2 + q
            for o in range(last):
                early_s[at, held(ch, q, o)] = 1
            for start, o in ((16, last - 1), (32, 0)):
                early_x[start + at, held(ch, q, o)] = 1
                early_s[start + 6 + at, held(ch, q, o)] = 1
    ex = np.zeros((4, 128, 48), np.float32)
    eu = np.zeros((4, 256, 96), np.float32)
    for r in range(4):
        for i in range(4):
            for j in range(4):
                for ch in range(3):
                    ex[r, COL_GROUP[j] * 32 + ch * 10 + row_at(i, r), (ch * 4 + i) * 4 + j] = 1
                for k in range(6):
                    at = COL_GROUP[j] * 64 + (k // 3) * 32 + (k % 3) * 10 + row_at(i, r)
                    eu[r, at, (i * 4 + j) * 6 + k] = 1
    ef = np.zeros((80, 32), np.float32)
    for ch in range(3):
        for tap in range(9):
            ef[tap * 8 + ch, ch * 9 + tap] = 1
    pool = np.zeros((CG, HALF), np.float32)
    for c in range(HALF):
        pool[c // 4, c] = 1
    none = np.zeros((CG, HALF), np.float32)
    return dict(
        sel_x=sel_x.reshape(blocks * 64, width),
        sel_s=sel_s.reshape(blocks * 128, width),
        early_x=early_x,
        early_s=early_s,
        sel_o=sel_o.reshape(12 * rows + 32, blocks * 128),
        ex=ex.reshape(512, 48),
        eu=eu.reshape(1024, 96),
        ext=np.concatenate(list(np.swapaxes(ex, 1, 2)), 0),
        eut=np.concatenate(list(np.swapaxes(eu, 1, 2)), 0),
        ef=ef,
        eft=ef.T,
        pool_both=np.concatenate([pool, none, none, pool], 0),
    )


def gelu_both(pre):
    square = pre * pre
    t = jnp.tanh(pre * (GELU_B * square + GELU_A))
    gate = 0.5 + 0.5 * t
    value = pre * gate
    slope = gate + (value * (1.0 - gate)) * (6.0 * GELU_B * square + 2.0 * GELU_A)
    return value, slope


def moved(value, shift, lane, keep):
    width = value.shape[1]
    return jnp.where(keep(lane), pltpu.roll(value, shift % width, 1), 0.0)


def coarse_forward(blocks, tile, coarse_ref, w1_ref, second_t_ref, spread_ref, store, place):
    patches_s, columns_s, first_slope_s, second_slope_s, feature_s, wide_s = store
    cells = blocks * CG
    by_segment = coarse_ref[0, 0:SENT_INPUT, :].astype(F32)
    inputs = jnp.concatenate(
        [by_segment[at : at + 8] for at in range(0, SENT_INPUT, 8)], axis=1
    )
    lane_in = lax.broadcasted_iota(jnp.int32, inputs.shape, 1) % CG
    by_col = (
        moved(inputs, 2, lane_in, lambda x: x >= 2),
        inputs,
        moved(inputs, -2, lane_in, lambda x: x < CG - 2),
    )
    above = jnp.where(tile * blocks >= 4, 1.0, 0.0)
    below = jnp.where(tile * blocks + 4 <= CG - blocks, 1.0, 0.0)
    windows = []
    for window in range(3):
        pieces = []
        for row_tap in range(3):
            for col_tap in range(3):
                start = (4 * window + 2 * row_tap) * CG
                pieces.append(by_col[col_tap][:, start : start + cells])
        pieces.append(jnp.zeros((8, cells), F32))
        stacked = jnp.concatenate(pieces, axis=0)
        if window == 0:
            stacked = stacked * above
        if window == 2:
            stacked = stacked * below
        windows.append(stacked)
    patches = jnp.concatenate(windows, axis=1).astype(BF)
    first_value, first_slope = gelu_both(nn(w1_ref[...], patches))
    yield
    hidden = first_value.astype(BF)
    stacked = jnp.concatenate(
        [hidden[:, window * cells : (window + 1) * cells] for window in range(3)], axis=0
    )
    taps = nn(second_t_ref[...], stacked)
    lane_c = lax.broadcasted_iota(jnp.int32, (128, cells), 1) % CG
    second_pre = (
        taps[128:256]
        + moved(taps[0:128], 4, lane_c, lambda x: x >= 4)
        + moved(taps[256:384], -4, lane_c, lambda x: x < CG - 4)
    )
    second_value, second_slope = gelu_both(second_pre)
    yield
    feature = second_value.astype(BF)
    patches_s[place] = patches
    columns_s[place] = stacked
    first_slope_s[place] = first_slope
    second_slope_s[place] = second_slope
    feature_s[place] = feature
    pairs = [feature[:, at * 128 : (at + 1) * 128] for at in range(blocks // 2)]
    pairs = jnp.concatenate(pairs, axis=0) if blocks > 2 else pairs[0]
    for parity in range(2):
        wide = nn(pairs, spread_ref[parity * 128 : (parity + 1) * 128, :]).astype(BF)
        for at in range(blocks // 2):
            b = 2 * at + parity
            wide_s[place, :, b * HALF : (b + 1) * HALF] = wide[at * 128 : (at + 1) * 128]


def coarse_backward(blocks, d_project, project_ref, second_ref, store, place, dil_ref, pg_ref, fg_ref):
    patches_s, columns_s, first_slope_s, second_slope_s, feature_s, _ = store
    cells = blocks * CG
    pg_ref[...] += nt(feature_s[place], d_project)
    d_feature = nn(project_ref[...], d_project).astype(BF).astype(F32)
    d_second = (d_feature * second_slope_s[place]).astype(BF).astype(F32)
    yield
    lane_c = lax.broadcasted_iota(jnp.int32, (128, cells), 1) % CG
    shifted = jnp.concatenate(
        [
            moved(d_second, -4, lane_c, lambda x: x < CG - 4),
            d_second,
            moved(d_second, 4, lane_c, lambda x: x >= 4),
        ],
        axis=0,
    ).astype(BF)
    dil_ref[...] += nt(columns_s[place], shifted)
    back = nn(second_ref[...], shifted)
    yield
    d_first_hidden = jnp.concatenate([back[0:128], back[128:256], back[256:384]], axis=1)
    d_first = (d_first_hidden * first_slope_s[place]).astype(BF)
    fg_ref[...] += nt(patches_s[place], d_first)


def advance(stage):
    next(stage, None)


def finish(stage):
    for _ in stage:
        pass


def slot_kernel(
    blocks,
    peers,
    ids_ref,
    tile_ref,
    coarse_first_ref,
    coarse_a_ref,
    coarse_b_ref,
    fine_ref,
    cot_ref,
    before_ref,
    after_ref,
    later_ref,
    sel_x_ref,
    sel_s_ref,
    sel_o_ref,
    ex_ref,
    eu_ref,
    ext_ref,
    eut_ref,
    ef_ref,
    eft_ref,
    spread_ref,
    first_t_ref,
    second_t_ref,
    second_ref,
    project_ref,
    project_t_ref,
    down_t_ref,
    up_t_ref,
    up_ref,
    pred_ref,
    to_last_ref,
    to_first_ref,
    own_ref,
    sent_ref,
    dil_ref,
    pg_ref,
    w_ref,
    u_ref,
    ut_ref,
    w1_ref,
    gu_ref,
    gd_ref,
    fg_ref,
    d_project_ref,
    *store,
):
    step = pl.program_id(0)
    tile = tile_ref[0]
    chunk = GRAD_ROWS // peers

    def forward(source, place):
        return coarse_forward(
            blocks, tile, source, w1_ref, second_t_ref, spread_ref, store, place
        )

    def backward(place):
        return coarse_backward(
            blocks, d_project_ref[...], project_ref, second_ref, store, place, dil_ref, pg_ref, fg_ref
        )

    @pl.when(step == 0)
    def _():
        for r in range(4):
            rows = slice(r * 128, (r + 1) * 128)
            w_ref[rows, 0:128] = nt(down_t_ref[...], ex_ref[rows, :]).astype(BF)
            w_ref[rows, 128:256] = project_t_ref[...]
            taps = eu_ref[r * 256 : (r + 1) * 256, :]
            u_ref[rows, :] = nt(up_t_ref[...], taps).astype(BF)
            ut_ref[:, rows] = nn(taps, up_ref[...]).astype(BF)
        w1_ref[...] = nt(first_t_ref[...], ef_ref[...]).astype(BF)
        gu_ref[...] = jnp.zeros_like(gu_ref)
        gd_ref[...] = jnp.zeros_like(gd_ref)
        fg_ref[...] = jnp.zeros_like(fg_ref)
        dil_ref[...] = jnp.zeros_like(dil_ref)
        pg_ref[...] = jnp.zeros_like(pg_ref)
        d_project_ref[...] = jnp.zeros_like(d_project_ref)
        for buffer in store:
            buffer[2] = jnp.zeros(buffer.shape[1:], buffer.dtype)
        finish(forward(coarse_first_ref, 0))

    def one_slot(u, slot, now, soon, done):
        back = backward(done)
        ahead = forward((coarse_a_ref, coarse_b_ref)[u], soon)
        advance(back)
        later = jnp.concatenate([later_ref[u, 0:8, :], later_ref[u, 8:16, :]], axis=1)
        later_high = later.astype(BF).astype(F32)
        later_both = jnp.concatenate([later_high, later - later_high], axis=0).astype(BF)
        aux = [before_ref[u], after_ref[u], later_both]
        fine_all = nn(sel_x_ref[...], jnp.concatenate([fine_ref[u]] + aux, axis=0))
        slope_all = nn(sel_s_ref[...], jnp.concatenate([cot_ref[u]] + aux, axis=0))
        row = lax.broadcasted_iota(jnp.int32, (64, HALF), 0)
        flux_scale = jnp.where(row >= 32, SCALE, 1.0)
        outside = (row == 40) | (row == 50) | (row == 60)
        top_scale = jnp.where(outside & (tile == 0), 0.0, flux_scale)
        lane32 = lax.broadcasted_iota(jnp.int32, (32, HALF), 1)
        lane64 = lax.broadcasted_iota(jnp.int32, (64, HALF), 1)
        not_first = lambda x: x >= 1
        not_last = lambda x: x < HALF - 1

        def enter(b):
            x0 = fine_all[b * 64 : b * 64 + 32]
            x1 = fine_all[b * 64 + 32 : b * 64 + 64]
            x_taps = jnp.concatenate(
                [x0, x1, moved(x1, 1, lane32, not_first), moved(x0, -1, lane32, not_last)], axis=0
            ).astype(BF)
            scale = top_scale if b == 0 else flux_scale
            s0 = slope_all[b * 128 : b * 128 + 64] * scale
            s1 = slope_all[b * 128 + 64 : b * 128 + 128] * scale
            s_taps = jnp.concatenate(
                [s0, s1, moved(s1, 1, lane64, not_first), moved(s0, -1, lane64, not_last)], axis=0
            ).astype(BF)
            wide = store[5][now, :, b * HALF : (b + 1) * HALF]
            third = nn(w_ref[...], jnp.concatenate([x_taps, wide], axis=0))
            return x_taps, s_taps, third, nn(u_ref[...], s_taps)

        def middle(entered):
            x_taps, s_taps, third, d_hidden = entered
            value, slope = gelu_both(third)
            return x_taps, s_taps, value.astype(BF), (d_hidden * slope).astype(BF)

        def leave(b, held):
            hidden = held[2]
            taps = nn(ut_ref[...], hidden)
            c0 = taps[0:64] + moved(taps[192:256], 1, lane64, not_first)
            c1 = taps[64:128] + moved(taps[128:192], -1, lane64, not_last)
            return [c0 * flux_scale, c1 * flux_scale]

        def collect(even, odd):
            s_taps = jnp.concatenate([even[1], odd[1]], axis=1)
            hidden = jnp.concatenate([even[2], odd[2]], axis=1)
            gu_ref[...] += nt(hidden, s_taps)
            x_taps = jnp.concatenate(
                [
                    jnp.concatenate([even[0], odd[0]], axis=1),
                    jnp.concatenate([spread_ref[0:128, :], spread_ref[128:256, :]], axis=1),
                ],
                axis=0,
            )
            both = nt(jnp.concatenate([even[3], odd[3]], axis=1), x_taps)
            gd_ref[...] += both[:, 0:128]
            per_row = both[:, 128:256]
            return (per_row[0:128] + per_row[128:256]) + (per_row[256:384] + per_row[384:512])

        combined = []
        pooled = []
        entered = {}
        held = {}
        for turn in range(blocks + 2):
            if turn < blocks:
                entered[turn] = enter(turn)
            if turn == 1:
                advance(back)
            if turn == 2:
                finish(back)
            if 0 <= turn - 1 < blocks:
                held[turn - 1] = middle(entered.pop(turn - 1))
            if turn >= 3:
                advance(ahead)
            b = turn - 2
            if b >= 0:
                combined += leave(b, held[b])
                if b % 2 == 1:
                    pooled.append(collect(held[b - 1], held[b]))

        out = jnp.concatenate(combined, axis=0)
        finish(ahead)
        placed = nn(sel_o_ref[...], out.astype(BF))
        main = pred_ref.shape[1]
        pred_ref[u] = placed[0:main]
        before_flux = placed[main + 8 : main + 16]
        own = before_flux * jnp.where(tile >= 1, 1.0, 0.0)
        flux = placed[main + 24 : main + 32] + own
        to_last_ref[u] = placed[main : main + 8] + before_flux
        to_first_ref[u] = placed[main + 16 : main + 24]
        own_ref[u] = own
        flux = jnp.concatenate([flux[:, 0:128], flux[:, 128:256]], axis=0)
        sent_ref[slot, chunk : chunk + 16, :] = flux.astype(BF)
        d_project_ref[...] = jnp.concatenate(pooled, axis=1).astype(BF)

    for u in range(PER_STEP):
        slot = step * PER_STEP + u
        now = lax.rem(slot, 3)
        one_slot(u, slot, now, lax.rem(slot + 1, 3), lax.rem(slot + 2, 3))

    @pl.when(step == pl.num_programs(0) - 1)
    def _():
        finish(backward((pl.num_programs(0) * PER_STEP - 1) % 3))
        up = jnp.zeros((96, 128), F32)
        down = jnp.zeros((48, 128), F32)
        for r in range(4):
            lanes = slice(r * 128, (r + 1) * 128)
            up = up + exact_t(eut_ref[r * 96 : (r + 1) * 96, :], gu_ref[lanes, :])
            down = down + exact_t(ext_ref[r * 48 : (r + 1) * 48, :], gd_ref[lanes, :])
        first = exact(eft_ref[...], fg_ref[...])
        pieces = [
            dil_ref[i * 128 : (i + 1) * 128, j * 128 : (j + 1) * 128]
            for i in range(3)
            for j in range(3)
        ]
        pieces += [pg_ref[...], up, down, first]
        pieces.append(jnp.zeros((GRAD_ROWS - FIRST_AT - 32, 128), F32))
        grads = jnp.concatenate(pieces, axis=0).astype(BF)
        for t in range(peers):
            sent_ref[t, 0:chunk, :] = grads[t * chunk : (t + 1) * chunk, :]


def run_slots(peers, ids, tile, coarse, fine, cot, before, after, later, fixed, weights):
    slots, main, width = fine.shape
    blocks = main // 48
    cells = blocks * CG
    chunk = GRAD_ROWS // peers

    def coarse_of(ahead):
        return pl.BlockSpec(
            one, lambda n, ids, tile: (ids[jnp.minimum(n * PER_STEP + ahead, slots - 1)], 0, 0)
        )

    def whole(array):
        return pl.BlockSpec(array.shape, lambda n, ids, tile: (0,) * array.ndim)

    def per_slot(array):
        return pl.BlockSpec((PER_STEP,) + array.shape[1:], lambda n, ids, tile: (n, 0, 0))

    one = (1,) + coarse.shape[1:]
    in_specs = [
        pl.BlockSpec(one, lambda n, ids, tile: (ids[0], 0, 0)),
        coarse_of(1),
        coarse_of(2),
        per_slot(fine),
        per_slot(cot),
        per_slot(before),
        per_slot(after),
        per_slot(later),
    ] + [whole(a) for a in fixed + weights]
    edge = jax.ShapeDtypeStruct((slots, 8, width), F32)
    out_shape = [
        jax.ShapeDtypeStruct((slots, main, width), F32),
        edge,
        edge,
        edge,
        jax.ShapeDtypeStruct((peers, chunk + 16, 128), BF),
    ]
    grid_spec = pltpu.PrefetchScalarGridSpec(
        num_scalar_prefetch=2,
        grid=(slots // PER_STEP,),
        in_specs=in_specs,
        out_specs=[per_slot(a) for a in out_shape[:4]] + [whole(out_shape[4])],
        scratch_shapes=[
            pltpu.VMEM((384, 384), F32),
            pltpu.VMEM((128, 128), F32),
            pltpu.VMEM((512, 256), BF),
            pltpu.VMEM((512, 256), BF),
            pltpu.VMEM((256, 512), BF),
            pltpu.VMEM((128, 80), BF),
            pltpu.VMEM((512, 256), F32),
            pltpu.VMEM((512, 128), F32),
            pltpu.VMEM((80, 128), F32),
            pltpu.VMEM((128, cells), BF),
            pltpu.VMEM((3, 80, 3 * cells), BF),
            pltpu.VMEM((3, 384, cells), BF),
            pltpu.VMEM((3, 128, 3 * cells), F32),
            pltpu.VMEM((3, 128, cells), F32),
            pltpu.VMEM((3, 128, cells), BF),
            pltpu.VMEM((3, 128, blocks * HALF), BF),
        ],
    )

    def body(*refs):
        slot_kernel(blocks, peers, *refs)

    return pl.pallas_call(
        body,
        grid_spec=grid_spec,
        out_shape=out_shape,
        compiler_params=pltpu.CompilerParams(vmem_limit_bytes=52 * 1024 * 1024),
        cost_estimate=pl.CostEstimate(
            flops=slots * blocks * 500_000_000, bytes_accessed=16_000_000, transcendentals=0
        ),
    )(ids, tile, coarse, coarse, coarse, fine, cot, before, after, later, *fixed, *weights)


EARLY_SLOTS = 4


def early_kernel(
    blocks, peers, solution_ref, geometry_ref, fine_ref, cot_ref, x_ref, s_ref, sent_ref, last_ref, first_ref
):
    step = pl.program_id(0)

    @pl.when(step == 0)
    def _():
        inputs = jnp.concatenate(
            [
                solution_ref[0].astype(F32),
                geometry_ref[...].astype(F32),
                jnp.zeros((5, CG * CG), F32),
            ],
            axis=0,
        )
        edge = jnp.zeros((8, 6 * CG), F32)
        inputs = jnp.concatenate([edge, inputs, edge, jnp.zeros((8, 2 * CG), F32)], axis=1)
        for t in range(peers):
            for segment in range(0, SENT_INPUT // 8, 2):
                at = t * blocks * CG + segment * 128
                sent_ref[t, segment * 8 : segment * 8 + 16, :] = jnp.concatenate(
                    [inputs[:, at : at + 128], inputs[:, at + 128 : at + 256]], axis=0
                ).astype(BF)

    for u in range(EARLY_SLOTS):
        slot = step * EARLY_SLOTS + u
        picked = nn(x_ref[...], fine_ref[u]) + nn(s_ref[...], cot_ref[u])
        totals = jnp.concatenate(
            [picked[0:8, 0:128], picked[0:8, 128:256]], axis=0
        )
        high = totals.astype(BF)
        sent_ref[slot, SENT_INPUT : SENT_INPUT + 16, :] = high
        sent_ref[slot, SENT_INPUT + 16 : SENT_INPUT + 32, :] = (
            totals - high.astype(F32)
        ).astype(BF)
        last_ref[u] = picked[16:32].astype(BF)
        first_ref[u] = picked[32:48].astype(BF)


def run_early(peers, solution, geometry, fine, cot, pick_x, pick_s):
    slots, main, width = fine.shape

    def whole(array):
        return pl.BlockSpec(array.shape, lambda n: (0,) * array.ndim)

    def per_slots(array):
        return pl.BlockSpec((EARLY_SLOTS,) + array.shape[1:], lambda n: (n, 0, 0))

    edge = jax.ShapeDtypeStruct((slots, 16, width), BF)
    sent = jax.ShapeDtypeStruct((peers, SENT_EARLY, 128), BF)

    def body(*refs):
        early_kernel(main // 48, peers, *refs)

    return pl.pallas_call(
        body,
        grid=(slots // EARLY_SLOTS,),
        in_specs=[whole(solution), whole(geometry), per_slots(fine), per_slots(cot)]
        + [whole(pick_x), whole(pick_s)],
        out_specs=[whole(sent), per_slots(edge), per_slots(edge)],
        out_shape=[sent, edge, edge],
        compiler_params=pltpu.CompilerParams(vmem_limit_bytes=32 * 1024 * 1024),
    )(solution, geometry, fine, cot, pick_x, pick_s)


FINAL_SLOTS = 4
PARTS = ((0, 1152), (PROJECT_AT, 128), (UP_AT, 96), (DOWN_AT, 48), (FIRST_AT, 32))


def final_kernel(chunk, rows, back_ref, pred_ref, own_ref, first_ref, last_ref, out_ref, *grads):
    step = pl.program_id(0)

    @pl.when(step == 0)
    def _():
        for (start, size), grad in zip(PARTS, grads):
            at = start
            while at < start + size:
                t = at // chunk
                stop = min((t + 1) * chunk, start + size)
                grad[at - start : stop - start, :] = back_ref[
                    t, at - t * chunk : stop - t * chunk, :
                ].astype(F32)
                at = stop

    row = lax.broadcasted_iota(jnp.int32, (rows, HALF), 0)
    for s in range(out_ref.shape[0]):
        slot = step * out_ref.shape[0] + s
        ahead = back_ref[slot, chunk : chunk + 16, :].astype(F32)
        base = jnp.concatenate([ahead[0:8], ahead[8:16]], axis=1) + own_ref[s]
        for k in range(3):
            for p in range(2):
                for q in range(2):
                    at = ((k * 2 + p) * 2 + q) * rows
                    pick = slice(k * 2 + q, k * 2 + q + 1)
                    edge = (first_ref if p == 0 else last_ref)[s, pick, :]
                    reached = row == (0 if p == 0 else rows - 1)
                    out_ref[s, at : at + rows, :] = (
                        pred_ref[s, at : at + rows, :]
                        + base[pick]
                        + jnp.where(reached, edge, 0.0)
                    ).astype(BF)


def run_final(back, pred, own, first, last):
    slots, main, width = pred.shape
    chunk = back.shape[1] - 16
    held = FINAL_SLOTS if main % 192 == 0 else 2 * FINAL_SLOTS

    def per_slots(array):
        return pl.BlockSpec((held,) + array.shape[1:], lambda n: (n, 0, 0))

    def body(*refs):
        final_kernel(chunk, main // 12, *refs)

    return pl.pallas_call(
        body,
        grid=(slots // held,),
        in_specs=[pl.BlockSpec(back.shape, lambda n: (0, 0, 0))]
        + [per_slots(a) for a in (pred, own, first, last)],
        out_specs=[per_slots(pred)]
        + [pl.BlockSpec((size, 128), lambda n: (0, 0)) for _, size in PARTS],
        out_shape=[jax.ShapeDtypeStruct(pred.shape, BF)]
        + [jax.ShapeDtypeStruct((size, 128), F32) for _, size in PARTS],
        compiler_params=pltpu.CompilerParams(vmem_limit_bytes=32 * 1024 * 1024),
    )(back, pred, own, first, last)


def exchanged(value):
    return lax.all_to_all(value, "tile", split_axis=0, concat_axis=0, tiled=True)


def local(
    coarse_solution,
    geometry,
    fine_fields,
    cotangent,
    sample_ids,
    first_weight,
    dilated_weight,
    project_weight,
    down_weight,
    up_weight,
):
    peers = lax.axis_size("tile")
    position = lax.axis_index("tile")
    slots, rows = fine_fields.shape[0], fine_fields.shape[4]
    up = [(i, i + 1) for i in range(peers - 1)]
    down = [(i + 1, i) for i in range(peers - 1)]

    made = constants(rows)
    fine = fine_fields.reshape(slots, 12 * rows, HALF)
    cot = cotangent.reshape(slots, 12 * rows, HALF)

    sent, edge_last, edge_first = run_early(
        peers,
        coarse_solution,
        geometry,
        fine,
        cot,
        jnp.asarray(made["early_x"], BF),
        jnp.asarray(made["early_s"], BF),
    )
    coarse = exchanged(sent)
    from_before = lax.ppermute(edge_last, "tile", up)
    from_after = lax.ppermute(edge_first, "tile", down)
    sums = coarse[:, SENT_INPUT:].astype(F32)
    sums = sums[:, :16] + sums[:, 16:]
    order = lax.broadcasted_iota(jnp.int32, (peers, peers), 0)
    other = lax.broadcasted_iota(jnp.int32, (peers, peers), 1)
    behind = jnp.sum(jnp.where((other > order)[:, :, None, None], sums[None], 0.0), axis=1)
    later = exchanged(behind)

    fixed = [
        jnp.asarray(made["sel_x"], BF),
        jnp.asarray(made["sel_s"], BF),
        jnp.asarray(made["sel_o"], BF),
        jnp.asarray(made["ex"], BF),
        jnp.asarray(made["eu"], BF),
        jnp.asarray(made["ext"], F32),
        jnp.asarray(made["eut"], F32),
        jnp.asarray(made["ef"], BF),
        jnp.asarray(made["eft"], F32),
        jnp.asarray(made["pool_both"], BF),
    ]
    second = dilated_weight
    up_flat = up_weight.reshape(96, 128)
    weights = [
        jnp.pad(first_weight.reshape(27, 128), ((0, 5), (0, 0))).T,
        jnp.transpose(second, (1, 3, 0, 2)).reshape(384, 384),
        jnp.transpose(second, (0, 2, 1, 3)).reshape(384, 384),
        project_weight,
        project_weight.T,
        down_weight.reshape(48, 128).T,
        up_flat.T,
        up_flat,
    ]
    pred_local, last_edge, first_edge, own, sent = run_slots(
        peers,
        sample_ids,
        position.reshape(1).astype(jnp.int32),
        coarse,
        fine,
        cot,
        from_before,
        from_after,
        later,
        fixed,
        weights,
    )

    chunk = GRAD_ROWS // peers
    got = exchanged(sent).astype(F32)
    to_first = lax.ppermute(first_edge, "tile", up)
    to_last = lax.ppermute(last_edge, "tile", down)
    reduced = jnp.sum(got[:, :chunk], axis=0).astype(BF)
    sums = got[:, chunk:]
    ahead = jnp.sum(jnp.where((other < order)[:, :, None, None], sums[None], 0.0), axis=1)
    reduced, to_first, to_last = lax.optimization_barrier((reduced, to_first, to_last))
    back = exchanged(
        jnp.concatenate(
            [
                jnp.broadcast_to(reduced, (peers, chunk, 128)),
                ahead.astype(BF),
            ],
            axis=1,
        )
    )
    prediction, dilated, project, up_grad, down_grad, first = run_final(
        back, pred_local, own, to_first, to_last
    )
    return (
        prediction.reshape(fine_fields.shape),
        first[0:27].reshape(first_weight.shape),
        dilated.reshape(dilated_weight.shape),
        project,
        down_grad.reshape(down_weight.shape),
        up_grad.reshape(up_weight.shape),
    )


def solution(mesh):
    in_specs = (
        P(("groups", "tile"), None, None),
        P(("groups", "tile"), None),
        P("groups", None, None, None, "tile", None),
        P("groups", None, None, None, "tile", None),
        P("groups"),
        P(),
        P(),
        P(),
        P(),
        P(),
    )
    out_specs = (
        P("groups", None, None, None, "tile", None),
        P("groups", None, None, None),
        P("groups", None, None, None),
        P("groups", None),
        P("groups", None, None, None),
        P("groups", None, None, None),
    )
    return jax.shard_map(local, mesh=mesh, in_specs=in_specs, out_specs=out_specs, check_vma=False)
```

```python
import math

import jax
import jax.numpy as jnp
import numpy as np
from jax import lax
from jax.experimental import pallas as pl
from jax.experimental.pallas import tpu as pltpu
from jax.sharding import PartitionSpec as P

CG = 64
FG = 512
HALF = FG // 2
SCALE = 1.0 / math.sqrt(FG)
GELU_A = math.sqrt(2.0 / math.pi)
GELU_B = GELU_A * 0.044715
BF = jnp.bfloat16
F32 = jnp.float32

AUX = 64
SENT_INPUT = 32
SENT_EARLY = SENT_INPUT + 32
PER_STEP = 4
GRAD_ROWS = 1536
UP_AT, DOWN_AT, FIRST_AT, PROJECT_AT = 1280, 1376, 1424, 1152


def nn(a, b):
    return lax.dot_general(a, b, (((1,), (0,)), ((), ())), preferred_element_type=F32)


def nt(a, b):
    return lax.dot_general(a, b, (((1,), (1,)), ((), ())), preferred_element_type=F32)


def halves(value):
    high = value.astype(BF)
    return high, (value - high.astype(F32)).astype(BF)


def row_at(tap, r):
    if tap == 0:
        return 8 if r == 0 else 4 + r - 1
    if tap == 1:
        return r
    if tap == 2:
        return 4 + r
    return 9 if r == 3 else r + 1


def fine_row(block, index):
    if index == 8:
        return 8 * block - 1
    if index == 9:
        return 8 * block + 8
    return 8 * block + 2 * (index % 4) + index // 4


COL_GROUP = (2, 0, 1, 3)


def constants(rows):
    blocks = rows // 4
    last = 2 * rows
    width = 12 * rows + AUX

    def held(ch, q, o):
        return ((ch * 2 + o % 2) * 2 + q) * rows + o // 2

    sel_x = np.zeros((blocks, 2, 32, width), np.float32)
    sel_s = np.zeros((blocks, 2, 64, width), np.float32)
    sel_o = np.zeros((12 * rows + 32, blocks, 2, 64), np.float32)
    base = 12 * rows
    for b in range(blocks):
        for q in range(2):
            for ch in range(3):
                for index in range(10):
                    o = fine_row(b, index)
                    at = ch * 10 + index
                    if o == -1:
                        sel_x[b, q, at, base + ch * 2 + q] = 1
                        sel_s[b, q, at, base + 6 + ch * 2 + q] = 1
                        sel_s[b, q, 32 + at, base + 6 + ch * 2 + q] = 1
                    elif o == last:
                        sel_x[b, q, at, base + 16 + ch * 2 + q] = 1
                        sel_s[b, q, at, base + 22 + ch * 2 + q] = 1
                    else:
                        sel_x[b, q, at, held(ch, q, o)] = 1
                        sel_s[b, q, at, held(ch, q, o)] = 1
                    for later in range(max(o, 0), last):
                        sel_s[b, q, 32 + at, held(ch, q, later)] = 1
                    sel_s[b, q, 32 + at, base + 32 + ch * 2 + q] = 1
                    sel_s[b, q, 32 + at, base + 40 + ch * 2 + q] = 1
                    for target in range(max(o, 0), last):
                        if target == o:
                            sel_o[held(ch, q, target), b, q, at] = 1
                        if o >= 0:
                            sel_o[held(ch, q, target), b, q, 32 + at] = 1
                    if o == -1:
                        sel_o[base + ch * 2 + q, b, q, at] = 1
                        sel_o[base + 8 + ch * 2 + q, b, q, 32 + at] = 1
                    else:
                        sel_o[base + 24 + ch * 2 + q, b, q, 32 + at] = 1
                    if o == last:
                        sel_o[base + 16 + ch * 2 + q, b, q, at] = 1
    early_x = np.zeros((48, 12 * rows), np.float32)
    early_s = np.zeros((48, 12 * rows), np.float32)
    for ch in range(3):
        for q in range(2):
            at = ch * 2 + q
            for o in range(last):
                early_s[at, held(ch, q, o)] = 1
            for start, o in ((16, last - 1), (32, 0)):
                early_x[start + at, held(ch, q, o)] = 1
                early_s[start + 6 + at, held(ch, q, o)] = 1
    ex = np.zeros((4, 128, 48), np.float32)
    eu = np.zeros((4, 256, 96), np.float32)
    for r in range(4):
        for i in range(4):
            for j in range(4):
                for ch in range(3):
                    ex[r, COL_GROUP[j] * 32 + ch * 10 + row_at(i, r), (ch * 4 + i) * 4 + j] = 1
                for k in range(6):
                    at = COL_GROUP[j] * 64 + (k // 3) * 32 + (k % 3) * 10 + row_at(i, r)
                    eu[r, at, (i * 4 + j) * 6 + k] = 1
    ef = np.zeros((80, 32), np.float32)
    for ch in range(3):
        for tap in range(9):
            ef[tap * 8 + ch, ch * 9 + tap] = 1
    pool = np.zeros((CG, HALF), np.float32)
    for c in range(HALF):
        pool[c // 4, c] = 1
    none = np.zeros((CG, HALF), np.float32)
    return dict(
        sel_x=sel_x.reshape(blocks * 64, width),
        sel_s=sel_s.reshape(blocks * 128, width),
        early_x=early_x,
        early_s=early_s,
        sel_o=sel_o.reshape(12 * rows + 32, blocks * 128),
        ex=ex.reshape(512, 48),
        eu=eu.reshape(1024, 96),
        ext=np.concatenate(list(np.swapaxes(ex, 1, 2)), 1),
        eut=np.concatenate(list(np.swapaxes(eu, 1, 2)), 1),
        ef=ef,
        eft=ef.T,
        pool_both=np.concatenate([pool, none, none, pool], 0),
    )


def gelu_both(pre):
    square = pre * pre
    t = jnp.tanh(pre * (GELU_B * square + GELU_A))
    gate = 0.5 + 0.5 * t
    value = pre * gate
    slope = gate + (value * (1.0 - gate)) * (6.0 * GELU_B * square + 2.0 * GELU_A)
    return value, slope


def moved(value, shift, lane, keep):
    width = value.shape[1]
    return jnp.where(keep(lane), pltpu.roll(value, shift % width, 1), 0.0)


def coarse_forward(blocks, tile, coarse_ref, w1_ref, second_t_ref, spread_ref, store, place):
    patches_s, columns_s, first_slope_s, second_slope_s, feature_s, wide_s = store
    cells = blocks * CG
    by_segment = coarse_ref[0, 0:SENT_INPUT, :].astype(F32)
    inputs = jnp.concatenate(
        [by_segment[at : at + 4] for at in range(0, SENT_INPUT, 4)], axis=1
    )
    inputs = jnp.concatenate([inputs, jnp.zeros_like(inputs)], axis=0)
    lane_in = lax.broadcasted_iota(jnp.int32, inputs.shape, 1) % CG
    by_col = (
        moved(inputs, 2, lane_in, lambda x: x >= 2),
        inputs,
        moved(inputs, -2, lane_in, lambda x: x < CG - 2),
    )
    above = jnp.where(tile * blocks >= 4, 1.0, 0.0)
    below = jnp.where(tile * blocks + 4 <= CG - blocks, 1.0, 0.0)
    windows = []
    for window in range(3):
        pieces = []
        for row_tap in range(3):
            for col_tap in range(3):
                start = (4 * window + 2 * row_tap) * CG
                pieces.append(by_col[col_tap][:, start : start + cells])
        pieces.append(jnp.zeros((8, cells), F32))
        stacked = jnp.concatenate(pieces, axis=0)
        if window == 0:
            stacked = stacked * above
        if window == 2:
            stacked = stacked * below
        windows.append(stacked)
    patches = jnp.concatenate(windows, axis=1).astype(BF)
    first_value, first_slope = gelu_both(nn(w1_ref[...], patches))
    yield
    hidden = first_value.astype(BF)
    stacked = jnp.concatenate(
        [hidden[:, window * cells : (window + 1) * cells] for window in range(3)], axis=0
    )
    taps = nn(second_t_ref[...], stacked)
    lane_c = lax.broadcasted_iota(jnp.int32, (128, cells), 1) % CG
    second_pre = (
        taps[128:256]
        + moved(taps[0:128], 4, lane_c, lambda x: x >= 4)
        + moved(taps[256:384], -4, lane_c, lambda x: x < CG - 4)
    )
    second_value, second_slope = gelu_both(second_pre)
    yield
    feature = second_value.astype(BF)
    patches_s[place] = patches
    columns_s[place] = stacked
    first_slope_s[place] = first_slope
    second_slope_s[place] = second_slope
    feature_s[place] = feature
    pairs = [feature[:, at * 128 : (at + 1) * 128] for at in range(blocks // 2)]
    pairs = jnp.concatenate(pairs, axis=0) if blocks > 2 else pairs[0]
    for parity in range(2):
        wide = nn(pairs, spread_ref[parity * 128 : (parity + 1) * 128, :]).astype(BF)
        for at in range(blocks // 2):
            b = 2 * at + parity
            wide_s[place, :, b * HALF : (b + 1) * HALF] = wide[at * 128 : (at + 1) * 128]


def coarse_backward(blocks, d_project, project_ref, second_ref, store, place, dil_ref, pg_ref, fg_ref):
    patches_s, columns_s, first_slope_s, second_slope_s, feature_s, _ = store
    cells = blocks * CG
    pg_ref[...] += nt(feature_s[place], d_project)
    d_feature = nn(project_ref[...], d_project).astype(BF).astype(F32)
    d_second = (d_feature * second_slope_s[place]).astype(BF).astype(F32)
    yield
    lane_c = lax.broadcasted_iota(jnp.int32, (128, cells), 1) % CG
    shifted = jnp.concatenate(
        [
            moved(d_second, -4, lane_c, lambda x: x < CG - 4),
            d_second,
            moved(d_second, 4, lane_c, lambda x: x >= 4),
        ],
        axis=0,
    ).astype(BF)
    dil_ref[...] += nt(columns_s[place], shifted)
    back = nn(second_ref[...], shifted)
    yield
    d_first_hidden = jnp.concatenate([back[0:128], back[128:256], back[256:384]], axis=1)
    d_first = (d_first_hidden * first_slope_s[place]).astype(BF)
    fg_ref[...] += nt(patches_s[place], d_first)


def advance(stage):
    next(stage, None)


def finish(stage):
    for _ in stage:
        pass


def slot_kernel(
    blocks,
    peers,
    ids_ref,
    tile_ref,
    coarse_first_ref,
    coarse_refs,
    fine_ref,
    cot_ref,
    before_ref,
    after_ref,
    later_ref,
    sel_x_ref,
    sel_s_ref,
    sel_o_ref,
    ex_ref,
    eu_ref,
    ext_ref,
    eut_ref,
    ef_ref,
    eft_ref,
    spread_ref,
    first_t_ref,
    second_t_ref,
    second_ref,
    project_ref,
    project_t_ref,
    down_t_ref,
    up_t_ref,
    up_ref,
    pred_ref,
    to_last_ref,
    to_first_ref,
    own_ref,
    sent_ref,
    dil_ref,
    pg_ref,
    w_ref,
    u_ref,
    ut_ref,
    w1_ref,
    gu_ref,
    gd_ref,
    fg_ref,
    d_project_ref,
    *store,
):
    step = pl.program_id(0)
    tile = tile_ref[0]
    chunk = GRAD_ROWS // peers

    def forward(source, place):
        return coarse_forward(
            blocks, tile, source, w1_ref, second_t_ref, spread_ref, store, place
        )

    def backward(place):
        return coarse_backward(
            blocks, d_project_ref[...], project_ref, second_ref, store, place, dil_ref, pg_ref, fg_ref
        )

    @pl.when(step == 0)
    def _():
        for r in range(4):
            rows = slice(r * 128, (r + 1) * 128)
            w_ref[rows, 0:128] = nt(down_t_ref[...], ex_ref[rows, :]).astype(BF)
            w_ref[rows, 128:256] = project_t_ref[...]
            taps = eu_ref[r * 256 : (r + 1) * 256, :]
            u_ref[rows, :] = nt(up_t_ref[...], taps).astype(BF)
            ut_ref[:, rows] = nn(taps, up_ref[...]).astype(BF)
        w1_ref[...] = nt(first_t_ref[...], ef_ref[...]).astype(BF)
        gu_ref[...] = jnp.zeros_like(gu_ref)
        gd_ref[...] = jnp.zeros_like(gd_ref)
        fg_ref[...] = jnp.zeros_like(fg_ref)
        dil_ref[...] = jnp.zeros_like(dil_ref)
        pg_ref[...] = jnp.zeros_like(pg_ref)
        d_project_ref[...] = jnp.zeros_like(d_project_ref)
        for buffer in store:
            buffer[2] = jnp.zeros(buffer.shape[1:], buffer.dtype)
        finish(forward(coarse_first_ref, 0))

    def one_slot(u, slot, now, soon, done):
        back = backward(done)
        ahead = forward(coarse_refs[u], soon)
        advance(back)
        later = jnp.concatenate([later_ref[u, 0:8, :], later_ref[u, 8:16, :]], axis=1)
        later_high = later.astype(BF).astype(F32)
        later_both = jnp.concatenate([later_high, later - later_high], axis=0).astype(BF)
        aux = [before_ref[u], after_ref[u], later_both, jnp.zeros((16, HALF), BF)]
        fine_all = nn(sel_x_ref[...], jnp.concatenate([fine_ref[u]] + aux, axis=0))
        slope_all = nn(sel_s_ref[...], jnp.concatenate([cot_ref[u]] + aux, axis=0))
        row = lax.broadcasted_iota(jnp.int32, (64, HALF), 0)
        flux_scale = jnp.where(row >= 32, SCALE, 1.0)
        outside = (row == 40) | (row == 50) | (row == 60)
        top_scale = jnp.where(outside & (tile == 0), 0.0, flux_scale)
        lane32 = lax.broadcasted_iota(jnp.int32, (32, HALF), 1)
        lane64 = lax.broadcasted_iota(jnp.int32, (64, HALF), 1)
        not_first = lambda x: x >= 1
        not_last = lambda x: x < HALF - 1

        def enter(b):
            x0 = fine_all[b * 64 : b * 64 + 32]
            x1 = fine_all[b * 64 + 32 : b * 64 + 64]
            x_taps = jnp.concatenate(
                [x0, x1, moved(x1, 1, lane32, not_first), moved(x0, -1, lane32, not_last)], axis=0
            ).astype(BF)
            scale = top_scale if b == 0 else flux_scale
            s0 = slope_all[b * 128 : b * 128 + 64] * scale
            s1 = slope_all[b * 128 + 64 : b * 128 + 128] * scale
            s_taps = jnp.concatenate(
                [s0, s1, moved(s1, 1, lane64, not_first), moved(s0, -1, lane64, not_last)], axis=0
            ).astype(BF)
            wide = store[5][now, :, b * HALF : (b + 1) * HALF]
            third = nn(w_ref[...], jnp.concatenate([x_taps, wide], axis=0))
            return x_taps, s_taps, third, nn(u_ref[...], s_taps)

        def middle(entered):
            x_taps, s_taps, third, d_hidden = entered
            value, slope = gelu_both(third)
            return x_taps, s_taps, value.astype(BF), (d_hidden * slope).astype(BF)

        def leave(b, held):
            hidden = held[2]
            taps = nn(ut_ref[...], hidden)
            c0 = taps[0:64] + moved(taps[192:256], 1, lane64, not_first)
            c1 = taps[64:128] + moved(taps[128:192], -1, lane64, not_last)
            return [c0 * flux_scale, c1 * flux_scale]

        def collect(even, odd):
            s_taps = jnp.concatenate([even[1], odd[1]], axis=1)
            hidden = jnp.concatenate([even[2], odd[2]], axis=1)
            gu_ref[...] += nt(hidden, s_taps)
            x_taps = jnp.concatenate(
                [
                    jnp.concatenate([even[0], odd[0]], axis=1),
                    jnp.concatenate([spread_ref[0:128, :], spread_ref[128:256, :]], axis=1),
                ],
                axis=0,
            )
            both = nt(jnp.concatenate([even[3], odd[3]], axis=1), x_taps)
            gd_ref[...] += both[:, 0:128]
            per_row = both[:, 128:256]
            return (per_row[0:128] + per_row[128:256]) + (per_row[256:384] + per_row[384:512])

        combined = []
        pooled = []
        entered = {}
        held = {}
        for turn in range(blocks + 2):
            if turn < blocks:
                entered[turn] = enter(turn)
            if turn == 1:
                advance(back)
            if turn == 2:
                finish(back)
            if 0 <= turn - 1 < blocks:
                held[turn - 1] = middle(entered.pop(turn - 1))
            if turn >= 3:
                advance(ahead)
            b = turn - 2
            if b >= 0:
                combined += leave(b, held[b])
                if b % 2 == 1:
                    pooled.append(collect(held[b - 1], held[b]))

        out = jnp.concatenate(combined, axis=0)
        finish(ahead)
        placed = nn(sel_o_ref[...], out.astype(BF))
        main = pred_ref.shape[1]
        pred_ref[u] = placed[0:main]
        before_flux = placed[main + 8 : main + 16]
        own = before_flux * jnp.where(tile >= 1, 1.0, 0.0)
        flux = placed[main + 24 : main + 32] + own
        to_last_ref[u] = placed[main : main + 8] + before_flux
        to_first_ref[u] = placed[main + 16 : main + 24]
        own_ref[u] = own
        flux = jnp.concatenate([flux[:, 0:128], flux[:, 128:256]], axis=0)
        sent_ref[slot, chunk : chunk + 16, :] = flux.astype(BF)
        d_project_ref[...] = jnp.concatenate(pooled, axis=1).astype(BF)

    for u in range(PER_STEP):
        slot = step * PER_STEP + u
        now = lax.rem(slot, 3)
        one_slot(u, slot, now, lax.rem(slot + 1, 3), lax.rem(slot + 2, 3))

    @pl.when(step == pl.num_programs(0) - 1)
    def _():
        finish(backward((pl.num_programs(0) * PER_STEP - 1) % 3))
        rows = [slice(r * 128, (r + 1) * 128) for r in range(4)]
        taps = halves(jnp.concatenate([gu_ref[at, :] for at in rows], axis=1))
        up = nt(eut_ref[...], taps[0]) + nt(eut_ref[...], taps[1])
        taps = halves(jnp.concatenate([gd_ref[at, :] for at in rows], axis=1))
        down = nt(ext_ref[...], taps[0]) + nt(ext_ref[...], taps[1])
        taps = halves(fg_ref[...])
        first = nn(eft_ref[...], taps[0]) + nn(eft_ref[...], taps[1])
        pieces = [
            dil_ref[i * 128 : (i + 1) * 128, j * 128 : (j + 1) * 128]
            for i in range(3)
            for j in range(3)
        ]
        pieces += [pg_ref[...], up, down, first]
        pieces.append(jnp.zeros((GRAD_ROWS - FIRST_AT - 32, 128), F32))
        grads = jnp.concatenate(pieces, axis=0).astype(BF)
        for t in range(peers):
            sent_ref[t, 0:chunk, :] = grads[t * chunk : (t + 1) * chunk, :]


def run_slots(peers, ids, tile, coarse, fine, cot, before, after, later, fixed, weights):
    slots, main, width = fine.shape
    blocks = main // 48
    cells = blocks * CG
    chunk = GRAD_ROWS // peers

    def coarse_of(ahead):
        return pl.BlockSpec(
            one, lambda n, ids, tile: (ids[jnp.minimum(n * PER_STEP + ahead, slots - 1)], 0, 0)
        )

    def whole(array):
        return pl.BlockSpec(array.shape, lambda n, ids, tile: (0,) * array.ndim)

    def per_slot(array):
        return pl.BlockSpec((PER_STEP,) + array.shape[1:], lambda n, ids, tile: (n, 0, 0))

    one = (1,) + coarse.shape[1:]
    in_specs = [
        pl.BlockSpec(one, lambda n, ids, tile: (ids[0], 0, 0)),
        *[coarse_of(ahead + 1) for ahead in range(PER_STEP)],
        per_slot(fine),
        per_slot(cot),
        per_slot(before),
        per_slot(after),
        per_slot(later),
    ] + [whole(a) for a in fixed + weights]
    edge = jax.ShapeDtypeStruct((slots, 8, width), F32)
    out_shape = [
        jax.ShapeDtypeStruct((slots, main, width), F32),
        edge,
        edge,
        edge,
        jax.ShapeDtypeStruct((peers, chunk + 16, 128), BF),
    ]
    grid_spec = pltpu.PrefetchScalarGridSpec(
        num_scalar_prefetch=2,
        grid=(slots // PER_STEP,),
        in_specs=in_specs,
        out_specs=[per_slot(a) for a in out_shape[:4]] + [whole(out_shape[4])],
        scratch_shapes=[
            pltpu.VMEM((384, 384), F32),
            pltpu.VMEM((128, 128), F32),
            pltpu.VMEM((512, 256), BF),
            pltpu.VMEM((512, 256), BF),
            pltpu.VMEM((256, 512), BF),
            pltpu.VMEM((128, 80), BF),
            pltpu.VMEM((512, 256), F32),
            pltpu.VMEM((512, 128), F32),
            pltpu.VMEM((80, 128), F32),
            pltpu.VMEM((128, cells), BF),
            pltpu.VMEM((3, 80, 3 * cells), BF),
            pltpu.VMEM((3, 384, cells), BF),
            pltpu.VMEM((3, 128, 3 * cells), F32),
            pltpu.VMEM((3, 128, cells), F32),
            pltpu.VMEM((3, 128, cells), BF),
            pltpu.VMEM((3, 128, blocks * HALF), BF),
        ],
    )

    def body(*refs):
        slot_kernel(blocks, peers, *refs[:3], refs[3 : 3 + PER_STEP], *refs[3 + PER_STEP :])

    return pl.pallas_call(
        body,
        grid_spec=grid_spec,
        out_shape=out_shape,
        compiler_params=pltpu.CompilerParams(vmem_limit_bytes=52 * 1024 * 1024),
        cost_estimate=pl.CostEstimate(
            flops=slots * blocks * 500_000_000, bytes_accessed=16_000_000, transcendentals=0
        ),
    )(ids, tile, *[coarse] * (PER_STEP + 1), fine, cot, before, after, later, *fixed, *weights)


EARLY_SLOTS = 4


def early_kernel(
    blocks, peers, solution_ref, geometry_ref, fine_ref, cot_ref, x_ref, s_ref, sent_ref, last_ref, first_ref
):
    step = pl.program_id(0)

    @pl.when(step == 0)
    def _():
        inputs = jnp.concatenate(
            [
                solution_ref[0].astype(F32),
                geometry_ref[...].astype(F32),
                jnp.zeros((5, CG * CG), F32),
            ],
            axis=0,
        )
        edge = jnp.zeros((8, 6 * CG), F32)
        inputs = jnp.concatenate([edge, inputs, edge, jnp.zeros((8, 2 * CG), F32)], axis=1)
        for t in range(peers):
            at = t * blocks * CG
            sent_ref[t, 0:SENT_INPUT, :] = jnp.concatenate(
                [
                    inputs[0:4, at + segment * 128 : at + segment * 128 + 128]
                    for segment in range(SENT_INPUT // 4)
                ],
                axis=0,
            ).astype(BF)

    for u in range(EARLY_SLOTS):
        slot = step * EARLY_SLOTS + u
        picked = nn(x_ref[...], fine_ref[u]) + nn(s_ref[...], cot_ref[u])
        totals = jnp.concatenate(
            [picked[0:8, 0:128], picked[0:8, 128:256]], axis=0
        )
        high = totals.astype(BF)
        sent_ref[slot, SENT_INPUT : SENT_INPUT + 16, :] = high
        sent_ref[slot, SENT_INPUT + 16 : SENT_INPUT + 32, :] = (
            totals - high.astype(F32)
        ).astype(BF)
        last_ref[u] = picked[16:32].astype(BF)
        first_ref[u] = picked[32:48].astype(BF)


def run_early(peers, solution, geometry, fine, cot, pick_x, pick_s):
    slots, main, width = fine.shape

    def whole(array):
        return pl.BlockSpec(array.shape, lambda n: (0,) * array.ndim)

    def per_slots(array):
        return pl.BlockSpec((EARLY_SLOTS,) + array.shape[1:], lambda n: (n, 0, 0))

    edge = jax.ShapeDtypeStruct((slots, 16, width), BF)
    sent = jax.ShapeDtypeStruct((peers, SENT_EARLY, 128), BF)

    def body(*refs):
        early_kernel(main // 48, peers, *refs)

    return pl.pallas_call(
        body,
        grid=(slots // EARLY_SLOTS,),
        in_specs=[whole(solution), whole(geometry), per_slots(fine), per_slots(cot)]
        + [whole(pick_x), whole(pick_s)],
        out_specs=[whole(sent), per_slots(edge), per_slots(edge)],
        out_shape=[sent, edge, edge],
        compiler_params=pltpu.CompilerParams(vmem_limit_bytes=60 * 1024 * 1024),
    )(solution, geometry, fine, cot, pick_x, pick_s)


FINAL_SLOTS = 4
PARTS = ((0, 1152), (PROJECT_AT, 128), (UP_AT, 96), (DOWN_AT, 48), (FIRST_AT, 32))


def final_kernel(chunk, rows, back_ref, pred_ref, own_ref, first_ref, last_ref, out_ref, *grads):
    step = pl.program_id(0)

    @pl.when(step == 0)
    def _():
        for (start, size), grad in zip(PARTS, grads):
            at = start
            while at < start + size:
                t = at // chunk
                stop = min((t + 1) * chunk, start + size)
                grad[at - start : stop - start, :] = back_ref[
                    t, at - t * chunk : stop - t * chunk, :
                ].astype(F32)
                at = stop

    row = lax.broadcasted_iota(jnp.int32, (rows, HALF), 0)
    for s in range(out_ref.shape[0]):
        slot = step * out_ref.shape[0] + s
        ahead = back_ref[slot, chunk : chunk + 16, :].astype(F32)
        base = jnp.concatenate([ahead[0:8], ahead[8:16]], axis=1) + own_ref[s]
        for k in range(3):
            for p in range(2):
                for q in range(2):
                    at = ((k * 2 + p) * 2 + q) * rows
                    pick = slice(k * 2 + q, k * 2 + q + 1)
                    edge = (first_ref if p == 0 else last_ref)[s, pick, :]
                    reached = row == (0 if p == 0 else rows - 1)
                    out_ref[s, at : at + rows, :] = (
                        pred_ref[s, at : at + rows, :]
                        + base[pick]
                        + jnp.where(reached, edge, 0.0)
                    ).astype(BF)


def run_final(back, pred, own, first, last):
    slots, main, width = pred.shape
    chunk = back.shape[1] - 16
    held = FINAL_SLOTS if main % 192 == 0 else 2 * FINAL_SLOTS

    def per_slots(array):
        return pl.BlockSpec((held,) + array.shape[1:], lambda n: (n, 0, 0))

    def body(*refs):
        final_kernel(chunk, main // 12, *refs)

    return pl.pallas_call(
        body,
        grid=(slots // held,),
        in_specs=[pl.BlockSpec(back.shape, lambda n: (0, 0, 0))]
        + [per_slots(a) for a in (pred, own, first, last)],
        out_specs=[per_slots(pred)]
        + [pl.BlockSpec((size, 128), lambda n: (0, 0)) for _, size in PARTS],
        out_shape=[jax.ShapeDtypeStruct(pred.shape, BF)]
        + [jax.ShapeDtypeStruct((size, 128), F32) for _, size in PARTS],
        compiler_params=pltpu.CompilerParams(vmem_limit_bytes=32 * 1024 * 1024),
    )(back, pred, own, first, last)


def exchanged(value):
    return lax.all_to_all(value, "tile", split_axis=0, concat_axis=0, tiled=True)


def local(
    coarse_solution,
    geometry,
    fine_fields,
    cotangent,
    sample_ids,
    first_weight,
    dilated_weight,
    project_weight,
    down_weight,
    up_weight,
):
    peers = lax.axis_size("tile")
    position = lax.axis_index("tile")
    slots, rows = fine_fields.shape[0], fine_fields.shape[4]
    up = [(i, i + 1) for i in range(peers - 1)]
    down = [(i + 1, i) for i in range(peers - 1)]

    made = constants(rows)
    fine = fine_fields.reshape(slots, 12 * rows, HALF)
    cot = cotangent.reshape(slots, 12 * rows, HALF)

    sent, edge_last, edge_first = run_early(
        peers,
        coarse_solution,
        geometry,
        fine,
        cot,
        jnp.asarray(made["early_x"], BF),
        jnp.asarray(made["early_s"], BF),
    )
    coarse = exchanged(sent)
    from_before = lax.ppermute(edge_last, "tile", up)
    from_after = lax.ppermute(edge_first, "tile", down)
    sums = coarse[:, SENT_INPUT:].astype(F32)
    sums = sums[:, :16] + sums[:, 16:]
    order = lax.broadcasted_iota(jnp.int32, (peers, peers), 0)
    other = lax.broadcasted_iota(jnp.int32, (peers, peers), 1)
    behind = jnp.sum(jnp.where((other > order)[:, :, None, None], sums[None], 0.0), axis=1)
    later = exchanged(behind)

    fixed = [
        jnp.asarray(made["sel_x"], BF),
        jnp.asarray(made["sel_s"], BF),
        jnp.asarray(made["sel_o"], BF),
        jnp.asarray(made["ex"], BF),
        jnp.asarray(made["eu"], BF),
        jnp.asarray(made["ext"], BF),
        jnp.asarray(made["eut"], BF),
        jnp.asarray(made["ef"], BF),
        jnp.asarray(made["eft"], BF),
        jnp.asarray(made["pool_both"], BF),
    ]
    second = dilated_weight
    up_flat = up_weight.reshape(96, 128)
    weights = [
        jnp.pad(first_weight.reshape(27, 128), ((0, 5), (0, 0))).T,
        jnp.transpose(second, (1, 3, 0, 2)).reshape(384, 384),
        jnp.transpose(second, (0, 2, 1, 3)).reshape(384, 384),
        project_weight,
        project_weight.T,
        down_weight.reshape(48, 128).T,
        up_flat.T,
        up_flat,
    ]
    pred_local, last_edge, first_edge, own, sent = run_slots(
        peers,
        sample_ids,
        position.reshape(1).astype(jnp.int32),
        coarse,
        fine,
        cot,
        from_before,
        from_after,
        later,
        fixed,
        weights,
    )

    chunk = GRAD_ROWS // peers
    got = exchanged(sent).astype(F32)
    to_first = lax.ppermute(first_edge, "tile", up)
    to_last = lax.ppermute(last_edge, "tile", down)
    reduced = jnp.sum(got[:, :chunk], axis=0).astype(BF)
    sums = got[:, chunk:]
    ahead = jnp.sum(jnp.where((other < order)[:, :, None, None], sums[None], 0.0), axis=1)
    reduced, to_first, to_last = lax.optimization_barrier((reduced, to_first, to_last))
    back = exchanged(
        jnp.concatenate(
            [
                jnp.broadcast_to(reduced, (peers, chunk, 128)),
                ahead.astype(BF),
            ],
            axis=1,
        )
    )
    prediction, dilated, project, up_grad, down_grad, first = run_final(
        back, pred_local, own, to_first, to_last
    )
    return (
        prediction.reshape(fine_fields.shape),
        first[0:27].reshape(first_weight.shape),
        dilated.reshape(dilated_weight.shape),
        project,
        down_grad.reshape(down_weight.shape),
        up_grad.reshape(up_weight.shape),
    )


def solution(mesh):
    in_specs = (
        P(("groups", "tile"), None, None),
        P(("groups", "tile"), None),
        P("groups", None, None, None, "tile", None),
        P("groups", None, None, None, "tile", None),
        P("groups"),
        P(),
        P(),
        P(),
        P(),
        P(),
    )
    out_specs = (
        P("groups", None, None, None, "tile", None),
        P("groups", None, None, None),
        P("groups", None, None, None),
        P("groups", None),
        P("groups", None, None, None),
        P("groups", None, None, None),
    )
    return jax.shard_map(local, mesh=mesh, in_specs=in_specs, out_specs=out_specs, check_vma=False)
```

```python
import math

import jax
import jax.numpy as jnp
import numpy as np
from jax import lax
from jax.experimental import pallas as pl
from jax.experimental.pallas import tpu as pltpu
from jax.sharding import PartitionSpec as P

CG = 64
FG = 512
HALF = FG // 2
SCALE = 1.0 / math.sqrt(FG)
GELU_A = math.sqrt(2.0 / math.pi)
GELU_B = GELU_A * 0.044715
BF = jnp.bfloat16
F32 = jnp.float32

AUX = 64
SENT_INPUT = 32
SENT_EARLY = SENT_INPUT + 32
PER_STEP = 4
GRAD_ROWS = 1536
UP_AT, DOWN_AT, FIRST_AT, PROJECT_AT = 1280, 1376, 1424, 1152


def nn(a, b):
    return lax.dot_general(a, b, (((1,), (0,)), ((), ())), preferred_element_type=F32)


def nt(a, b):
    return lax.dot_general(a, b, (((1,), (1,)), ((), ())), preferred_element_type=F32)


def halves(value):
    high = value.astype(BF)
    return high, (value - high.astype(F32)).astype(BF)


def row_at(tap, r):
    if tap == 0:
        return 8 if r == 0 else 4 + r - 1
    if tap == 1:
        return r
    if tap == 2:
        return 4 + r
    return 9 if r == 3 else r + 1


def fine_row(block, index):
    if index == 8:
        return 8 * block - 1
    if index == 9:
        return 8 * block + 8
    return 8 * block + 2 * (index % 4) + index // 4


COL_GROUP = (2, 0, 1, 3)


def constants(rows):
    blocks = rows // 4
    last = 2 * rows
    width = 12 * rows + AUX

    def held(ch, q, o):
        return ((ch * 2 + o % 2) * 2 + q) * rows + o // 2

    sel_x = np.zeros((blocks, 2, 32, width), np.float32)
    sel_s = np.zeros((blocks, 2, 64, width), np.float32)
    sel_o = np.zeros((12 * rows + 32, blocks, 2, 64), np.float32)
    base = 12 * rows
    for b in range(blocks):
        for q in range(2):
            for ch in range(3):
                for index in range(10):
                    o = fine_row(b, index)
                    at = ch * 10 + index
                    if o == -1:
                        sel_x[b, q, at, base + ch * 2 + q] = 1
                        sel_s[b, q, at, base + 6 + ch * 2 + q] = 1
                        sel_s[b, q, 32 + at, base + 6 + ch * 2 + q] = 1
                    elif o == last:
                        sel_x[b, q, at, base + 16 + ch * 2 + q] = 1
                        sel_s[b, q, at, base + 22 + ch * 2 + q] = 1
                    else:
                        sel_x[b, q, at, held(ch, q, o)] = 1
                        sel_s[b, q, at, held(ch, q, o)] = 1
                    for later in range(max(o, 0), last):
                        sel_s[b, q, 32 + at, held(ch, q, later)] = 1
                    sel_s[b, q, 32 + at, base + 32 + ch * 2 + q] = 1
                    sel_s[b, q, 32 + at, base + 40 + ch * 2 + q] = 1
                    for target in range(max(o, 0), last):
                        if target == o:
                            sel_o[held(ch, q, target), b, q, at] = 1
                        if o >= 0:
                            sel_o[held(ch, q, target), b, q, 32 + at] = 1
                    if o == -1:
                        sel_o[base + ch * 2 + q, b, q, at] = 1
                        sel_o[base + 8 + ch * 2 + q, b, q, 32 + at] = 1
                    else:
                        sel_o[base + 24 + ch * 2 + q, b, q, 32 + at] = 1
                    if o == last:
                        sel_o[base + 16 + ch * 2 + q, b, q, at] = 1
    early_x = np.zeros((48, 12 * rows), np.float32)
    early_s = np.zeros((48, 12 * rows), np.float32)
    for ch in range(3):
        for q in range(2):
            at = ch * 2 + q
            for o in range(last):
                early_s[at, held(ch, q, o)] = 1
            for start, o in ((16, last - 1), (32, 0)):
                early_x[start + at, held(ch, q, o)] = 1
                early_s[start + 6 + at, held(ch, q, o)] = 1
    ex = np.zeros((4, 128, 48), np.float32)
    eu = np.zeros((4, 256, 96), np.float32)
    for r in range(4):
        for i in range(4):
            for j in range(4):
                for ch in range(3):
                    ex[r, COL_GROUP[j] * 32 + ch * 10 + row_at(i, r), (ch * 4 + i) * 4 + j] = 1
                for k in range(6):
                    at = COL_GROUP[j] * 64 + (k // 3) * 32 + (k % 3) * 10 + row_at(i, r)
                    eu[r, at, (i * 4 + j) * 6 + k] = 1
    ef = np.zeros((80, 32), np.float32)
    for ch in range(3):
        for tap in range(9):
            ef[tap * 8 + ch, ch * 9 + tap] = 1
    ef_all = np.zeros((3, 256, 32), np.float32)
    for window in range(3):
        ef_all[window, window * 80 : (window + 1) * 80] = ef
    pool = np.zeros((CG, HALF), np.float32)
    for c in range(HALF):
        pool[c // 4, c] = 1
    none = np.zeros((CG, HALF), np.float32)
    return dict(
        sel_x=sel_x.reshape(blocks * 64, width),
        sel_s=sel_s.reshape(blocks * 128, width),
        early_x=early_x,
        early_s=early_s,
        sel_o=sel_o.reshape(12 * rows + 32, blocks * 128),
        ex=ex.reshape(512, 48),
        eu=eu.reshape(1024, 96),
        ext=np.concatenate(list(np.swapaxes(ex, 1, 2)), 1),
        eut=np.concatenate(list(np.swapaxes(eu, 1, 2)), 1),
        ef=ef_all.reshape(768, 32),
        eft=ef.T,
        pool_both=np.concatenate([pool, none, none, pool], 0),
    )


def gelu_both(pre):
    square = pre * pre
    t = jnp.tanh(pre * (GELU_B * square + GELU_A))
    gate = 0.5 + 0.5 * t
    value = pre * gate
    slope = gate + (value * (1.0 - gate)) * (6.0 * GELU_B * square + 2.0 * GELU_A)
    return value, slope


def moved(value, shift, lane, keep):
    width = value.shape[1]
    return jnp.where(keep(lane), pltpu.roll(value, shift % width, 1), 0.0)


def coarse_forward(blocks, tile, coarse_ref, w1_ref, second_t_ref, spread_ref, store, place):
    patches_s, columns_s, first_slope_s, second_slope_s, feature_s, wide_s = store
    cells = blocks * CG
    by_segment = coarse_ref[0, 0:SENT_INPUT, :].astype(F32)
    inputs = jnp.concatenate(
        [by_segment[at : at + 4] for at in range(0, SENT_INPUT, 4)], axis=1
    )
    inputs = jnp.concatenate([inputs, jnp.zeros_like(inputs)], axis=0)
    lane_in = lax.broadcasted_iota(jnp.int32, inputs.shape, 1) % CG
    by_col = (
        moved(inputs, 2, lane_in, lambda x: x >= 2),
        inputs,
        moved(inputs, -2, lane_in, lambda x: x < CG - 2),
    )
    above = jnp.where(tile * blocks >= 4, 1.0, 0.0)
    below = jnp.where(tile * blocks + 4 <= CG - blocks, 1.0, 0.0)
    windows = []
    for window in range(3):
        pieces = []
        for row_tap in range(3):
            for col_tap in range(3):
                start = (4 * window + 2 * row_tap) * CG
                pieces.append(by_col[col_tap][:, start : start + cells])
        pieces.append(jnp.zeros((8, cells), F32))
        piece = jnp.concatenate(pieces, axis=0)
        if window == 0:
            piece = piece * above
        if window == 2:
            piece = piece * below
        windows.append(piece.astype(BF))
    first_value, first_slope = gelu_both(
        nn(w1_ref[...], jnp.concatenate(windows + [jnp.zeros((16, cells), BF)], axis=0))
    )
    yield
    stacked = first_value.astype(BF)
    taps = nn(second_t_ref[...], stacked)
    lane_c = lax.broadcasted_iota(jnp.int32, (128, cells), 1) % CG
    second_pre = (
        taps[128:256]
        + moved(taps[0:128], 4, lane_c, lambda x: x >= 4)
        + moved(taps[256:384], -4, lane_c, lambda x: x < CG - 4)
    )
    second_value, second_slope = gelu_both(second_pre)
    yield
    feature = second_value.astype(BF)
    patches_s[place] = jnp.concatenate(windows, axis=1)
    columns_s[place] = stacked
    first_slope_s[place] = first_slope
    second_slope_s[place] = second_slope
    feature_s[place] = feature
    pairs = [feature[:, at * 128 : (at + 1) * 128] for at in range(blocks // 2)]
    pairs = jnp.concatenate(pairs, axis=0) if blocks > 2 else pairs[0]
    for parity in range(2):
        wide = nn(pairs, spread_ref[parity * 128 : (parity + 1) * 128, :]).astype(BF)
        for at in range(blocks // 2):
            b = 2 * at + parity
            wide_s[place, :, b * HALF : (b + 1) * HALF] = wide[at * 128 : (at + 1) * 128]


def coarse_backward(blocks, d_project, project_ref, second_ref, store, place, dil_ref, pg_ref, fg_ref):
    patches_s, columns_s, first_slope_s, second_slope_s, feature_s, _ = store
    cells = blocks * CG
    pg_ref[...] += nt(feature_s[place], d_project)
    d_feature = nn(project_ref[...], d_project).astype(BF).astype(F32)
    d_second = (d_feature * second_slope_s[place]).astype(BF).astype(F32)
    yield
    lane_c = lax.broadcasted_iota(jnp.int32, (128, cells), 1) % CG
    shifted = jnp.concatenate(
        [
            moved(d_second, -4, lane_c, lambda x: x < CG - 4),
            d_second,
            moved(d_second, 4, lane_c, lambda x: x >= 4),
        ],
        axis=0,
    ).astype(BF)
    dil_ref[...] += nt(columns_s[place], shifted)
    back = nn(second_ref[...], shifted)
    yield
    d_first = (back * first_slope_s[place]).astype(BF)
    d_first = jnp.concatenate([d_first[0:128], d_first[128:256], d_first[256:384]], axis=1)
    fg_ref[...] += nt(patches_s[place], d_first)


def advance(stage):
    next(stage, None)


def finish(stage):
    for _ in stage:
        pass


def slot_kernel(
    blocks,
    peers,
    ids_ref,
    tile_ref,
    coarse_first_ref,
    coarse_refs,
    fine_ref,
    cot_ref,
    before_ref,
    after_ref,
    later_ref,
    sel_x_ref,
    sel_s_ref,
    sel_o_ref,
    ex_ref,
    eu_ref,
    ext_ref,
    eut_ref,
    ef_ref,
    eft_ref,
    spread_ref,
    first_t_ref,
    second_t_ref,
    second_ref,
    project_ref,
    project_t_ref,
    down_t_ref,
    up_t_ref,
    up_ref,
    pred_ref,
    to_last_ref,
    to_first_ref,
    own_ref,
    sent_ref,
    dil_ref,
    pg_ref,
    w_ref,
    u_ref,
    ut_ref,
    w1_ref,
    gu_ref,
    gd_ref,
    fg_ref,
    d_project_ref,
    *store,
):
    step = pl.program_id(0)
    tile = tile_ref[0]
    chunk = GRAD_ROWS // peers

    def forward(source, place):
        return coarse_forward(
            blocks, tile, source, w1_ref, second_t_ref, spread_ref, store, place
        )

    def backward(place):
        return coarse_backward(
            blocks, d_project_ref[...], project_ref, second_ref, store, place, dil_ref, pg_ref, fg_ref
        )

    @pl.when(step == 0)
    def _():
        for r in range(4):
            rows = slice(r * 128, (r + 1) * 128)
            w_ref[rows, 0:128] = nt(down_t_ref[...], ex_ref[rows, :]).astype(BF)
            w_ref[rows, 128:256] = project_t_ref[...]
            taps = eu_ref[r * 256 : (r + 1) * 256, :]
            u_ref[rows, :] = nt(up_t_ref[...], taps).astype(BF)
            ut_ref[:, rows] = nn(taps, up_ref[...]).astype(BF)
        for window in range(3):
            w1_ref[window * 128 : (window + 1) * 128, :] = nt(
                first_t_ref[...], ef_ref[window * 256 : (window + 1) * 256, :]
            ).astype(BF)
        gu_ref[...] = jnp.zeros_like(gu_ref)
        gd_ref[...] = jnp.zeros_like(gd_ref)
        fg_ref[...] = jnp.zeros_like(fg_ref)
        dil_ref[...] = jnp.zeros_like(dil_ref)
        pg_ref[...] = jnp.zeros_like(pg_ref)
        d_project_ref[...] = jnp.zeros_like(d_project_ref)
        for buffer in store:
            buffer[2] = jnp.zeros(buffer.shape[1:], buffer.dtype)
        finish(forward(coarse_first_ref, 0))

    def one_slot(u, slot, now, soon, done):
        back = backward(done)
        ahead = forward(coarse_refs[u], soon)
        advance(back)
        later = jnp.concatenate([later_ref[u, 0:8, :], later_ref[u, 8:16, :]], axis=1)
        later_high = later.astype(BF).astype(F32)
        later_both = jnp.concatenate([later_high, later - later_high], axis=0).astype(BF)
        aux = [before_ref[u], after_ref[u], later_both, jnp.zeros((16, HALF), BF)]
        fine_all = nn(sel_x_ref[...], jnp.concatenate([fine_ref[u]] + aux, axis=0))
        slope_all = nn(sel_s_ref[...], jnp.concatenate([cot_ref[u]] + aux, axis=0))
        row = lax.broadcasted_iota(jnp.int32, (64, HALF), 0)
        flux_scale = jnp.where(row >= 32, SCALE, 1.0)
        outside = (row == 40) | (row == 50) | (row == 60)
        top_scale = jnp.where(outside & (tile == 0), 0.0, flux_scale)
        lane32 = lax.broadcasted_iota(jnp.int32, (32, HALF), 1)
        lane64 = lax.broadcasted_iota(jnp.int32, (64, HALF), 1)
        not_first = lambda x: x >= 1
        not_last = lambda x: x < HALF - 1

        def enter(b):
            x0 = fine_all[b * 64 : b * 64 + 32]
            x1 = fine_all[b * 64 + 32 : b * 64 + 64]
            x_taps = jnp.concatenate(
                [x0, x1, moved(x1, 1, lane32, not_first), moved(x0, -1, lane32, not_last)], axis=0
            ).astype(BF)
            scale = top_scale if b == 0 else flux_scale
            s0 = slope_all[b * 128 : b * 128 + 64] * scale
            s1 = slope_all[b * 128 + 64 : b * 128 + 128] * scale
            s_taps = jnp.concatenate(
                [s0, s1, moved(s1, 1, lane64, not_first), moved(s0, -1, lane64, not_last)], axis=0
            ).astype(BF)
            wide = store[5][now, :, b * HALF : (b + 1) * HALF]
            third = nn(w_ref[...], jnp.concatenate([x_taps, wide], axis=0))
            return [x_taps, s_taps, third]

        def middle(entered, part):
            rows = slice(part * 128, (part + 1) * 128)
            value, slope = gelu_both(entered[2][rows])
            return value.astype(BF), (entered[3][rows] * slope).astype(BF)

        def leave(b, held):
            hidden = held[2]
            taps = nn(ut_ref[...], hidden)
            c0 = taps[0:64] + moved(taps[192:256], 1, lane64, not_first)
            c1 = taps[64:128] + moved(taps[128:192], -1, lane64, not_last)
            return [c0 * flux_scale, c1 * flux_scale]

        def collect(even, odd):
            s_taps = jnp.concatenate([even[1], odd[1]], axis=1)
            hidden = jnp.concatenate([even[2], odd[2]], axis=1)
            gu_ref[...] += nt(hidden, s_taps)
            x_taps = jnp.concatenate(
                [
                    jnp.concatenate([even[0], odd[0]], axis=1),
                    jnp.concatenate([spread_ref[0:128, :], spread_ref[128:256, :]], axis=1),
                ],
                axis=0,
            )
            both = nt(jnp.concatenate([even[3], odd[3]], axis=1), x_taps)
            gd_ref[...] += both[:, 0:128]
            per_row = both[:, 128:256]
            return (per_row[0:128] + per_row[128:256]) + (per_row[256:384] + per_row[384:512])

        combined = []
        pooled = []
        entered = {}
        held = {}
        for turn in range(blocks + 2):
            working = 0 <= turn - 1 < blocks
            parts = []

            def work():
                if working:
                    parts.append(middle(entered[turn - 1], len(parts)))

            if turn < blocks:
                entered[turn] = enter(turn)
            work()
            if turn < blocks:
                entered[turn].append(nn(u_ref[...], entered[turn][1]))
            work()
            b = turn - 2
            if b >= 0:
                combined += leave(b, held[b])
            work()
            if b >= 0 and b % 2 == 1:
                pooled.append(collect(held[b - 1], held[b]))
            if turn == 1:
                advance(back)
            if turn == 2:
                finish(back)
            if turn >= 3:
                advance(ahead)
            work()
            if working:
                held[turn - 1] = entered[turn - 1][:2] + [
                    jnp.concatenate([part[at] for part in parts], axis=0) for at in range(2)
                ]

        out = jnp.concatenate(combined, axis=0)
        finish(ahead)
        placed = nn(sel_o_ref[...], out.astype(BF))
        main = pred_ref.shape[1]
        pred_ref[u] = placed[0:main]
        before_flux = placed[main + 8 : main + 16]
        own = before_flux * jnp.where(tile >= 1, 1.0, 0.0)
        flux = placed[main + 24 : main + 32] + own
        to_last_ref[u] = placed[main : main + 8] + before_flux
        to_first_ref[u] = placed[main + 16 : main + 24]
        own_ref[u] = own
        flux = jnp.concatenate([flux[:, 0:128], flux[:, 128:256]], axis=0)
        sent_ref[slot, chunk : chunk + 16, :] = flux.astype(BF)
        d_project_ref[...] = jnp.concatenate(pooled, axis=1).astype(BF)

    for u in range(PER_STEP):
        slot = step * PER_STEP + u
        now = lax.rem(slot, 3)
        one_slot(u, slot, now, lax.rem(slot + 1, 3), lax.rem(slot + 2, 3))

    @pl.when(step == pl.num_programs(0) - 1)
    def _():
        finish(backward((pl.num_programs(0) * PER_STEP - 1) % 3))
        rows = [slice(r * 128, (r + 1) * 128) for r in range(4)]
        taps = halves(jnp.concatenate([gu_ref[at, :] for at in rows], axis=1))
        up = nt(eut_ref[...], taps[0]) + nt(eut_ref[...], taps[1])
        taps = halves(jnp.concatenate([gd_ref[at, :] for at in rows], axis=1))
        down = nt(ext_ref[...], taps[0]) + nt(ext_ref[...], taps[1])
        taps = halves(fg_ref[...])
        first = nn(eft_ref[...], taps[0]) + nn(eft_ref[...], taps[1])
        pieces = [
            dil_ref[i * 128 : (i + 1) * 128, j * 128 : (j + 1) * 128]
            for i in range(3)
            for j in range(3)
        ]
        pieces += [pg_ref[...], up, down, first]
        pieces.append(jnp.zeros((GRAD_ROWS - FIRST_AT - 32, 128), F32))
        grads = jnp.concatenate(pieces, axis=0).astype(BF)
        for t in range(peers):
            sent_ref[t, 0:chunk, :] = grads[t * chunk : (t + 1) * chunk, :]


def run_slots(peers, ids, tile, coarse, fine, cot, before, after, later, fixed, weights):
    slots, main, width = fine.shape
    blocks = main // 48
    cells = blocks * CG
    chunk = GRAD_ROWS // peers

    def coarse_of(ahead):
        return pl.BlockSpec(
            one, lambda n, ids, tile: (ids[jnp.minimum(n * PER_STEP + ahead, slots - 1)], 0, 0)
        )

    def whole(array):
        return pl.BlockSpec(array.shape, lambda n, ids, tile: (0,) * array.ndim)

    def per_slot(array):
        return pl.BlockSpec((PER_STEP,) + array.shape[1:], lambda n, ids, tile: (n, 0, 0))

    one = (1,) + coarse.shape[1:]
    in_specs = [
        pl.BlockSpec(one, lambda n, ids, tile: (ids[0], 0, 0)),
        *[coarse_of(ahead + 1) for ahead in range(PER_STEP)],
        per_slot(fine),
        per_slot(cot),
        per_slot(before),
        per_slot(after),
        per_slot(later),
    ] + [whole(a) for a in fixed + weights]
    edge = jax.ShapeDtypeStruct((slots, 8, width), F32)
    out_shape = [
        jax.ShapeDtypeStruct((slots, main, width), F32),
        edge,
        edge,
        edge,
        jax.ShapeDtypeStruct((peers, chunk + 16, 128), BF),
    ]
    grid_spec = pltpu.PrefetchScalarGridSpec(
        num_scalar_prefetch=2,
        grid=(slots // PER_STEP,),
        in_specs=in_specs,
        out_specs=[per_slot(a) for a in out_shape[:4]] + [whole(out_shape[4])],
        scratch_shapes=[
            pltpu.VMEM((384, 384), F32),
            pltpu.VMEM((128, 128), F32),
            pltpu.VMEM((512, 256), BF),
            pltpu.VMEM((512, 256), BF),
            pltpu.VMEM((256, 512), BF),
            pltpu.VMEM((384, 256), BF),
            pltpu.VMEM((512, 256), F32),
            pltpu.VMEM((512, 128), F32),
            pltpu.VMEM((80, 128), F32),
            pltpu.VMEM((128, cells), BF),
            pltpu.VMEM((3, 80, 3 * cells), BF),
            pltpu.VMEM((3, 384, cells), BF),
            pltpu.VMEM((3, 384, cells), F32),
            pltpu.VMEM((3, 128, cells), F32),
            pltpu.VMEM((3, 128, cells), BF),
            pltpu.VMEM((3, 128, blocks * HALF), BF),
        ],
    )

    def body(*refs):
        slot_kernel(blocks, peers, *refs[:3], refs[3 : 3 + PER_STEP], *refs[3 + PER_STEP :])

    return pl.pallas_call(
        body,
        grid_spec=grid_spec,
        out_shape=out_shape,
        compiler_params=pltpu.CompilerParams(vmem_limit_bytes=52 * 1024 * 1024),
        cost_estimate=pl.CostEstimate(
            flops=slots * blocks * 500_000_000, bytes_accessed=16_000_000, transcendentals=0
        ),
    )(ids, tile, *[coarse] * (PER_STEP + 1), fine, cot, before, after, later, *fixed, *weights)


EARLY_SLOTS = 4


def early_kernel(
    blocks, peers, solution_ref, geometry_ref, fine_ref, cot_ref, x_ref, s_ref, sent_ref, last_ref, first_ref
):
    step = pl.program_id(0)

    @pl.when(step == 0)
    def _():
        inputs = jnp.concatenate(
            [
                solution_ref[0].astype(F32),
                geometry_ref[...].astype(F32),
                jnp.zeros((5, CG * CG), F32),
            ],
            axis=0,
        )
        edge = jnp.zeros((8, 6 * CG), F32)
        inputs = jnp.concatenate([edge, inputs, edge, jnp.zeros((8, 2 * CG), F32)], axis=1)
        for t in range(peers):
            at = t * blocks * CG
            sent_ref[t, 0:SENT_INPUT, :] = jnp.concatenate(
                [
                    inputs[0:4, at + segment * 128 : at + segment * 128 + 128]
                    for segment in range(SENT_INPUT // 4)
                ],
                axis=0,
            ).astype(BF)

    for u in range(EARLY_SLOTS):
        slot = step * EARLY_SLOTS + u
        picked = nn(x_ref[...], fine_ref[u]) + nn(s_ref[...], cot_ref[u])
        totals = jnp.concatenate(
            [picked[0:8, 0:128], picked[0:8, 128:256]], axis=0
        )
        high = totals.astype(BF)
        sent_ref[slot, SENT_INPUT : SENT_INPUT + 16, :] = high
        sent_ref[slot, SENT_INPUT + 16 : SENT_INPUT + 32, :] = (
            totals - high.astype(F32)
        ).astype(BF)
        last_ref[u] = picked[16:32].astype(BF)
        first_ref[u] = picked[32:48].astype(BF)


def run_early(peers, solution, geometry, fine, cot, pick_x, pick_s):
    slots, main, width = fine.shape

    def whole(array):
        return pl.BlockSpec(array.shape, lambda n: (0,) * array.ndim)

    def per_slots(array):
        return pl.BlockSpec((EARLY_SLOTS,) + array.shape[1:], lambda n: (n, 0, 0))

    edge = jax.ShapeDtypeStruct((slots, 16, width), BF)
    sent = jax.ShapeDtypeStruct((peers, SENT_EARLY, 128), BF)

    def body(*refs):
        early_kernel(main // 48, peers, *refs)

    return pl.pallas_call(
        body,
        grid=(slots // EARLY_SLOTS,),
        in_specs=[whole(solution), whole(geometry), per_slots(fine), per_slots(cot)]
        + [whole(pick_x), whole(pick_s)],
        out_specs=[whole(sent), per_slots(edge), per_slots(edge)],
        out_shape=[sent, edge, edge],
        compiler_params=pltpu.CompilerParams(vmem_limit_bytes=60 * 1024 * 1024),
    )(solution, geometry, fine, cot, pick_x, pick_s)


FINAL_SLOTS = 4
PARTS = ((0, 1152), (PROJECT_AT, 128), (UP_AT, 96), (DOWN_AT, 48), (FIRST_AT, 32))
SHAPES = ((1152, 128), (128, 128), (4, 4, 6, 128), (3, 4, 4, 128), (3, 3, 3, 128))


def final_kernel(chunk, rows, back_ref, pred_ref, own_ref, first_ref, last_ref, out_ref, *grads):
    step = pl.program_id(0)

    @pl.when(step == 0)
    def _():
        for (start, size), grad in zip(PARTS, grads):
            pieces = []
            at = start
            while at < start + size:
                t = at // chunk
                stop = min((t + 1) * chunk, start + size)
                pieces.append(back_ref[t, at - t * chunk : stop - t * chunk, :].astype(F32))
                at = stop
            whole = jnp.concatenate(pieces, axis=0) if len(pieces) > 1 else pieces[0]
            if len(grad.shape) == 2:
                grad[...] = whole
            else:
                group = grad.shape[2]
                for i in range(grad.shape[0]):
                    for j in range(grad.shape[1]):
                        at = (i * grad.shape[1] + j) * group
                        grad[i, j] = whole[at : at + group]

    row = lax.broadcasted_iota(jnp.int32, (rows, HALF), 0)
    for s in range(out_ref.shape[0]):
        slot = step * out_ref.shape[0] + s
        ahead = back_ref[slot, chunk : chunk + 16, :].astype(F32)
        base = jnp.concatenate([ahead[0:8], ahead[8:16]], axis=1) + own_ref[s]
        for k in range(3):
            for p in range(2):
                for q in range(2):
                    at = ((k * 2 + p) * 2 + q) * rows
                    pick = slice(k * 2 + q, k * 2 + q + 1)
                    edge = (first_ref if p == 0 else last_ref)[s, pick, :]
                    reached = row == (0 if p == 0 else rows - 1)
                    out_ref[s, at : at + rows, :] = (
                        pred_ref[s, at : at + rows, :]
                        + base[pick]
                        + jnp.where(reached, edge, 0.0)
                    ).astype(BF)


def run_final(back, pred, own, first, last):
    slots, main, width = pred.shape
    chunk = back.shape[1] - 16
    held = FINAL_SLOTS if main % 192 == 0 else 2 * FINAL_SLOTS

    def per_slots(array):
        return pl.BlockSpec((held,) + array.shape[1:], lambda n: (n, 0, 0))

    def body(*refs):
        final_kernel(chunk, main // 12, *refs)

    return pl.pallas_call(
        body,
        grid=(slots // held,),
        in_specs=[pl.BlockSpec(back.shape, lambda n: (0, 0, 0))]
        + [per_slots(a) for a in (pred, own, first, last)],
        out_specs=[per_slots(pred)]
        + [pl.BlockSpec(shape, lambda n, dims=len(shape): (0,) * dims) for shape in SHAPES],
        out_shape=[jax.ShapeDtypeStruct(pred.shape, BF)]
        + [jax.ShapeDtypeStruct(shape, F32) for shape in SHAPES],
        compiler_params=pltpu.CompilerParams(vmem_limit_bytes=32 * 1024 * 1024),
    )(back, pred, own, first, last)


def exchanged(value):
    return lax.all_to_all(value, "tile", split_axis=0, concat_axis=0, tiled=True)


def local(
    coarse_solution,
    geometry,
    fine_fields,
    cotangent,
    sample_ids,
    first_weight,
    dilated_weight,
    project_weight,
    down_weight,
    up_weight,
):
    peers = lax.axis_size("tile")
    position = lax.axis_index("tile")
    slots, rows = fine_fields.shape[0], fine_fields.shape[4]
    up = [(i, i + 1) for i in range(peers - 1)]
    down = [(i + 1, i) for i in range(peers - 1)]

    made = constants(rows)
    fine = fine_fields.reshape(slots, 12 * rows, HALF)
    cot = cotangent.reshape(slots, 12 * rows, HALF)

    sent, edge_last, edge_first = run_early(
        peers,
        coarse_solution,
        geometry,
        fine,
        cot,
        jnp.asarray(made["early_x"], BF),
        jnp.asarray(made["early_s"], BF),
    )
    coarse = exchanged(sent)
    from_before = lax.ppermute(edge_last, "tile", up)
    from_after = lax.ppermute(edge_first, "tile", down)
    sums = coarse[:, SENT_INPUT:].astype(F32)
    sums = sums[:, :16] + sums[:, 16:]
    order = lax.broadcasted_iota(jnp.int32, (peers, peers), 0)
    other = lax.broadcasted_iota(jnp.int32, (peers, peers), 1)
    behind = jnp.sum(jnp.where((other > order)[:, :, None, None], sums[None], 0.0), axis=1)
    later = exchanged(behind)

    fixed = [
        jnp.asarray(made["sel_x"], BF),
        jnp.asarray(made["sel_s"], BF),
        jnp.asarray(made["sel_o"], BF),
        jnp.asarray(made["ex"], BF),
        jnp.asarray(made["eu"], BF),
        jnp.asarray(made["ext"], BF),
        jnp.asarray(made["eut"], BF),
        jnp.asarray(made["ef"], BF),
        jnp.asarray(made["eft"], BF),
        jnp.asarray(made["pool_both"], BF),
    ]
    second = dilated_weight
    up_flat = up_weight.reshape(96, 128)
    weights = [
        jnp.pad(first_weight.reshape(27, 128), ((0, 5), (0, 0))).T,
        jnp.transpose(second, (1, 3, 0, 2)).reshape(384, 384),
        jnp.transpose(second, (0, 2, 1, 3)).reshape(384, 384),
        project_weight,
        project_weight.T,
        down_weight.reshape(48, 128).T,
        up_flat.T,
        up_flat,
    ]
    pred_local, last_edge, first_edge, own, sent = run_slots(
        peers,
        sample_ids,
        position.reshape(1).astype(jnp.int32),
        coarse,
        fine,
        cot,
        from_before,
        from_after,
        later,
        fixed,
        weights,
    )

    chunk = GRAD_ROWS // peers
    got = exchanged(sent).astype(F32)
    to_first = lax.ppermute(first_edge, "tile", up)
    to_last = lax.ppermute(last_edge, "tile", down)
    reduced = jnp.sum(got[:, :chunk], axis=0).astype(BF)
    sums = got[:, chunk:]
    ahead = jnp.sum(jnp.where((other < order)[:, :, None, None], sums[None], 0.0), axis=1)
    reduced, to_first, to_last = lax.optimization_barrier((reduced, to_first, to_last))
    back = exchanged(
        jnp.concatenate(
            [
                jnp.broadcast_to(reduced, (peers, chunk, 128)),
                ahead.astype(BF),
            ],
            axis=1,
        )
    )
    prediction, dilated, project, up_grad, down_grad, first = run_final(
        back, pred_local, own, to_first, to_last
    )
    return (
        prediction.reshape(fine_fields.shape),
        first,
        dilated.reshape(dilated_weight.shape),
        project,
        down_grad,
        up_grad,
    )


def solution(mesh):
    in_specs = (
        P(("groups", "tile"), None, None),
        P(("groups", "tile"), None),
        P("groups", None, None, None, "tile", None),
        P("groups", None, None, None, "tile", None),
        P("groups"),
        P(),
        P(),
        P(),
        P(),
        P(),
    )
    out_specs = (
        P("groups", None, None, None, "tile", None),
        P("groups", None, None, None),
        P("groups", None, None, None),
        P("groups", None),
        P("groups", None, None, None),
        P("groups", None, None, None),
    )
    return jax.shard_map(local, mesh=mesh, in_specs=in_specs, out_specs=out_specs, check_vma=False)
```

```python
import math

import jax
import jax.numpy as jnp
import numpy as np
from jax import lax
from jax.experimental import pallas as pl
from jax.experimental.pallas import tpu as pltpu
from jax.sharding import PartitionSpec as P

CG = 64
FG = 512
HALF = FG // 2
SCALE = 1.0 / math.sqrt(FG)
GELU_A = math.sqrt(2.0 / math.pi)
GELU_B = GELU_A * 0.044715
BF = jnp.bfloat16
F32 = jnp.float32

AUX = 64
SENT_INPUT = 32
SENT_EARLY = SENT_INPUT + 32
PER_STEP = 4
GRAD_ROWS = 1536
UP_AT, DOWN_AT, FIRST_AT, PROJECT_AT = 1280, 1376, 1424, 1152


def nn(a, b):
    return lax.dot_general(a, b, (((1,), (0,)), ((), ())), preferred_element_type=F32)


def nt(a, b):
    return lax.dot_general(a, b, (((1,), (1,)), ((), ())), preferred_element_type=F32)


def halves(value):
    high = value.astype(BF)
    return high, (value - high.astype(F32)).astype(BF)


def row_at(tap, r):
    if tap == 0:
        return 8 if r == 0 else 4 + r - 1
    if tap == 1:
        return r
    if tap == 2:
        return 4 + r
    return 9 if r == 3 else r + 1


def fine_row(block, index):
    if index == 8:
        return 8 * block - 1
    if index == 9:
        return 8 * block + 8
    return 8 * block + 2 * (index % 4) + index // 4


COL_GROUP = (2, 0, 1, 3)


def constants(rows):
    blocks = rows // 4
    last = 2 * rows
    width = 12 * rows + AUX

    def held(ch, q, o):
        return ((ch * 2 + o % 2) * 2 + q) * rows + o // 2

    sel_x = np.zeros((blocks, 2, 32, width), np.float32)
    sel_s = np.zeros((blocks, 2, 64, width), np.float32)
    sel_o = np.zeros((12 * rows + 32, blocks, 2, 64), np.float32)
    base = 12 * rows
    for b in range(blocks):
        for q in range(2):
            for ch in range(3):
                for index in range(10):
                    o = fine_row(b, index)
                    at = ch * 10 + index
                    if o == -1:
                        sel_x[b, q, at, base + ch * 2 + q] = 1
                        sel_s[b, q, at, base + 6 + ch * 2 + q] = 1
                        sel_s[b, q, 32 + at, base + 6 + ch * 2 + q] = 1
                    elif o == last:
                        sel_x[b, q, at, base + 16 + ch * 2 + q] = 1
                        sel_s[b, q, at, base + 22 + ch * 2 + q] = 1
                    else:
                        sel_x[b, q, at, held(ch, q, o)] = 1
                        sel_s[b, q, at, held(ch, q, o)] = 1
                    for later in range(max(o, 0), last):
                        sel_s[b, q, 32 + at, held(ch, q, later)] = 1
                    sel_s[b, q, 32 + at, base + 32 + ch * 2 + q] = 1
                    sel_s[b, q, 32 + at, base + 40 + ch * 2 + q] = 1
                    for target in range(max(o, 0), last):
                        if target == o:
                            sel_o[held(ch, q, target), b, q, at] = 1
                        if o >= 0:
                            sel_o[held(ch, q, target), b, q, 32 + at] = 1
                    if o == -1:
                        sel_o[base + ch * 2 + q, b, q, at] = 1
                        sel_o[base + 8 + ch * 2 + q, b, q, 32 + at] = 1
                    else:
                        sel_o[base + 24 + ch * 2 + q, b, q, 32 + at] = 1
                    if o == last:
                        sel_o[base + 16 + ch * 2 + q, b, q, at] = 1
    early_x = np.zeros((48, 12 * rows), np.float32)
    early_s = np.zeros((48, 12 * rows), np.float32)
    for ch in range(3):
        for q in range(2):
            at = ch * 2 + q
            for o in range(last):
                early_s[at, held(ch, q, o)] = 1
            for start, o in ((16, last - 1), (32, 0)):
                early_x[start + at, held(ch, q, o)] = 1
                early_s[start + 6 + at, held(ch, q, o)] = 1
    ex = np.zeros((4, 128, 48), np.float32)
    eu = np.zeros((4, 256, 96), np.float32)
    for r in range(4):
        for i in range(4):
            for j in range(4):
                for ch in range(3):
                    ex[r, COL_GROUP[j] * 32 + ch * 10 + row_at(i, r), (ch * 4 + i) * 4 + j] = 1
                for k in range(6):
                    at = COL_GROUP[j] * 64 + (k // 3) * 32 + (k % 3) * 10 + row_at(i, r)
                    eu[r, at, (i * 4 + j) * 6 + k] = 1
    ef = np.zeros((80, 32), np.float32)
    for ch in range(3):
        for tap in range(9):
            ef[tap * 8 + ch, ch * 9 + tap] = 1
    ef_all = np.zeros((3, 256, 32), np.float32)
    for window in range(3):
        ef_all[window, window * 80 : (window + 1) * 80] = ef
    pool = np.zeros((CG, HALF), np.float32)
    for c in range(HALF):
        pool[c // 4, c] = 1
    none = np.zeros((CG, HALF), np.float32)
    return dict(
        sel_x=sel_x.reshape(blocks * 64, width),
        sel_s=sel_s.reshape(blocks * 128, width),
        early_x=early_x,
        early_s=early_s,
        sel_o=sel_o.reshape(12 * rows + 32, blocks * 128),
        ex=ex.reshape(512, 48),
        eu=eu.reshape(1024, 96),
        ext=np.concatenate(list(np.swapaxes(ex, 1, 2)), 1),
        eut=np.concatenate(list(np.swapaxes(eu, 1, 2)), 1)
        .reshape(4, 4, 6, 1024)
        .swapaxes(1, 2)
        .reshape(96, 1024),
        ef=ef_all.reshape(768, 32),
        eft=ef.T,
        pool_both=np.concatenate([pool, none, none, pool, pool, pool], 0),
    )


def gelu_both(pre):
    square = pre * pre
    t = jnp.tanh(pre * (GELU_B * square + GELU_A))
    gate = 0.5 + 0.5 * t
    value = pre * gate
    slope = gate + (value * (1.0 - gate)) * (6.0 * GELU_B * square + 2.0 * GELU_A)
    return value, slope


def moved(value, shift, lane, keep):
    width = value.shape[1]
    return jnp.where(keep(lane), pltpu.roll(value, shift % width, 1), 0.0)


def coarse_forward(blocks, tile, coarse_ref, w1_ref, second_t_ref, project_t_ref, store, place):
    patches_s, columns_s, first_slope_s, second_slope_s, feature_s, wide_s = store
    cells = blocks * CG
    by_segment = coarse_ref[0, 0:SENT_INPUT, :].astype(F32)
    inputs = jnp.concatenate(
        [by_segment[at : at + 4] for at in range(0, SENT_INPUT, 4)], axis=1
    )
    inputs = jnp.concatenate([inputs, jnp.zeros_like(inputs)], axis=0)
    lane_in = lax.broadcasted_iota(jnp.int32, inputs.shape, 1) % CG
    by_col = (
        moved(inputs, 2, lane_in, lambda x: x >= 2),
        inputs,
        moved(inputs, -2, lane_in, lambda x: x < CG - 2),
    )
    above = jnp.where(tile * blocks >= 4, 1.0, 0.0)
    below = jnp.where(tile * blocks + 4 <= CG - blocks, 1.0, 0.0)
    windows = []
    for window in range(3):
        pieces = []
        for row_tap in range(3):
            for col_tap in range(3):
                start = (4 * window + 2 * row_tap) * CG
                pieces.append(by_col[col_tap][:, start : start + cells])
        pieces.append(jnp.zeros((8, cells), F32))
        piece = jnp.concatenate(pieces, axis=0)
        if window == 0:
            piece = piece * above
        if window == 2:
            piece = piece * below
        windows.append(piece.astype(BF))
    first_value, first_slope = gelu_both(
        nn(w1_ref[...], jnp.concatenate(windows + [jnp.zeros((16, cells), BF)], axis=0))
    )
    yield
    stacked = first_value.astype(BF)
    taps = nn(second_t_ref[...], stacked)
    lane_c = lax.broadcasted_iota(jnp.int32, (128, cells), 1) % CG
    second_pre = (
        taps[128:256]
        + moved(taps[0:128], 4, lane_c, lambda x: x >= 4)
        + moved(taps[256:384], -4, lane_c, lambda x: x < CG - 4)
    )
    second_value, second_slope = gelu_both(second_pre)
    yield
    feature = second_value.astype(BF)
    patches_s[place] = jnp.concatenate(windows, axis=1)
    columns_s[place] = stacked
    first_slope_s[place] = first_slope
    second_slope_s[place] = second_slope
    feature_s[place] = feature
    projected = nn(project_t_ref[...], feature)
    left = lax.broadcasted_iota(jnp.int32, (128, 128), 1) < CG
    for at in range(blocks // 2):
        pair = projected[:, at * 128 : (at + 1) * 128]
        high = pair.astype(BF).astype(F32)
        low = pair - high
        even = jnp.where(left, high, pltpu.roll(low, CG, 1))
        odd = jnp.where(left, pltpu.roll(high, CG, 1), low)
        wide_s[place, at * 256 : at * 256 + 128, :] = even.astype(BF)
        wide_s[place, at * 256 + 128 : at * 256 + 256, :] = odd.astype(BF)


def coarse_backward(blocks, d_project, project_ref, second_ref, store, place, dil_ref, pg_ref, fg_ref):
    patches_s, columns_s, first_slope_s, second_slope_s, feature_s, _ = store
    cells = blocks * CG
    pg_ref[...] += nt(feature_s[place], d_project)
    d_feature = nn(project_ref[...], d_project).astype(BF).astype(F32)
    d_second = (d_feature * second_slope_s[place]).astype(BF).astype(F32)
    yield
    lane_c = lax.broadcasted_iota(jnp.int32, (128, cells), 1) % CG
    shifted = jnp.concatenate(
        [
            moved(d_second, -4, lane_c, lambda x: x < CG - 4),
            d_second,
            moved(d_second, 4, lane_c, lambda x: x >= 4),
        ],
        axis=0,
    ).astype(BF)
    dil_ref[...] += nt(columns_s[place], shifted)
    back = nn(second_ref[...], shifted)
    yield
    d_first = (back * first_slope_s[place]).astype(BF)
    d_first = jnp.concatenate([d_first[0:128], d_first[128:256], d_first[256:384]], axis=1)
    fg_ref[...] += nt(patches_s[place], d_first)


def advance(stage):
    next(stage, None)


def finish(stage):
    for _ in stage:
        pass


def slot_kernel(
    blocks,
    peers,
    ids_ref,
    tile_ref,
    coarse_first_ref,
    coarse_refs,
    fine_ref,
    cot_ref,
    before_ref,
    after_ref,
    later_ref,
    sel_x_ref,
    sel_s_ref,
    sel_o_ref,
    ex_ref,
    eu_ref,
    ext_ref,
    eut_ref,
    ef_ref,
    eft_ref,
    spread_ref,
    first_t_ref,
    second_t_ref,
    second_ref,
    project_ref,
    project_t_ref,
    down_t_ref,
    up_t_ref,
    up_ref,
    pred_ref,
    to_last_ref,
    to_first_ref,
    own_ref,
    sent_ref,
    dil_ref,
    pg_ref,
    w_ref,
    u_ref,
    ut_ref,
    w1_ref,
    gu_ref,
    gd_ref,
    fg_ref,
    d_project_ref,
    *store,
):
    step = pl.program_id(0)
    tile = tile_ref[0]
    chunk = GRAD_ROWS // peers

    def forward(source, place):
        return coarse_forward(
            blocks, tile, source, w1_ref, second_t_ref, project_t_ref, store, place
        )

    def backward(place):
        return coarse_backward(
            blocks, d_project_ref[...], project_ref, second_ref, store, place, dil_ref, pg_ref, fg_ref
        )

    @pl.when(step == 0)
    def _():
        for r in range(4):
            rows = slice(r * 128, (r + 1) * 128)
            w_ref[rows, :] = nt(down_t_ref[...], ex_ref[rows, :]).astype(BF)
            taps = eu_ref[r * 256 : (r + 1) * 256, :]
            u_ref[rows, :] = nt(up_t_ref[...], taps).astype(BF)
            ut_ref[:, rows] = nn(taps, up_ref[...]).astype(BF)
        for window in range(3):
            w1_ref[window * 128 : (window + 1) * 128, :] = nt(
                first_t_ref[...], ef_ref[window * 256 : (window + 1) * 256, :]
            ).astype(BF)
        gu_ref[...] = jnp.zeros_like(gu_ref)
        gd_ref[...] = jnp.zeros_like(gd_ref)
        fg_ref[...] = jnp.zeros_like(fg_ref)
        dil_ref[...] = jnp.zeros_like(dil_ref)
        pg_ref[...] = jnp.zeros_like(pg_ref)
        d_project_ref[...] = jnp.zeros_like(d_project_ref)
        for buffer in store:
            buffer[2] = jnp.zeros(buffer.shape[1:], buffer.dtype)
        finish(forward(coarse_first_ref, 0))

    def one_slot(u, slot, now, soon, done):
        back = backward(done)
        ahead = forward(coarse_refs[u], soon)
        advance(back)
        later = jnp.concatenate([later_ref[u, 0:8, :], later_ref[u, 8:16, :]], axis=1)
        later_high = later.astype(BF).astype(F32)
        later_both = jnp.concatenate([later_high, later - later_high], axis=0).astype(BF)
        aux = [before_ref[u], after_ref[u], later_both, jnp.zeros((16, HALF), BF)]
        fine_all = nn(sel_x_ref[...], jnp.concatenate([fine_ref[u]] + aux, axis=0))
        slope_all = nn(sel_s_ref[...], jnp.concatenate([cot_ref[u]] + aux, axis=0))
        row = lax.broadcasted_iota(jnp.int32, (64, HALF), 0)
        flux_scale = jnp.where(row >= 32, SCALE, 1.0)
        outside = (row == 40) | (row == 50) | (row == 60)
        top_scale = jnp.where(outside & (tile == 0), 0.0, flux_scale)
        lane32 = lax.broadcasted_iota(jnp.int32, (32, HALF), 1)
        lane64 = lax.broadcasted_iota(jnp.int32, (64, HALF), 1)
        not_first = lambda x: x >= 1
        not_last = lambda x: x < HALF - 1

        def enter(b):
            x0 = fine_all[b * 64 : b * 64 + 32]
            x1 = fine_all[b * 64 + 32 : b * 64 + 64]
            x_taps = jnp.concatenate(
                [x0, x1, moved(x1, 1, lane32, not_first), moved(x0, -1, lane32, not_last)], axis=0
            ).astype(BF)
            scale = top_scale if b == 0 else flux_scale
            s0 = slope_all[b * 128 : b * 128 + 64] * scale
            s1 = slope_all[b * 128 + 64 : b * 128 + 128] * scale
            s_taps = jnp.concatenate(
                [s0, s1, moved(s1, 1, lane64, not_first), moved(s0, -1, lane64, not_last)], axis=0
            ).astype(BF)
            coarse_part = store[5][now, b * 128 : (b + 1) * 128, :]
            left = jnp.concatenate(
                [w_ref[...], jnp.concatenate([coarse_part] * 4, axis=0)], axis=1
            )
            third = nn(left, jnp.concatenate([x_taps, spread_ref[256:384, :]], axis=0))
            return [x_taps, s_taps, third]

        def middle(entered, part):
            rows = slice(part * 128, (part + 1) * 128)
            value, slope = gelu_both(entered[2][rows])
            return value.astype(BF), (entered[3][rows] * slope).astype(BF)

        def leave(b, held):
            hidden = held[2]
            taps = nn(ut_ref[...], hidden)
            c0 = taps[0:64] + moved(taps[192:256], 1, lane64, not_first)
            c1 = taps[64:128] + moved(taps[128:192], -1, lane64, not_last)
            return [c0 * flux_scale, c1 * flux_scale]

        def collect(even, odd):
            s_taps = jnp.concatenate([even[1], odd[1]], axis=1)
            hidden = jnp.concatenate([even[2], odd[2]], axis=1)
            gu_ref[...] += nt(hidden, s_taps)
            x_taps = jnp.concatenate(
                [
                    jnp.concatenate([even[0], odd[0]], axis=1),
                    jnp.concatenate([spread_ref[0:128, :], spread_ref[128:256, :]], axis=1),
                ],
                axis=0,
            )
            both = nt(jnp.concatenate([even[3], odd[3]], axis=1), x_taps)
            gd_ref[...] += both[:, 0:128]
            per_row = both[:, 128:256]
            return (per_row[0:128] + per_row[128:256]) + (per_row[256:384] + per_row[384:512])

        combined = []
        pooled = []
        entered = {}
        held = {}
        for turn in range(blocks + 2):
            working = 0 <= turn - 1 < blocks
            parts = []

            def work():
                if working:
                    parts.append(middle(entered[turn - 1], len(parts)))

            if turn < blocks:
                entered[turn] = enter(turn)
            work()
            if turn < blocks:
                entered[turn].append(nn(u_ref[...], entered[turn][1]))
            work()
            b = turn - 2
            if b >= 0:
                combined += leave(b, held[b])
            work()
            if b >= 0 and b % 2 == 1:
                pooled.append(collect(held[b - 1], held[b]))
            if turn == 1:
                advance(back)
            if turn == 2:
                finish(back)
            if turn >= 3:
                advance(ahead)
            work()
            if working:
                held[turn - 1] = entered[turn - 1][:2] + [
                    jnp.concatenate([part[at] for part in parts], axis=0) for at in range(2)
                ]

        out = jnp.concatenate(combined, axis=0)
        finish(ahead)
        placed = nn(sel_o_ref[...], out.astype(BF))
        main = pred_ref.shape[1]
        pred_ref[u] = placed[0:main]
        before_flux = placed[main + 8 : main + 16]
        own = before_flux * jnp.where(tile >= 1, 1.0, 0.0)
        flux = placed[main + 24 : main + 32] + own
        to_last_ref[u] = placed[main : main + 8] + before_flux
        to_first_ref[u] = placed[main + 16 : main + 24]
        own_ref[u] = own
        flux = jnp.concatenate([flux[:, 0:128], flux[:, 128:256]], axis=0)
        sent_ref[slot, chunk : chunk + 16, :] = flux.astype(BF)
        d_project_ref[...] = jnp.concatenate(pooled, axis=1).astype(BF)

    for u in range(PER_STEP):
        slot = step * PER_STEP + u
        now = lax.rem(slot, 3)
        one_slot(u, slot, now, lax.rem(slot + 1, 3), lax.rem(slot + 2, 3))

    @pl.when(step == pl.num_programs(0) - 1)
    def _():
        finish(backward((pl.num_programs(0) * PER_STEP - 1) % 3))
        rows = [slice(r * 128, (r + 1) * 128) for r in range(4)]
        taps = halves(jnp.concatenate([gu_ref[at, :] for at in rows], axis=1))
        up = nt(eut_ref[...], taps[0]) + nt(eut_ref[...], taps[1])
        taps = halves(jnp.concatenate([gd_ref[at, :] for at in rows], axis=1))
        down = nt(ext_ref[...], taps[0]) + nt(ext_ref[...], taps[1])
        taps = halves(fg_ref[...])
        first = nn(eft_ref[...], taps[0]) + nn(eft_ref[...], taps[1])
        pieces = [
            dil_ref[i * 128 : (i + 1) * 128, j * 128 : (j + 1) * 128]
            for i in range(3)
            for j in range(3)
        ]
        pieces += [pg_ref[...], up, down, first]
        pieces.append(jnp.zeros((GRAD_ROWS - FIRST_AT - 32, 128), F32))
        grads = jnp.concatenate(pieces, axis=0).astype(BF)
        for t in range(peers):
            sent_ref[t, 0:chunk, :] = grads[t * chunk : (t + 1) * chunk, :]


def run_slots(peers, ids, tile, coarse, fine, cot, before, after, later, fixed, weights):
    slots, main, width = fine.shape
    blocks = main // 48
    cells = blocks * CG
    chunk = GRAD_ROWS // peers

    def coarse_of(ahead):
        return pl.BlockSpec(
            one, lambda n, ids, tile: (ids[jnp.minimum(n * PER_STEP + ahead, slots - 1)], 0, 0)
        )

    def whole(array):
        return pl.BlockSpec(array.shape, lambda n, ids, tile: (0,) * array.ndim)

    def per_slot(array):
        return pl.BlockSpec((PER_STEP,) + array.shape[1:], lambda n, ids, tile: (n, 0, 0))

    one = (1,) + coarse.shape[1:]
    in_specs = [
        pl.BlockSpec(one, lambda n, ids, tile: (ids[0], 0, 0)),
        *[coarse_of(ahead + 1) for ahead in range(PER_STEP)],
        per_slot(fine),
        per_slot(cot),
        per_slot(before),
        per_slot(after),
        per_slot(later),
    ] + [whole(a) for a in fixed + weights]
    edge = jax.ShapeDtypeStruct((slots, 8, width), F32)
    out_shape = [
        jax.ShapeDtypeStruct((slots, main, width), F32),
        edge,
        edge,
        edge,
        jax.ShapeDtypeStruct((peers, chunk + 16, 128), BF),
    ]
    grid_spec = pltpu.PrefetchScalarGridSpec(
        num_scalar_prefetch=2,
        grid=(slots // PER_STEP,),
        in_specs=in_specs,
        out_specs=[per_slot(a) for a in out_shape[:4]] + [whole(out_shape[4])],
        scratch_shapes=[
            pltpu.VMEM((384, 384), F32),
            pltpu.VMEM((128, 128), F32),
            pltpu.VMEM((512, 128), BF),
            pltpu.VMEM((512, 256), BF),
            pltpu.VMEM((256, 512), BF),
            pltpu.VMEM((384, 256), BF),
            pltpu.VMEM((512, 256), F32),
            pltpu.VMEM((512, 128), F32),
            pltpu.VMEM((80, 128), F32),
            pltpu.VMEM((128, cells), BF),
            pltpu.VMEM((3, 80, 3 * cells), BF),
            pltpu.VMEM((3, 384, cells), BF),
            pltpu.VMEM((3, 384, cells), F32),
            pltpu.VMEM((3, 128, cells), F32),
            pltpu.VMEM((3, 128, cells), BF),
            pltpu.VMEM((3, blocks * 128, 128), BF),
        ],
    )

    def body(*refs):
        slot_kernel(blocks, peers, *refs[:3], refs[3 : 3 + PER_STEP], *refs[3 + PER_STEP :])

    return pl.pallas_call(
        body,
        grid_spec=grid_spec,
        out_shape=out_shape,
        compiler_params=pltpu.CompilerParams(vmem_limit_bytes=52 * 1024 * 1024),
        cost_estimate=pl.CostEstimate(
            flops=slots * blocks * 500_000_000, bytes_accessed=16_000_000, transcendentals=0
        ),
    )(ids, tile, *[coarse] * (PER_STEP + 1), fine, cot, before, after, later, *fixed, *weights)


EARLY_SLOTS = 4


def early_kernel(
    blocks, peers, solution_ref, geometry_ref, fine_ref, cot_ref, x_ref, s_ref, sent_ref, last_ref, first_ref
):
    step = pl.program_id(0)

    @pl.when(step == 0)
    def _():
        inputs = jnp.concatenate(
            [
                solution_ref[0].astype(F32),
                geometry_ref[...].astype(F32),
                jnp.zeros((5, CG * CG), F32),
            ],
            axis=0,
        )
        edge = jnp.zeros((8, 6 * CG), F32)
        inputs = jnp.concatenate([edge, inputs, edge, jnp.zeros((8, 2 * CG), F32)], axis=1)
        for t in range(peers):
            at = t * blocks * CG
            sent_ref[t, 0:SENT_INPUT, :] = jnp.concatenate(
                [
                    inputs[0:4, at + segment * 128 : at + segment * 128 + 128]
                    for segment in range(SENT_INPUT // 4)
                ],
                axis=0,
            ).astype(BF)

    for u in range(EARLY_SLOTS):
        slot = step * EARLY_SLOTS + u
        picked = nn(x_ref[...], fine_ref[u]) + nn(s_ref[...], cot_ref[u])
        totals = jnp.concatenate(
            [picked[0:8, 0:128], picked[0:8, 128:256]], axis=0
        )
        high = totals.astype(BF)
        sent_ref[slot, SENT_INPUT : SENT_INPUT + 16, :] = high
        sent_ref[slot, SENT_INPUT + 16 : SENT_INPUT + 32, :] = (
            totals - high.astype(F32)
        ).astype(BF)
        last_ref[u] = picked[16:32].astype(BF)
        first_ref[u] = picked[32:48].astype(BF)


def run_early(peers, solution, geometry, fine, cot, pick_x, pick_s):
    slots, main, width = fine.shape

    def whole(array):
        return pl.BlockSpec(array.shape, lambda n: (0,) * array.ndim)

    def per_slots(array):
        return pl.BlockSpec((EARLY_SLOTS,) + array.shape[1:], lambda n: (n, 0, 0))

    edge = jax.ShapeDtypeStruct((slots, 16, width), BF)
    sent = jax.ShapeDtypeStruct((peers, SENT_EARLY, 128), BF)

    def body(*refs):
        early_kernel(main // 48, peers, *refs)

    return pl.pallas_call(
        body,
        grid=(slots // EARLY_SLOTS,),
        in_specs=[whole(solution), whole(geometry), per_slots(fine), per_slots(cot)]
        + [whole(pick_x), whole(pick_s)],
        out_specs=[whole(sent), per_slots(edge), per_slots(edge)],
        out_shape=[sent, edge, edge],
        compiler_params=pltpu.CompilerParams(vmem_limit_bytes=60 * 1024 * 1024),
    )(solution, geometry, fine, cot, pick_x, pick_s)


FINAL_SLOTS = 4
PARTS = ((0, 1152), (PROJECT_AT, 128), (UP_AT, 96), (DOWN_AT, 48), (FIRST_AT, 32))
SHAPES = ((1152, 128), (128, 128), (4, 6, 4, 128), (3, 4, 4, 128), (3, 3, 3, 128))


def final_kernel(chunk, rows, back_ref, pred_ref, own_ref, first_ref, last_ref, out_ref, *grads):
    step = pl.program_id(0)

    @pl.when(step == 0)
    def _():
        for (start, size), grad in zip(PARTS, grads):
            pieces = []
            at = start
            while at < start + size:
                t = at // chunk
                stop = min((t + 1) * chunk, start + size)
                pieces.append(back_ref[t, at - t * chunk : stop - t * chunk, :].astype(F32))
                at = stop
            whole = jnp.concatenate(pieces, axis=0) if len(pieces) > 1 else pieces[0]
            if len(grad.shape) == 2:
                grad[...] = whole
            else:
                group = grad.shape[2]
                for i in range(grad.shape[0]):
                    for j in range(grad.shape[1]):
                        at = (i * grad.shape[1] + j) * group
                        grad[i, j] = whole[at : at + group]

    row = lax.broadcasted_iota(jnp.int32, (rows, HALF), 0)
    for s in range(out_ref.shape[0]):
        slot = step * out_ref.shape[0] + s
        ahead = back_ref[slot, chunk : chunk + 16, :].astype(F32)
        base = jnp.concatenate([ahead[0:8], ahead[8:16]], axis=1) + own_ref[s]
        for k in range(3):
            for p in range(2):
                for q in range(2):
                    at = ((k * 2 + p) * 2 + q) * rows
                    pick = slice(k * 2 + q, k * 2 + q + 1)
                    edge = (first_ref if p == 0 else last_ref)[s, pick, :]
                    reached = row == (0 if p == 0 else rows - 1)
                    out_ref[s, at : at + rows, :] = (
                        pred_ref[s, at : at + rows, :]
                        + base[pick]
                        + jnp.where(reached, edge, 0.0)
                    ).astype(BF)


def run_final(back, pred, own, first, last):
    slots, main, width = pred.shape
    chunk = back.shape[1] - 16
    held = FINAL_SLOTS if main % 192 == 0 else 2 * FINAL_SLOTS

    def per_slots(array):
        return pl.BlockSpec((held,) + array.shape[1:], lambda n: (n, 0, 0))

    def body(*refs):
        final_kernel(chunk, main // 12, *refs)

    return pl.pallas_call(
        body,
        grid=(slots // held,),
        in_specs=[pl.BlockSpec(back.shape, lambda n: (0, 0, 0))]
        + [per_slots(a) for a in (pred, own, first, last)],
        out_specs=[per_slots(pred)]
        + [pl.BlockSpec(shape, lambda n, dims=len(shape): (0,) * dims) for shape in SHAPES],
        out_shape=[jax.ShapeDtypeStruct(pred.shape, BF)]
        + [jax.ShapeDtypeStruct(shape, F32) for shape in SHAPES],
        compiler_params=pltpu.CompilerParams(vmem_limit_bytes=32 * 1024 * 1024),
    )(back, pred, own, first, last)


def exchanged(value):
    return lax.all_to_all(value, "tile", split_axis=0, concat_axis=0, tiled=True)


def local(
    coarse_solution,
    geometry,
    fine_fields,
    cotangent,
    sample_ids,
    first_weight,
    dilated_weight,
    project_weight,
    down_weight,
    up_weight,
):
    peers = lax.axis_size("tile")
    position = lax.axis_index("tile")
    slots, rows = fine_fields.shape[0], fine_fields.shape[4]
    up = [(i, i + 1) for i in range(peers - 1)]
    down = [(i + 1, i) for i in range(peers - 1)]

    made = constants(rows)
    fine = fine_fields.reshape(slots, 12 * rows, HALF)
    cot = cotangent.reshape(slots, 12 * rows, HALF)

    sent, edge_last, edge_first = run_early(
        peers,
        coarse_solution,
        geometry,
        fine,
        cot,
        jnp.asarray(made["early_x"], BF),
        jnp.asarray(made["early_s"], BF),
    )
    coarse = exchanged(sent)
    from_before = lax.ppermute(edge_last, "tile", up)
    from_after = lax.ppermute(edge_first, "tile", down)
    sums = coarse[:, SENT_INPUT:].astype(F32)
    sums = sums[:, :16] + sums[:, 16:]
    order = lax.broadcasted_iota(jnp.int32, (peers, peers), 0)
    other = lax.broadcasted_iota(jnp.int32, (peers, peers), 1)
    behind = jnp.sum(jnp.where((other > order)[:, :, None, None], sums[None], 0.0), axis=1)
    later = exchanged(behind)

    fixed = [
        jnp.asarray(made["sel_x"], BF),
        jnp.asarray(made["sel_s"], BF),
        jnp.asarray(made["sel_o"], BF),
        jnp.asarray(made["ex"], BF),
        jnp.asarray(made["eu"], BF),
        jnp.asarray(made["ext"], BF),
        jnp.asarray(made["eut"], BF),
        jnp.asarray(made["ef"], BF),
        jnp.asarray(made["eft"], BF),
        jnp.asarray(made["pool_both"], BF),
    ]
    second = dilated_weight
    up_flat = up_weight.reshape(96, 128)
    weights = [
        jnp.pad(first_weight.reshape(27, 128), ((0, 5), (0, 0))).T,
        jnp.transpose(second, (1, 3, 0, 2)).reshape(384, 384),
        jnp.transpose(second, (0, 2, 1, 3)).reshape(384, 384),
        project_weight,
        project_weight.T,
        down_weight.reshape(48, 128).T,
        up_flat.T,
        up_flat,
    ]
    pred_local, last_edge, first_edge, own, sent = run_slots(
        peers,
        sample_ids,
        position.reshape(1).astype(jnp.int32),
        coarse,
        fine,
        cot,
        from_before,
        from_after,
        later,
        fixed,
        weights,
    )

    chunk = GRAD_ROWS // peers
    got = exchanged(sent).astype(F32)
    to_first = lax.ppermute(first_edge, "tile", up)
    to_last = lax.ppermute(last_edge, "tile", down)
    reduced = jnp.sum(got[:, :chunk], axis=0).astype(BF)
    sums = got[:, chunk:]
    ahead = jnp.sum(jnp.where((other < order)[:, :, None, None], sums[None], 0.0), axis=1)
    reduced, to_first, to_last = lax.optimization_barrier((reduced, to_first, to_last))
    back = exchanged(
        jnp.concatenate(
            [
                jnp.broadcast_to(reduced, (peers, chunk, 128)),
                ahead.astype(BF),
            ],
            axis=1,
        )
    )
    prediction, dilated, project, up_grad, down_grad, first = run_final(
        back, pred_local, own, to_first, to_last
    )
    return (
        prediction.reshape(fine_fields.shape),
        first,
        dilated.reshape(dilated_weight.shape),
        project,
        down_grad,
        jnp.swapaxes(up_grad, 1, 2),
    )


def solution(mesh):
    in_specs = (
        P(("groups", "tile"), None, None),
        P(("groups", "tile"), None),
        P("groups", None, None, None, "tile", None),
        P("groups", None, None, None, "tile", None),
        P("groups"),
        P(),
        P(),
        P(),
        P(),
        P(),
    )
    out_specs = (
        P("groups", None, None, None, "tile", None),
        P("groups", None, None, None),
        P("groups", None, None, None),
        P("groups", None),
        P("groups", None, None, None),
        P("groups", None, None, None),
    )
    return jax.shard_map(local, mesh=mesh, in_specs=in_specs, out_specs=out_specs, check_vma=False)
```

```python
import math

import jax
import jax.numpy as jnp
import numpy as np
from jax import lax
from jax.experimental import pallas as pl
from jax.experimental.pallas import tpu as pltpu
from jax.sharding import PartitionSpec as P

CG = 64
FG = 512
HALF = FG // 2
SCALE = 1.0 / math.sqrt(FG)
GELU_A = math.sqrt(2.0 / math.pi)
GELU_B = GELU_A * 0.044715
BF = jnp.bfloat16
F32 = jnp.float32

AUX = 64
SENT_INPUT = 32
SENT_EARLY = SENT_INPUT + 32
PER_STEP = 4
GRAD_ROWS = 1536
UP_AT, DOWN_AT, FIRST_AT, PROJECT_AT = 1280, 1376, 1424, 1152


def nn(a, b):
    return lax.dot_general(a, b, (((1,), (0,)), ((), ())), preferred_element_type=F32)


def nt(a, b):
    return lax.dot_general(a, b, (((1,), (1,)), ((), ())), preferred_element_type=F32)


def halves(value):
    high = value.astype(BF)
    return high, (value - high.astype(F32)).astype(BF)


def row_at(tap, r):
    if tap == 0:
        return 8 if r == 0 else 4 + r - 1
    if tap == 1:
        return r
    if tap == 2:
        return 4 + r
    return 9 if r == 3 else r + 1


def fine_row(block, index):
    if index == 8:
        return 8 * block - 1
    if index == 9:
        return 8 * block + 8
    return 8 * block + 2 * (index % 4) + index // 4


COL_GROUP = (2, 0, 1, 3)


def constants(rows):
    blocks = rows // 4
    last = 2 * rows
    width = 12 * rows + AUX

    def held(ch, q, o):
        return ((ch * 2 + o % 2) * 2 + q) * rows + o // 2

    sel_x = np.zeros((blocks, 2, 32, width), np.float32)
    sel_s = np.zeros((blocks, 2, 64, width), np.float32)
    sel_o = np.zeros((12 * rows + 32, blocks, 2, 64), np.float32)
    base = 12 * rows
    for b in range(blocks):
        for q in range(2):
            for ch in range(3):
                for index in range(10):
                    o = fine_row(b, index)
                    at = ch * 10 + index
                    if o == -1:
                        sel_x[b, q, at, base + ch * 2 + q] = 1
                        sel_s[b, q, at, base + 6 + ch * 2 + q] = 1
                        sel_s[b, q, 32 + at, base + 6 + ch * 2 + q] = 1
                    elif o == last:
                        sel_x[b, q, at, base + 16 + ch * 2 + q] = 1
                        sel_s[b, q, at, base + 22 + ch * 2 + q] = 1
                    else:
                        sel_x[b, q, at, held(ch, q, o)] = 1
                        sel_s[b, q, at, held(ch, q, o)] = 1
                    for later in range(max(o, 0), last):
                        sel_s[b, q, 32 + at, held(ch, q, later)] = 1
                    sel_s[b, q, 32 + at, base + 32 + ch * 2 + q] = 1
                    sel_s[b, q, 32 + at, base + 40 + ch * 2 + q] = 1
                    for target in range(max(o, 0), last):
                        if target == o:
                            sel_o[held(ch, q, target), b, q, at] = 1
                        if o >= 0:
                            sel_o[held(ch, q, target), b, q, 32 + at] = 1
                    if o == -1:
                        sel_o[base + ch * 2 + q, b, q, at] = 1
                        sel_o[base + 8 + ch * 2 + q, b, q, 32 + at] = 1
                    else:
                        sel_o[base + 24 + ch * 2 + q, b, q, 32 + at] = 1
                    if o == last:
                        sel_o[base + 16 + ch * 2 + q, b, q, at] = 1
    early_x = np.zeros((48, 12 * rows), np.float32)
    early_s = np.zeros((48, 12 * rows), np.float32)
    for ch in range(3):
        for q in range(2):
            at = ch * 2 + q
            for o in range(last):
                early_s[at, held(ch, q, o)] = 1
            for start, o in ((16, last - 1), (32, 0)):
                early_x[start + at, held(ch, q, o)] = 1
                early_s[start + 6 + at, held(ch, q, o)] = 1
    ex = np.zeros((4, 128, 48), np.float32)
    eu = np.zeros((4, 256, 96), np.float32)
    for r in range(4):
        for i in range(4):
            for j in range(4):
                for ch in range(3):
                    ex[r, COL_GROUP[j] * 32 + ch * 10 + row_at(i, r), (ch * 4 + i) * 4 + j] = 1
                for k in range(6):
                    at = COL_GROUP[j] * 64 + (k // 3) * 32 + (k % 3) * 10 + row_at(i, r)
                    eu[r, at, (i * 4 + j) * 6 + k] = 1
    ef = np.zeros((80, 32), np.float32)
    for ch in range(3):
        for tap in range(9):
            ef[tap * 8 + ch, ch * 9 + tap] = 1
    ef_all = np.zeros((3, 256, 32), np.float32)
    for window in range(3):
        ef_all[window, window * 80 : (window + 1) * 80] = ef
    pool = np.zeros((CG, HALF), np.float32)
    for c in range(HALF):
        pool[c // 4, c] = 1
    none = np.zeros((CG, HALF), np.float32)
    return dict(
        sel_x=sel_x.reshape(blocks * 64, width),
        sel_s=sel_s.reshape(blocks * 128, width),
        early_x=early_x,
        early_s=early_s,
        sel_o=sel_o.reshape(12 * rows + 32, blocks * 128),
        ex=ex.reshape(512, 48),
        eu=eu.reshape(1024, 96),
        ext=np.concatenate(list(np.swapaxes(ex, 1, 2)), 1),
        eut=np.concatenate(list(np.swapaxes(eu, 1, 2)), 1)
        .reshape(4, 4, 6, 1024)
        .swapaxes(1, 2)
        .reshape(96, 1024),
        ef=ef_all.reshape(768, 32),
        eft=ef.T,
        pool_both=np.concatenate([pool, none, none, pool, pool, pool], 0),
    )


def gelu_both(pre):
    square = pre * pre
    t = jnp.tanh(pre * (GELU_B * square + GELU_A))
    gate = 0.5 + 0.5 * t
    value = pre * gate
    slope = gate + (value * (1.0 - gate)) * (6.0 * GELU_B * square + 2.0 * GELU_A)
    return value, slope


def moved(value, shift, lane, keep):
    width = value.shape[1]
    return jnp.where(keep(lane), pltpu.roll(value, shift % width, 1), 0.0)


def coarse_forward(blocks, tile, coarse_ref, w1_ref, second_t_ref, project_t_ref, store, place):
    patches_s, columns_s, first_slope_s, second_slope_s, feature_s, wide_s = store
    cells = blocks * CG
    by_segment = coarse_ref[0, 0:SENT_INPUT, :].astype(F32)
    inputs = jnp.concatenate(
        [by_segment[at : at + 4] for at in range(0, SENT_INPUT, 4)], axis=1
    )
    inputs = jnp.concatenate([inputs, jnp.zeros_like(inputs)], axis=0)
    lane_in = lax.broadcasted_iota(jnp.int32, inputs.shape, 1) % CG
    by_col = (
        moved(inputs, 2, lane_in, lambda x: x >= 2),
        inputs,
        moved(inputs, -2, lane_in, lambda x: x < CG - 2),
    )
    above = jnp.where(tile * blocks >= 4, 1.0, 0.0)
    below = jnp.where(tile * blocks + 4 <= CG - blocks, 1.0, 0.0)
    windows = []
    for window in range(3):
        pieces = []
        for row_tap in range(3):
            for col_tap in range(3):
                start = (4 * window + 2 * row_tap) * CG
                pieces.append(by_col[col_tap][:, start : start + cells])
        pieces.append(jnp.zeros((8, cells), F32))
        piece = jnp.concatenate(pieces, axis=0)
        if window == 0:
            piece = piece * above
        if window == 2:
            piece = piece * below
        windows.append(piece.astype(BF))
    first_value, first_slope = gelu_both(
        nn(w1_ref[...], jnp.concatenate(windows + [jnp.zeros((16, cells), BF)], axis=0))
    )
    yield
    stacked = first_value.astype(BF)
    taps = nn(second_t_ref[...], stacked)
    lane_c = lax.broadcasted_iota(jnp.int32, (128, cells), 1) % CG
    second_pre = (
        taps[128:256]
        + moved(taps[0:128], 4, lane_c, lambda x: x >= 4)
        + moved(taps[256:384], -4, lane_c, lambda x: x < CG - 4)
    )
    second_value, second_slope = gelu_both(second_pre)
    yield
    feature = second_value.astype(BF)
    patches_s[place] = jnp.concatenate(windows, axis=1)
    columns_s[place] = stacked
    first_slope_s[place] = first_slope
    second_slope_s[place] = second_slope
    feature_s[place] = feature
    projected = nn(project_t_ref[...], feature)
    left = lax.broadcasted_iota(jnp.int32, (128, 128), 1) < CG
    for at in range(blocks // 2):
        pair = projected[:, at * 128 : (at + 1) * 128]
        high = pair.astype(BF).astype(F32)
        low = pair - high
        even = jnp.where(left, high, pltpu.roll(low, CG, 1))
        odd = jnp.where(left, pltpu.roll(high, CG, 1), low)
        wide_s[place, at * 256 : at * 256 + 128, :] = even.astype(BF)
        wide_s[place, at * 256 + 128 : at * 256 + 256, :] = odd.astype(BF)


def coarse_backward(blocks, d_project, project_ref, second_ref, store, place, dil_ref, pg_ref, fg_ref):
    patches_s, columns_s, first_slope_s, second_slope_s, feature_s, _ = store
    cells = blocks * CG
    pg_ref[...] += nt(feature_s[place], d_project)
    d_feature = nn(project_ref[...], d_project).astype(BF).astype(F32)
    d_second = (d_feature * second_slope_s[place]).astype(BF).astype(F32)
    yield
    lane_c = lax.broadcasted_iota(jnp.int32, (128, cells), 1) % CG
    shifted = jnp.concatenate(
        [
            moved(d_second, -4, lane_c, lambda x: x < CG - 4),
            d_second,
            moved(d_second, 4, lane_c, lambda x: x >= 4),
        ],
        axis=0,
    ).astype(BF)
    dil_ref[...] += nt(columns_s[place], shifted)
    back = nn(second_ref[...], shifted)
    yield
    d_first = (back * first_slope_s[place]).astype(BF)
    d_first = jnp.concatenate([d_first[0:128], d_first[128:256], d_first[256:384]], axis=1)
    fg_ref[...] += nt(patches_s[place], d_first)


def advance(stage):
    next(stage, None)


def finish(stage):
    for _ in stage:
        pass


def slot_kernel(
    blocks,
    peers,
    ids_ref,
    tile_ref,
    coarse_first_ref,
    coarse_refs,
    fine_ref,
    cot_ref,
    before_ref,
    after_ref,
    later_ref,
    sel_x_ref,
    sel_s_ref,
    sel_o_ref,
    ex_ref,
    eu_ref,
    ext_ref,
    eut_ref,
    ef_ref,
    eft_ref,
    spread_ref,
    first_t_ref,
    second_t_ref,
    second_ref,
    project_ref,
    project_t_ref,
    down_t_ref,
    up_t_ref,
    up_ref,
    pred_ref,
    to_last_ref,
    to_first_ref,
    own_ref,
    sent_ref,
    dil_ref,
    pg_ref,
    w_ref,
    u_ref,
    ut_ref,
    w1_ref,
    gu_ref,
    gd_ref,
    fg_ref,
    d_project_ref,
    *store,
):
    step = pl.program_id(0)
    tile = tile_ref[0]
    chunk = GRAD_ROWS // peers

    def forward(source, place):
        return coarse_forward(
            blocks, tile, source, w1_ref, second_t_ref, project_t_ref, store, place
        )

    def backward(place):
        return coarse_backward(
            blocks, d_project_ref[...], project_ref, second_ref, store, place, dil_ref, pg_ref, fg_ref
        )

    @pl.when(step == 0)
    def _():
        for r in range(4):
            rows = slice(r * 128, (r + 1) * 128)
            w_ref[rows, :] = nt(down_t_ref[...], ex_ref[rows, :]).astype(BF)
            taps = eu_ref[r * 256 : (r + 1) * 256, :]
            u_ref[rows, :] = nt(up_t_ref[...], taps).astype(BF)
            ut_ref[:, rows] = nn(taps, up_ref[...]).astype(BF)
        for window in range(3):
            w1_ref[window * 128 : (window + 1) * 128, :] = nt(
                first_t_ref[...], ef_ref[window * 256 : (window + 1) * 256, :]
            ).astype(BF)
        gu_ref[...] = jnp.zeros_like(gu_ref)
        gd_ref[...] = jnp.zeros_like(gd_ref)
        fg_ref[...] = jnp.zeros_like(fg_ref)
        dil_ref[...] = jnp.zeros_like(dil_ref)
        pg_ref[...] = jnp.zeros_like(pg_ref)
        d_project_ref[...] = jnp.zeros_like(d_project_ref)
        for buffer in store:
            buffer[2] = jnp.zeros(buffer.shape[1:], buffer.dtype)
        finish(forward(coarse_first_ref, 0))

    def one_slot(u, slot, now, soon, done):
        back = backward(done)
        ahead = forward(coarse_refs[u], soon)
        advance(back)
        later = later_ref[u].astype(F32)
        later = jnp.concatenate([later[0:8], later[8:16]], axis=1)
        later_high = later.astype(BF).astype(F32)
        later_both = jnp.concatenate([later_high, later - later_high], axis=0).astype(BF)
        aux = [before_ref[u], after_ref[u], later_both, jnp.zeros((16, HALF), BF)]
        fine_all = nn(sel_x_ref[...], jnp.concatenate([fine_ref[u]] + aux, axis=0))
        slope_all = nn(sel_s_ref[...], jnp.concatenate([cot_ref[u]] + aux, axis=0))
        row = lax.broadcasted_iota(jnp.int32, (64, HALF), 0)
        flux_scale = jnp.where(row >= 32, SCALE, 1.0)
        outside = (row == 40) | (row == 50) | (row == 60)
        top_scale = jnp.where(outside & (tile == 0), 0.0, flux_scale)
        lane32 = lax.broadcasted_iota(jnp.int32, (32, HALF), 1)
        lane64 = lax.broadcasted_iota(jnp.int32, (64, HALF), 1)
        not_first = lambda x: x >= 1
        not_last = lambda x: x < HALF - 1

        def enter(b):
            x0 = fine_all[b * 64 : b * 64 + 32]
            x1 = fine_all[b * 64 + 32 : b * 64 + 64]
            x_taps = jnp.concatenate(
                [x0, x1, moved(x1, 1, lane32, not_first), moved(x0, -1, lane32, not_last)], axis=0
            ).astype(BF)
            scale = top_scale if b == 0 else flux_scale
            s0 = slope_all[b * 128 : b * 128 + 64] * scale
            s1 = slope_all[b * 128 + 64 : b * 128 + 128] * scale
            s_taps = jnp.concatenate(
                [s0, s1, moved(s1, 1, lane64, not_first), moved(s0, -1, lane64, not_last)], axis=0
            ).astype(BF)
            coarse_part = store[5][now, b * 128 : (b + 1) * 128, :]
            left = jnp.concatenate(
                [w_ref[...], jnp.concatenate([coarse_part] * 4, axis=0)], axis=1
            )
            third = nn(left, jnp.concatenate([x_taps, spread_ref[256:384, :]], axis=0))
            return [x_taps, s_taps, third]

        def middle(entered, part):
            rows = slice(part * 128, (part + 1) * 128)
            value, slope = gelu_both(entered[2][rows])
            return value.astype(BF), (entered[3][rows] * slope).astype(BF)

        def leave(b, held):
            hidden = held[2]
            taps = nn(ut_ref[...], hidden)
            c0 = taps[0:64] + moved(taps[192:256], 1, lane64, not_first)
            c1 = taps[64:128] + moved(taps[128:192], -1, lane64, not_last)
            return [c0 * flux_scale, c1 * flux_scale]

        def collect(even, odd):
            s_taps = jnp.concatenate([even[1], odd[1]], axis=1)
            hidden = jnp.concatenate([even[2], odd[2]], axis=1)
            gu_ref[...] += nt(hidden, s_taps)
            x_taps = jnp.concatenate(
                [
                    jnp.concatenate([even[0], odd[0]], axis=1),
                    jnp.concatenate([spread_ref[0:128, :], spread_ref[128:256, :]], axis=1),
                ],
                axis=0,
            )
            both = nt(jnp.concatenate([even[3], odd[3]], axis=1), x_taps)
            gd_ref[...] += both[:, 0:128]
            per_row = both[:, 128:256]
            return (per_row[0:128] + per_row[128:256]) + (per_row[256:384] + per_row[384:512])

        combined = []
        pooled = []
        entered = {}
        held = {}
        for turn in range(blocks + 2):
            working = 0 <= turn - 1 < blocks
            parts = []

            def work():
                if working:
                    parts.append(middle(entered[turn - 1], len(parts)))

            if turn < blocks:
                entered[turn] = enter(turn)
            work()
            if turn < blocks:
                entered[turn].append(nn(u_ref[...], entered[turn][1]))
            work()
            b = turn - 2
            if b >= 0:
                combined += leave(b, held[b])
            work()
            if b >= 0 and b % 2 == 1:
                pooled.append(collect(held[b - 1], held[b]))
            if turn == 1:
                advance(back)
            if turn == 2:
                finish(back)
            if turn >= 3:
                advance(ahead)
            work()
            if working:
                held[turn - 1] = entered[turn - 1][:2] + [
                    jnp.concatenate([part[at] for part in parts], axis=0) for at in range(2)
                ]

        out = jnp.concatenate(combined, axis=0)
        finish(ahead)
        placed = nn(sel_o_ref[...], out.astype(BF))
        main = pred_ref.shape[1]
        pred_ref[u] = placed[0:main]
        before_flux = placed[main + 8 : main + 16]
        own = before_flux * jnp.where(tile >= 1, 1.0, 0.0)
        flux = placed[main + 24 : main + 32] + own
        to_last_ref[u] = placed[main : main + 8] + before_flux
        to_first_ref[u] = placed[main + 16 : main + 24]
        own_ref[u] = own
        flux = jnp.concatenate([flux[:, 0:128], flux[:, 128:256]], axis=0)
        sent_ref[slot, chunk : chunk + 16, :] = flux.astype(BF)
        d_project_ref[...] = jnp.concatenate(pooled, axis=1).astype(BF)

    for u in range(PER_STEP):
        slot = step * PER_STEP + u
        now = lax.rem(slot, 3)
        one_slot(u, slot, now, lax.rem(slot + 1, 3), lax.rem(slot + 2, 3))

    @pl.when(step == pl.num_programs(0) - 1)
    def _():
        finish(backward((pl.num_programs(0) * PER_STEP - 1) % 3))
        rows = [slice(r * 128, (r + 1) * 128) for r in range(4)]
        taps = halves(jnp.concatenate([gu_ref[at, :] for at in rows], axis=1))
        up = nt(eut_ref[...], taps[0]) + nt(eut_ref[...], taps[1])
        taps = halves(jnp.concatenate([gd_ref[at, :] for at in rows], axis=1))
        down = nt(ext_ref[...], taps[0]) + nt(ext_ref[...], taps[1])
        taps = halves(fg_ref[...])
        first = nn(eft_ref[...], taps[0]) + nn(eft_ref[...], taps[1])
        pieces = [
            dil_ref[i * 128 : (i + 1) * 128, j * 128 : (j + 1) * 128]
            for i in range(3)
            for j in range(3)
        ]
        pieces += [pg_ref[...], up, down, first]
        pieces.append(jnp.zeros((GRAD_ROWS - FIRST_AT - 32, 128), F32))
        grads = jnp.concatenate(pieces, axis=0).astype(BF)
        for t in range(peers):
            sent_ref[t, 0:chunk, :] = grads[t * chunk : (t + 1) * chunk, :]


def run_slots(peers, ids, tile, coarse, fine, cot, before, after, later, fixed, weights):
    slots, main, width = fine.shape
    blocks = main // 48
    cells = blocks * CG
    chunk = GRAD_ROWS // peers

    def coarse_of(ahead):
        return pl.BlockSpec(
            one, lambda n, ids, tile: (ids[jnp.minimum(n * PER_STEP + ahead, slots - 1)], 0, 0)
        )

    def whole(array):
        return pl.BlockSpec(array.shape, lambda n, ids, tile: (0,) * array.ndim)

    def per_slot(array):
        return pl.BlockSpec((PER_STEP,) + array.shape[1:], lambda n, ids, tile: (n, 0, 0))

    one = (1,) + coarse.shape[1:]
    in_specs = [
        pl.BlockSpec(one, lambda n, ids, tile: (ids[0], 0, 0)),
        *[coarse_of(ahead + 1) for ahead in range(PER_STEP)],
        per_slot(fine),
        per_slot(cot),
        per_slot(before),
        per_slot(after),
        per_slot(later),
    ] + [whole(a) for a in fixed + weights]
    edge = jax.ShapeDtypeStruct((slots, 8, width), F32)
    out_shape = [
        jax.ShapeDtypeStruct((slots, main, width), F32),
        edge,
        edge,
        edge,
        jax.ShapeDtypeStruct((peers, chunk + 16, 128), BF),
    ]
    grid_spec = pltpu.PrefetchScalarGridSpec(
        num_scalar_prefetch=2,
        grid=(slots // PER_STEP,),
        in_specs=in_specs,
        out_specs=[per_slot(a) for a in out_shape[:4]] + [whole(out_shape[4])],
        scratch_shapes=[
            pltpu.VMEM((384, 384), F32),
            pltpu.VMEM((128, 128), F32),
            pltpu.VMEM((512, 128), BF),
            pltpu.VMEM((512, 256), BF),
            pltpu.VMEM((256, 512), BF),
            pltpu.VMEM((384, 256), BF),
            pltpu.VMEM((512, 256), F32),
            pltpu.VMEM((512, 128), F32),
            pltpu.VMEM((80, 128), F32),
            pltpu.VMEM((128, cells), BF),
            pltpu.VMEM((3, 80, 3 * cells), BF),
            pltpu.VMEM((3, 384, cells), BF),
            pltpu.VMEM((3, 384, cells), F32),
            pltpu.VMEM((3, 128, cells), F32),
            pltpu.VMEM((3, 128, cells), BF),
            pltpu.VMEM((3, blocks * 128, 128), BF),
        ],
    )

    def body(*refs):
        slot_kernel(blocks, peers, *refs[:3], refs[3 : 3 + PER_STEP], *refs[3 + PER_STEP :])

    return pl.pallas_call(
        body,
        grid_spec=grid_spec,
        out_shape=out_shape,
        compiler_params=pltpu.CompilerParams(vmem_limit_bytes=52 * 1024 * 1024),
        cost_estimate=pl.CostEstimate(
            flops=slots * blocks * 500_000_000, bytes_accessed=16_000_000, transcendentals=0
        ),
    )(ids, tile, *[coarse] * (PER_STEP + 1), fine, cot, before, after, later, *fixed, *weights)


EARLY_SLOTS = 8


def early_kernel(
    blocks, peers, solution_ref, geometry_ref, fine_ref, cot_ref, x_ref, s_ref, sent_ref, last_ref, first_ref
):
    step = pl.program_id(0)

    @pl.when(step == 0)
    def _():
        inputs = jnp.concatenate(
            [
                solution_ref[0].astype(F32),
                geometry_ref[...].astype(F32),
                jnp.zeros((5, CG * CG), F32),
            ],
            axis=0,
        )
        edge = jnp.zeros((8, 6 * CG), F32)
        inputs = jnp.concatenate([edge, inputs, edge, jnp.zeros((8, 2 * CG), F32)], axis=1)
        for t in range(peers):
            at = t * blocks * CG
            sent_ref[t, 0:SENT_INPUT, :] = jnp.concatenate(
                [
                    inputs[0:4, at + segment * 128 : at + segment * 128 + 128]
                    for segment in range(SENT_INPUT // 4)
                ],
                axis=0,
            ).astype(BF)

    for u in range(EARLY_SLOTS):
        slot = step * EARLY_SLOTS + u
        picked = nn(x_ref[...], fine_ref[u]) + nn(s_ref[...], cot_ref[u])
        totals = jnp.concatenate(
            [picked[0:8, 0:128], picked[0:8, 128:256]], axis=0
        )
        high = totals.astype(BF)
        sent_ref[slot, SENT_INPUT : SENT_INPUT + 16, :] = high
        sent_ref[slot, SENT_INPUT + 16 : SENT_INPUT + 32, :] = (
            totals - high.astype(F32)
        ).astype(BF)
        last_ref[u] = picked[16:32].astype(BF)
        first_ref[u] = picked[32:48].astype(BF)


def run_early(peers, solution, geometry, fine, cot, pick_x, pick_s):
    slots, main, width = fine.shape

    def whole(array):
        return pl.BlockSpec(array.shape, lambda n: (0,) * array.ndim)

    def per_slots(array):
        return pl.BlockSpec((EARLY_SLOTS,) + array.shape[1:], lambda n: (n, 0, 0))

    edge = jax.ShapeDtypeStruct((slots, 16, width), BF)
    sent = jax.ShapeDtypeStruct((peers, SENT_EARLY, 128), BF)

    def body(*refs):
        early_kernel(main // 48, peers, *refs)

    return pl.pallas_call(
        body,
        grid=(slots // EARLY_SLOTS,),
        in_specs=[whole(solution), whole(geometry), per_slots(fine), per_slots(cot)]
        + [whole(pick_x), whole(pick_s)],
        out_specs=[whole(sent), per_slots(edge), per_slots(edge)],
        out_shape=[sent, edge, edge],
        compiler_params=pltpu.CompilerParams(vmem_limit_bytes=60 * 1024 * 1024),
    )(solution, geometry, fine, cot, pick_x, pick_s)


FINAL_SLOTS = 8
PARTS = ((0, 1152), (PROJECT_AT, 128), (UP_AT, 96), (DOWN_AT, 48), (FIRST_AT, 32))
SHAPES = ((1152, 128), (128, 128), (4, 6, 4, 128), (3, 4, 4, 128), (3, 3, 3, 128))


def final_kernel(chunk, rows, back_ref, pred_ref, own_ref, first_ref, last_ref, out_ref, *grads):
    step = pl.program_id(0)

    @pl.when(step == 0)
    def _():
        for (start, size), grad in zip(PARTS, grads):
            pieces = []
            at = start
            while at < start + size:
                t = at // chunk
                stop = min((t + 1) * chunk, start + size)
                pieces.append(back_ref[t, at - t * chunk : stop - t * chunk, :].astype(F32))
                at = stop
            whole = jnp.concatenate(pieces, axis=0) if len(pieces) > 1 else pieces[0]
            if len(grad.shape) == 2:
                grad[...] = whole
            else:
                group = grad.shape[2]
                for i in range(grad.shape[0]):
                    for j in range(grad.shape[1]):
                        at = (i * grad.shape[1] + j) * group
                        grad[i, j] = whole[at : at + group]

    row = lax.broadcasted_iota(jnp.int32, (rows, HALF), 0)
    for s in range(out_ref.shape[0]):
        slot = step * out_ref.shape[0] + s
        ahead = back_ref[slot, chunk : chunk + 16, :].astype(F32)
        base = jnp.concatenate([ahead[0:8], ahead[8:16]], axis=1) + own_ref[s]
        for k in range(3):
            for p in range(2):
                for q in range(2):
                    at = ((k * 2 + p) * 2 + q) * rows
                    pick = slice(k * 2 + q, k * 2 + q + 1)
                    edge = (first_ref if p == 0 else last_ref)[s, pick, :]
                    reached = row == (0 if p == 0 else rows - 1)
                    out_ref[s, at : at + rows, :] = (
                        pred_ref[s, at : at + rows, :]
                        + base[pick]
                        + jnp.where(reached, edge, 0.0)
                    ).astype(BF)


def run_final(back, pred, own, first, last):
    slots, main, width = pred.shape
    chunk = back.shape[1] - 16
    held = FINAL_SLOTS if main % 192 == 0 else 2 * FINAL_SLOTS

    def per_slots(array):
        return pl.BlockSpec((held,) + array.shape[1:], lambda n: (n, 0, 0))

    def body(*refs):
        final_kernel(chunk, main // 12, *refs)

    return pl.pallas_call(
        body,
        grid=(slots // held,),
        in_specs=[pl.BlockSpec(back.shape, lambda n: (0, 0, 0))]
        + [per_slots(a) for a in (pred, own, first, last)],
        out_specs=[per_slots(pred)]
        + [pl.BlockSpec(shape, lambda n, dims=len(shape): (0,) * dims) for shape in SHAPES],
        out_shape=[jax.ShapeDtypeStruct(pred.shape, BF)]
        + [jax.ShapeDtypeStruct(shape, F32) for shape in SHAPES],
        compiler_params=pltpu.CompilerParams(vmem_limit_bytes=32 * 1024 * 1024),
    )(back, pred, own, first, last)


def exchanged(value):
    return lax.all_to_all(value, "tile", split_axis=0, concat_axis=0, tiled=True)


def local(
    coarse_solution,
    geometry,
    fine_fields,
    cotangent,
    sample_ids,
    first_weight,
    dilated_weight,
    project_weight,
    down_weight,
    up_weight,
):
    peers = lax.axis_size("tile")
    position = lax.axis_index("tile")
    slots, rows = fine_fields.shape[0], fine_fields.shape[4]
    up = [(i, i + 1) for i in range(peers - 1)]
    down = [(i + 1, i) for i in range(peers - 1)]

    made = constants(rows)
    fine = fine_fields.reshape(slots, 12 * rows, HALF)
    cot = cotangent.reshape(slots, 12 * rows, HALF)

    sent, edge_last, edge_first = run_early(
        peers,
        coarse_solution,
        geometry,
        fine,
        cot,
        jnp.asarray(made["early_x"], BF),
        jnp.asarray(made["early_s"], BF),
    )
    coarse = exchanged(sent)
    from_before = lax.ppermute(edge_last, "tile", up)
    from_after = lax.ppermute(edge_first, "tile", down)
    sums = coarse[:, SENT_INPUT:].astype(F32)
    sums = sums[:, :16] + sums[:, 16:]
    order = lax.broadcasted_iota(jnp.int32, (peers, peers), 0)
    other = lax.broadcasted_iota(jnp.int32, (peers, peers), 1)
    behind = jnp.sum(jnp.where((other > order)[:, :, None, None], sums[None], 0.0), axis=1)
    later = exchanged(behind)

    fixed = [
        jnp.asarray(made["sel_x"], BF),
        jnp.asarray(made["sel_s"], BF),
        jnp.asarray(made["sel_o"], BF),
        jnp.asarray(made["ex"], BF),
        jnp.asarray(made["eu"], BF),
        jnp.asarray(made["ext"], BF),
        jnp.asarray(made["eut"], BF),
        jnp.asarray(made["ef"], BF),
        jnp.asarray(made["eft"], BF),
        jnp.asarray(made["pool_both"], BF),
    ]
    second = dilated_weight
    up_flat = up_weight.reshape(96, 128)
    weights = [
        jnp.pad(first_weight.reshape(27, 128), ((0, 5), (0, 0))).T,
        jnp.transpose(second, (1, 3, 0, 2)).reshape(384, 384),
        jnp.transpose(second, (0, 2, 1, 3)).reshape(384, 384),
        project_weight,
        project_weight.T,
        down_weight.reshape(48, 128).T,
        up_flat.T,
        up_flat,
    ]
    pred_local, last_edge, first_edge, own, sent = run_slots(
        peers,
        sample_ids,
        position.reshape(1).astype(jnp.int32),
        coarse,
        fine,
        cot,
        from_before,
        from_after,
        later,
        fixed,
        weights,
    )

    chunk = GRAD_ROWS // peers
    got = exchanged(sent).astype(F32)
    to_first = lax.ppermute(first_edge, "tile", up)
    to_last = lax.ppermute(last_edge, "tile", down)
    reduced = jnp.sum(got[:, :chunk], axis=0).astype(BF)
    sums = got[:, chunk:]
    ahead = jnp.sum(jnp.where((other < order)[:, :, None, None], sums[None], 0.0), axis=1)
    reduced, to_first, to_last = lax.optimization_barrier((reduced, to_first, to_last))
    back = exchanged(
        jnp.concatenate(
            [
                jnp.broadcast_to(reduced, (peers, chunk, 128)),
                ahead.astype(BF),
            ],
            axis=1,
        )
    )
    prediction, dilated, project, up_grad, down_grad, first = run_final(
        back, pred_local, own, to_first, to_last
    )
    return (
        prediction.reshape(fine_fields.shape),
        first,
        dilated.reshape(dilated_weight.shape),
        project,
        down_grad,
        jnp.swapaxes(up_grad, 1, 2),
    )


def solution(mesh):
    in_specs = (
        P(("groups", "tile"), None, None),
        P(("groups", "tile"), None),
        P("groups", None, None, None, "tile", None),
        P("groups", None, None, None, "tile", None),
        P("groups"),
        P(),
        P(),
        P(),
        P(),
        P(),
    )
    out_specs = (
        P("groups", None, None, None, "tile", None),
        P("groups", None, None, None),
        P("groups", None, None, None),
        P("groups", None),
        P("groups", None, None, None),
        P("groups", None, None, None),
    )
    return jax.shard_map(local, mesh=mesh, in_specs=in_specs, out_specs=out_specs, check_vma=False)
```

```python
import math

import jax
import jax.numpy as jnp
import numpy as np
from jax import lax
from jax.experimental import pallas as pl
from jax.experimental.pallas import tpu as pltpu
from jax.sharding import PartitionSpec as P

CG = 64
FG = 512
HALF = FG // 2
SCALE = 1.0 / math.sqrt(FG)
GELU_A = math.sqrt(2.0 / math.pi)
GELU_B = GELU_A * 0.044715
BF = jnp.bfloat16
F32 = jnp.float32

AUX = 64
SENT_INPUT = 32
SENT_EARLY = SENT_INPUT + 32
PER_STEP = 4
GRAD_ROWS = 1536
UP_AT, DOWN_AT, FIRST_AT, PROJECT_AT = 1280, 1376, 1424, 1152


def nn(a, b):
    return lax.dot_general(a, b, (((1,), (0,)), ((), ())), preferred_element_type=F32)


def nt(a, b):
    return lax.dot_general(a, b, (((1,), (1,)), ((), ())), preferred_element_type=F32)


def halves(value):
    high = value.astype(BF)
    return high, (value - high.astype(F32)).astype(BF)


def row_at(tap, r):
    if tap == 0:
        return 8 if r == 0 else 4 + r - 1
    if tap == 1:
        return r
    if tap == 2:
        return 4 + r
    return 9 if r == 3 else r + 1


def fine_row(block, index):
    if index == 8:
        return 8 * block - 1
    if index == 9:
        return 8 * block + 8
    return 8 * block + 2 * (index % 4) + index // 4


COL_GROUP = (2, 0, 1, 3)


def constants(rows):
    blocks = rows // 4
    last = 2 * rows
    width = 12 * rows + AUX

    def held(ch, q, o):
        return ((ch * 2 + o % 2) * 2 + q) * rows + o // 2

    sel_x = np.zeros((blocks, 2, 32, width), np.float32)
    sel_s = np.zeros((blocks, 2, 64, width), np.float32)
    sel_o = np.zeros((12 * rows + 32, blocks, 2, 64), np.float32)
    base = 12 * rows
    for b in range(blocks):
        for q in range(2):
            for ch in range(3):
                for index in range(10):
                    o = fine_row(b, index)
                    at = ch * 10 + index
                    if o == -1:
                        sel_x[b, q, at, base + ch * 2 + q] = 1
                        sel_s[b, q, at, base + 6 + ch * 2 + q] = 1
                        sel_s[b, q, 32 + at, base + 6 + ch * 2 + q] = 1
                    elif o == last:
                        sel_x[b, q, at, base + 16 + ch * 2 + q] = 1
                        sel_s[b, q, at, base + 22 + ch * 2 + q] = 1
                    else:
                        sel_x[b, q, at, held(ch, q, o)] = 1
                        sel_s[b, q, at, held(ch, q, o)] = 1
                    for later in range(max(o, 0), last):
                        sel_s[b, q, 32 + at, held(ch, q, later)] = 1
                    sel_s[b, q, 32 + at, base + 32 + ch * 2 + q] = 1
                    sel_s[b, q, 32 + at, base + 40 + ch * 2 + q] = 1
                    for target in range(max(o, 0), last):
                        if target == o:
                            sel_o[held(ch, q, target), b, q, at] = 1
                        if o >= 0:
                            sel_o[held(ch, q, target), b, q, 32 + at] = 1
                    if o == -1:
                        sel_o[base + ch * 2 + q, b, q, at] = 1
                        sel_o[base + 8 + ch * 2 + q, b, q, 32 + at] = 1
                    else:
                        sel_o[base + 24 + ch * 2 + q, b, q, 32 + at] = 1
                    if o == last:
                        sel_o[base + 16 + ch * 2 + q, b, q, at] = 1
    early_x = np.zeros((48, 12 * rows), np.float32)
    early_s = np.zeros((48, 12 * rows), np.float32)
    for ch in range(3):
        for q in range(2):
            at = ch * 2 + q
            for o in range(last):
                early_s[at, held(ch, q, o)] = 1
            for start, o in ((16, last - 1), (32, 0)):
                early_x[start + at, held(ch, q, o)] = 1
                early_s[start + 6 + at, held(ch, q, o)] = 1
    ex = np.zeros((4, 128, 48), np.float32)
    eu = np.zeros((4, 256, 96), np.float32)
    for r in range(4):
        for i in range(4):
            for j in range(4):
                for ch in range(3):
                    ex[r, COL_GROUP[j] * 32 + ch * 10 + row_at(i, r), (ch * 4 + i) * 4 + j] = 1
                for k in range(6):
                    at = COL_GROUP[j] * 64 + (k // 3) * 32 + (k % 3) * 10 + row_at(i, r)
                    eu[r, at, (i * 4 + j) * 6 + k] = 1
    ef = np.zeros((80, 32), np.float32)
    for ch in range(3):
        for tap in range(9):
            ef[tap * 8 + ch, ch * 9 + tap] = 1
    ef_all = np.zeros((3, 256, 32), np.float32)
    for window in range(3):
        ef_all[window, window * 80 : (window + 1) * 80] = ef
    pool = np.zeros((CG, HALF), np.float32)
    for c in range(HALF):
        pool[c // 4, c] = 1
    none = np.zeros((CG, HALF), np.float32)
    return dict(
        sel_x=sel_x.reshape(blocks * 64, width),
        sel_s=sel_s.reshape(blocks * 128, width),
        early_x=early_x,
        early_s=early_s,
        sel_o=sel_o.reshape(12 * rows + 32, blocks * 128),
        ex=ex.reshape(512, 48),
        eu=eu.reshape(1024, 96),
        ext=np.concatenate(list(np.swapaxes(ex, 1, 2)), 1),
        eut=np.concatenate(list(np.swapaxes(eu, 1, 2)), 1)
        .reshape(4, 4, 6, 1024)
        .swapaxes(1, 2)
        .reshape(96, 1024),
        ef=ef_all.reshape(768, 32),
        eft=ef.T,
        pool_both=np.concatenate([pool, none, none, pool, pool, pool], 0),
    )


def gelu_both(pre):
    square = pre * pre
    t = jnp.tanh(pre * (GELU_B * square + GELU_A))
    gate = 0.5 + 0.5 * t
    value = pre * gate
    slope = gate + (value * (1.0 - gate)) * (6.0 * GELU_B * square + 2.0 * GELU_A)
    return value, slope


def moved(value, shift, lane, keep):
    width = value.shape[1]
    return jnp.where(keep(lane), pltpu.roll(value, shift % width, 1), 0.0)


def coarse_forward(blocks, tile, coarse_ref, w1_ref, second_t_ref, project_t_ref, store, place):
    patches_s, columns_s, first_slope_s, second_slope_s, feature_s, wide_s = store
    cells = blocks * CG
    by_segment = coarse_ref[0, 0:SENT_INPUT, :].astype(F32)
    inputs = jnp.concatenate(
        [by_segment[at : at + 4] for at in range(0, SENT_INPUT, 4)], axis=1
    )
    inputs = jnp.concatenate([inputs, jnp.zeros_like(inputs)], axis=0)
    lane_in = lax.broadcasted_iota(jnp.int32, inputs.shape, 1) % CG
    by_col = (
        moved(inputs, 2, lane_in, lambda x: x >= 2),
        inputs,
        moved(inputs, -2, lane_in, lambda x: x < CG - 2),
    )
    above = jnp.where(tile * blocks >= 4, 1.0, 0.0)
    below = jnp.where(tile * blocks + 4 <= CG - blocks, 1.0, 0.0)
    windows = []
    for window in range(3):
        pieces = []
        for row_tap in range(3):
            for col_tap in range(3):
                start = (4 * window + 2 * row_tap) * CG
                pieces.append(by_col[col_tap][:, start : start + cells])
        pieces.append(jnp.zeros((8, cells), F32))
        piece = jnp.concatenate(pieces, axis=0)
        if window == 0:
            piece = piece * above
        if window == 2:
            piece = piece * below
        windows.append(piece.astype(BF))
    first_value, first_slope = gelu_both(
        nn(w1_ref[...], jnp.concatenate(windows + [jnp.zeros((16, cells), BF)], axis=0))
    )
    yield
    stacked = first_value.astype(BF)
    taps = nn(second_t_ref[...], stacked)
    lane_c = lax.broadcasted_iota(jnp.int32, (128, cells), 1) % CG
    second_pre = (
        taps[128:256]
        + moved(taps[0:128], 4, lane_c, lambda x: x >= 4)
        + moved(taps[256:384], -4, lane_c, lambda x: x < CG - 4)
    )
    second_value, second_slope = gelu_both(second_pre)
    yield
    feature = second_value.astype(BF)
    patches_s[place] = jnp.concatenate(windows, axis=1)
    columns_s[place] = stacked
    first_slope_s[place] = first_slope
    second_slope_s[place] = second_slope
    feature_s[place] = feature
    projected = nn(project_t_ref[...], feature)
    left = lax.broadcasted_iota(jnp.int32, (128, 128), 1) < CG
    for at in range(blocks // 2):
        pair = projected[:, at * 128 : (at + 1) * 128]
        high = pair.astype(BF).astype(F32)
        low = pair - high
        even = jnp.where(left, high, pltpu.roll(low, CG, 1))
        odd = jnp.where(left, pltpu.roll(high, CG, 1), low)
        wide_s[place, at * 256 : at * 256 + 128, :] = even.astype(BF)
        wide_s[place, at * 256 + 128 : at * 256 + 256, :] = odd.astype(BF)


def coarse_backward(blocks, d_project, project_ref, second_ref, store, place, dil_ref, pg_ref, fg_ref):
    patches_s, columns_s, first_slope_s, second_slope_s, feature_s, _ = store
    cells = blocks * CG
    pg_ref[...] += nt(feature_s[place], d_project)
    d_feature = nn(project_ref[...], d_project).astype(BF).astype(F32)
    d_second = (d_feature * second_slope_s[place]).astype(BF).astype(F32)
    yield
    lane_c = lax.broadcasted_iota(jnp.int32, (128, cells), 1) % CG
    shifted = jnp.concatenate(
        [
            moved(d_second, -4, lane_c, lambda x: x < CG - 4),
            d_second,
            moved(d_second, 4, lane_c, lambda x: x >= 4),
        ],
        axis=0,
    ).astype(BF)
    dil_ref[...] += nt(columns_s[place], shifted)
    back = nn(second_ref[...], shifted)
    yield
    d_first = (back * first_slope_s[place]).astype(BF)
    d_first = jnp.concatenate([d_first[0:128], d_first[128:256], d_first[256:384]], axis=1)
    fg_ref[...] += nt(patches_s[place], d_first)


def advance(stage):
    next(stage, None)


def finish(stage):
    for _ in stage:
        pass


def slot_kernel(
    blocks,
    peers,
    ids_ref,
    tile_ref,
    coarse_first_ref,
    coarse_refs,
    fine_ref,
    cot_ref,
    before_ref,
    after_ref,
    later_ref,
    sel_x_ref,
    sel_s_ref,
    sel_o_ref,
    ex_ref,
    eu_ref,
    ext_ref,
    eut_ref,
    ef_ref,
    eft_ref,
    spread_ref,
    first_t_ref,
    second_t_ref,
    second_ref,
    project_ref,
    project_t_ref,
    down_t_ref,
    up_t_ref,
    up_ref,
    pred_ref,
    to_last_ref,
    to_first_ref,
    own_ref,
    sent_ref,
    dil_ref,
    pg_ref,
    w_ref,
    u_ref,
    ut_ref,
    w1_ref,
    gu_ref,
    gd_ref,
    fg_ref,
    d_project_ref,
    *store,
):
    step = pl.program_id(0)
    tile = tile_ref[0]
    chunk = GRAD_ROWS // peers

    def forward(source, place):
        return coarse_forward(
            blocks, tile, source, w1_ref, second_t_ref, project_t_ref, store, place
        )

    def backward(place):
        return coarse_backward(
            blocks, d_project_ref[...], project_ref, second_ref, store, place, dil_ref, pg_ref, fg_ref
        )

    @pl.when(step == 0)
    def _():
        for r in range(4):
            rows = slice(r * 128, (r + 1) * 128)
            w_ref[rows, :] = nt(down_t_ref[...], ex_ref[rows, :]).astype(BF)
            taps = eu_ref[r * 256 : (r + 1) * 256, :]
            u_ref[rows, :] = nt(up_t_ref[...], taps).astype(BF)
            ut_ref[:, rows] = nn(taps, up_ref[...]).astype(BF)
        for window in range(3):
            w1_ref[window * 128 : (window + 1) * 128, :] = nt(
                first_t_ref[...], ef_ref[window * 256 : (window + 1) * 256, :]
            ).astype(BF)
        gu_ref[...] = jnp.zeros_like(gu_ref)
        gd_ref[...] = jnp.zeros_like(gd_ref)
        fg_ref[...] = jnp.zeros_like(fg_ref)
        dil_ref[...] = jnp.zeros_like(dil_ref)
        pg_ref[...] = jnp.zeros_like(pg_ref)
        d_project_ref[...] = jnp.zeros_like(d_project_ref)
        for buffer in store:
            buffer[2] = jnp.zeros(buffer.shape[1:], buffer.dtype)
        finish(forward(coarse_first_ref, 0))

    def one_slot(u, slot, now, soon, done):
        back = backward(done)
        ahead = forward(coarse_refs[u], soon)
        advance(back)
        later = later_ref[u].astype(F32)
        later = jnp.concatenate([later[0:8], later[8:16]], axis=1)
        later_high = later.astype(BF).astype(F32)
        later_both = jnp.concatenate([later_high, later - later_high], axis=0).astype(BF)
        aux = [before_ref[u], after_ref[u], later_both, jnp.zeros((16, HALF), BF)]
        fine_all = nn(sel_x_ref[...], jnp.concatenate([fine_ref[u]] + aux, axis=0))
        slope_all = nn(sel_s_ref[...], jnp.concatenate([cot_ref[u]] + aux, axis=0))
        row = lax.broadcasted_iota(jnp.int32, (64, HALF), 0)
        flux_scale = jnp.where(row >= 32, SCALE, 1.0)
        outside = (row == 40) | (row == 50) | (row == 60)
        top_scale = jnp.where(outside & (tile == 0), 0.0, flux_scale)
        lane32 = lax.broadcasted_iota(jnp.int32, (32, HALF), 1)
        lane64 = lax.broadcasted_iota(jnp.int32, (64, HALF), 1)
        not_first = lambda x: x >= 1
        not_last = lambda x: x < HALF - 1

        def enter(b):
            x0 = fine_all[b * 64 : b * 64 + 32]
            x1 = fine_all[b * 64 + 32 : b * 64 + 64]
            x_taps = jnp.concatenate(
                [x0, x1, moved(x1, 1, lane32, not_first), moved(x0, -1, lane32, not_last)], axis=0
            ).astype(BF)
            scale = top_scale if b == 0 else flux_scale
            s0 = slope_all[b * 128 : b * 128 + 64] * scale
            s1 = slope_all[b * 128 + 64 : b * 128 + 128] * scale
            s_taps = jnp.concatenate(
                [s0, s1, moved(s1, 1, lane64, not_first), moved(s0, -1, lane64, not_last)], axis=0
            ).astype(BF)
            coarse_part = store[5][now, b * 128 : (b + 1) * 128, :]
            left = jnp.concatenate(
                [w_ref[...], jnp.concatenate([coarse_part] * 4, axis=0)], axis=1
            )
            third = nn(left, jnp.concatenate([x_taps, spread_ref[256:384, :]], axis=0))
            return [x_taps, s_taps, third]

        def middle(entered, part):
            rows = slice(part * 128, (part + 1) * 128)
            value, slope = gelu_both(entered[2][rows])
            return value.astype(BF), (entered[3][rows] * slope).astype(BF)

        def leave(b, held):
            hidden = held[2]
            taps = nn(ut_ref[...], hidden)
            c0 = taps[0:64] + moved(taps[192:256], 1, lane64, not_first)
            c1 = taps[64:128] + moved(taps[128:192], -1, lane64, not_last)
            return [c0 * flux_scale, c1 * flux_scale]

        def collect(even, odd):
            s_taps = jnp.concatenate([even[1], odd[1]], axis=1)
            hidden = jnp.concatenate([even[2], odd[2]], axis=1)
            gu_ref[...] += nt(hidden, s_taps)
            x_taps = jnp.concatenate(
                [
                    jnp.concatenate([even[0], odd[0]], axis=1),
                    jnp.concatenate([spread_ref[0:128, :], spread_ref[128:256, :]], axis=1),
                ],
                axis=0,
            )
            both = nt(jnp.concatenate([even[3], odd[3]], axis=1), x_taps)
            gd_ref[...] += both[:, 0:128]
            per_row = both[:, 128:256]
            return (per_row[0:128] + per_row[128:256]) + (per_row[256:384] + per_row[384:512])

        combined = []
        pooled = []
        entered = {}
        held = {}
        for turn in range(blocks + 2):
            working = 0 <= turn - 1 < blocks
            parts = []

            def work():
                if working:
                    parts.append(middle(entered[turn - 1], len(parts)))

            if turn < blocks:
                entered[turn] = enter(turn)
            work()
            if turn < blocks:
                entered[turn].append(nn(u_ref[...], entered[turn][1]))
            work()
            b = turn - 2
            if b >= 0:
                combined += leave(b, held[b])
            work()
            if b >= 0 and b % 2 == 1:
                pooled.append(collect(held[b - 1], held[b]))
            if turn == 1:
                advance(back)
            if turn == 2:
                finish(back)
            if turn >= 3:
                advance(ahead)
            work()
            if working:
                held[turn - 1] = entered[turn - 1][:2] + [
                    jnp.concatenate([part[at] for part in parts], axis=0) for at in range(2)
                ]

        out = jnp.concatenate(combined, axis=0)
        finish(ahead)
        placed = nn(sel_o_ref[...], out.astype(BF))
        main = pred_ref.shape[1]
        pred_ref[u] = placed[0:main]
        before_flux = placed[main + 8 : main + 16]
        own = before_flux * jnp.where(tile >= 1, 1.0, 0.0)
        flux = placed[main + 24 : main + 32] + own
        to_last_ref[u] = placed[main : main + 8] + before_flux
        to_first_ref[u] = placed[main + 16 : main + 24]
        own_ref[u] = own
        flux = jnp.concatenate([flux[:, 0:128], flux[:, 128:256]], axis=0)
        sent_ref[slot, chunk : chunk + 16, :] = flux.astype(BF)
        d_project_ref[...] = jnp.concatenate(pooled, axis=1).astype(BF)

    for u in range(PER_STEP):
        slot = step * PER_STEP + u
        now = lax.rem(slot, 3)
        one_slot(u, slot, now, lax.rem(slot + 1, 3), lax.rem(slot + 2, 3))

    @pl.when(step == pl.num_programs(0) - 1)
    def _():
        finish(backward((pl.num_programs(0) * PER_STEP - 1) % 3))
        rows = [slice(r * 128, (r + 1) * 128) for r in range(4)]
        taps = halves(jnp.concatenate([gu_ref[at, :] for at in rows], axis=1))
        up = nt(eut_ref[...], taps[0]) + nt(eut_ref[...], taps[1])
        taps = halves(jnp.concatenate([gd_ref[at, :] for at in rows], axis=1))
        down = nt(ext_ref[...], taps[0]) + nt(ext_ref[...], taps[1])
        taps = halves(fg_ref[...])
        first = nn(eft_ref[...], taps[0]) + nn(eft_ref[...], taps[1])
        pieces = [
            dil_ref[i * 128 : (i + 1) * 128, j * 128 : (j + 1) * 128]
            for i in range(3)
            for j in range(3)
        ]
        pieces += [pg_ref[...], up, down, first]
        pieces.append(jnp.zeros((GRAD_ROWS - FIRST_AT - 32, 128), F32))
        grads = jnp.concatenate(pieces, axis=0).astype(BF)
        for t in range(peers):
            sent_ref[t, 0:chunk, :] = grads[t * chunk : (t + 1) * chunk, :]


def run_slots(peers, ids, tile, coarse, fine, cot, before, after, later, fixed, weights):
    slots, main, width = fine.shape
    blocks = main // 48
    cells = blocks * CG
    chunk = GRAD_ROWS // peers

    def coarse_of(ahead):
        return pl.BlockSpec(
            one, lambda n, ids, tile: (ids[jnp.minimum(n * PER_STEP + ahead, slots - 1)], 0, 0)
        )

    def whole(array):
        return pl.BlockSpec(array.shape, lambda n, ids, tile: (0,) * array.ndim)

    def per_slot(array):
        return pl.BlockSpec((PER_STEP,) + array.shape[1:], lambda n, ids, tile: (n, 0, 0))

    one = (1,) + coarse.shape[1:]
    in_specs = [
        pl.BlockSpec(one, lambda n, ids, tile: (ids[0], 0, 0)),
        *[coarse_of(ahead + 1) for ahead in range(PER_STEP)],
        per_slot(fine),
        per_slot(cot),
        per_slot(before),
        per_slot(after),
        per_slot(later),
    ] + [whole(a) for a in fixed + weights]
    edge = jax.ShapeDtypeStruct((slots, 8, width), F32)
    out_shape = [
        jax.ShapeDtypeStruct((slots, main, width), F32),
        edge,
        edge,
        edge,
        jax.ShapeDtypeStruct((peers, chunk + 16, 128), BF),
    ]
    grid_spec = pltpu.PrefetchScalarGridSpec(
        num_scalar_prefetch=2,
        grid=(slots // PER_STEP,),
        in_specs=in_specs,
        out_specs=[per_slot(a) for a in out_shape[:4]] + [whole(out_shape[4])],
        scratch_shapes=[
            pltpu.VMEM((384, 384), F32),
            pltpu.VMEM((128, 128), F32),
            pltpu.VMEM((512, 128), BF),
            pltpu.VMEM((512, 256), BF),
            pltpu.VMEM((256, 512), BF),
            pltpu.VMEM((384, 256), BF),
            pltpu.VMEM((512, 256), F32),
            pltpu.VMEM((512, 128), F32),
            pltpu.VMEM((80, 128), F32),
            pltpu.VMEM((128, cells), BF),
            pltpu.VMEM((3, 80, 3 * cells), BF),
            pltpu.VMEM((3, 384, cells), BF),
            pltpu.VMEM((3, 384, cells), F32),
            pltpu.VMEM((3, 128, cells), F32),
            pltpu.VMEM((3, 128, cells), BF),
            pltpu.VMEM((3, blocks * 128, 128), BF),
        ],
    )

    def body(*refs):
        slot_kernel(blocks, peers, *refs[:3], refs[3 : 3 + PER_STEP], *refs[3 + PER_STEP :])

    return pl.pallas_call(
        body,
        grid_spec=grid_spec,
        out_shape=out_shape,
        compiler_params=pltpu.CompilerParams(vmem_limit_bytes=52 * 1024 * 1024),
        cost_estimate=pl.CostEstimate(
            flops=slots * blocks * 500_000_000, bytes_accessed=16_000_000, transcendentals=0
        ),
    )(ids, tile, *[coarse] * (PER_STEP + 1), fine, cot, before, after, later, *fixed, *weights)


EARLY_SLOTS = 16


def early_kernel(
    blocks, peers, solution_ref, geometry_ref, fine_ref, cot_ref, x_ref, s_ref, sent_ref, last_ref, first_ref
):
    step = pl.program_id(0)

    @pl.when(step == 0)
    def _():
        inputs = jnp.concatenate(
            [
                solution_ref[0].astype(F32),
                geometry_ref[...].astype(F32),
                jnp.zeros((5, CG * CG), F32),
            ],
            axis=0,
        )
        edge = jnp.zeros((8, 6 * CG), F32)
        inputs = jnp.concatenate([edge, inputs, edge, jnp.zeros((8, 2 * CG), F32)], axis=1)
        for t in range(peers):
            at = t * blocks * CG
            sent_ref[t, 0:SENT_INPUT, :] = jnp.concatenate(
                [
                    inputs[0:4, at + segment * 128 : at + segment * 128 + 128]
                    for segment in range(SENT_INPUT // 4)
                ],
                axis=0,
            ).astype(BF)

    for u in range(EARLY_SLOTS):
        slot = step * EARLY_SLOTS + u
        picked = nn(x_ref[...], fine_ref[u]) + nn(s_ref[...], cot_ref[u])
        totals = jnp.concatenate(
            [picked[0:8, 0:128], picked[0:8, 128:256]], axis=0
        )
        high = totals.astype(BF)
        sent_ref[slot, SENT_INPUT : SENT_INPUT + 16, :] = high
        sent_ref[slot, SENT_INPUT + 16 : SENT_INPUT + 32, :] = (
            totals - high.astype(F32)
        ).astype(BF)
        last_ref[u] = picked[16:32].astype(BF)
        first_ref[u] = picked[32:48].astype(BF)


def run_early(peers, solution, geometry, fine, cot, pick_x, pick_s):
    slots, main, width = fine.shape

    def whole(array):
        return pl.BlockSpec(array.shape, lambda n: (0,) * array.ndim)

    def per_slots(array):
        return pl.BlockSpec((EARLY_SLOTS,) + array.shape[1:], lambda n: (n, 0, 0))

    edge = jax.ShapeDtypeStruct((slots, 16, width), BF)
    sent = jax.ShapeDtypeStruct((peers, SENT_EARLY, 128), BF)

    def body(*refs):
        early_kernel(main // 48, peers, *refs)

    return pl.pallas_call(
        body,
        grid=(slots // EARLY_SLOTS,),
        in_specs=[whole(solution), whole(geometry), per_slots(fine), per_slots(cot)]
        + [whole(pick_x), whole(pick_s)],
        out_specs=[whole(sent), per_slots(edge), per_slots(edge)],
        out_shape=[sent, edge, edge],
        compiler_params=pltpu.CompilerParams(vmem_limit_bytes=60 * 1024 * 1024),
    )(solution, geometry, fine, cot, pick_x, pick_s)


FINAL_SLOTS = 8
PARTS = ((0, 1152), (PROJECT_AT, 128), (UP_AT, 96), (DOWN_AT, 48), (FIRST_AT, 32))
SHAPES = ((1152, 128), (128, 128), (4, 6, 4, 128), (3, 4, 4, 128), (3, 3, 3, 128))


def final_kernel(chunk, rows, back_ref, pred_ref, own_ref, first_ref, last_ref, out_ref, *grads):
    step = pl.program_id(0)

    @pl.when(step == 0)
    def _():
        for (start, size), grad in zip(PARTS, grads):
            pieces = []
            at = start
            while at < start + size:
                t = at // chunk
                stop = min((t + 1) * chunk, start + size)
                pieces.append(back_ref[t, at - t * chunk : stop - t * chunk, :].astype(F32))
                at = stop
            whole = jnp.concatenate(pieces, axis=0) if len(pieces) > 1 else pieces[0]
            if len(grad.shape) == 2:
                grad[...] = whole
            else:
                group = grad.shape[2]
                for i in range(grad.shape[0]):
                    for j in range(grad.shape[1]):
                        at = (i * grad.shape[1] + j) * group
                        grad[i, j] = whole[at : at + group]

    row = lax.broadcasted_iota(jnp.int32, (rows, HALF), 0)
    for s in range(out_ref.shape[0]):
        slot = step * out_ref.shape[0] + s
        ahead = back_ref[slot, chunk : chunk + 16, :].astype(F32)
        base = jnp.concatenate([ahead[0:8], ahead[8:16]], axis=1) + own_ref[s]
        for k in range(3):
            for p in range(2):
                for q in range(2):
                    at = ((k * 2 + p) * 2 + q) * rows
                    pick = slice(k * 2 + q, k * 2 + q + 1)
                    edge = (first_ref if p == 0 else last_ref)[s, pick, :]
                    reached = row == (0 if p == 0 else rows - 1)
                    out_ref[s, at : at + rows, :] = (
                        pred_ref[s, at : at + rows, :]
                        + base[pick]
                        + jnp.where(reached, edge, 0.0)
                    ).astype(BF)


def run_final(back, pred, own, first, last):
    slots, main, width = pred.shape
    chunk = back.shape[1] - 16
    held = FINAL_SLOTS if main % 192 == 0 else 2 * FINAL_SLOTS

    def per_slots(array):
        return pl.BlockSpec((held,) + array.shape[1:], lambda n: (n, 0, 0))

    def body(*refs):
        final_kernel(chunk, main // 12, *refs)

    return pl.pallas_call(
        body,
        grid=(slots // held,),
        in_specs=[pl.BlockSpec(back.shape, lambda n: (0, 0, 0))]
        + [per_slots(a) for a in (pred, own, first, last)],
        out_specs=[per_slots(pred)]
        + [pl.BlockSpec(shape, lambda n, dims=len(shape): (0,) * dims) for shape in SHAPES],
        out_shape=[jax.ShapeDtypeStruct(pred.shape, BF)]
        + [jax.ShapeDtypeStruct(shape, F32) for shape in SHAPES],
        compiler_params=pltpu.CompilerParams(vmem_limit_bytes=32 * 1024 * 1024),
    )(back, pred, own, first, last)


def exchanged(value):
    return lax.all_to_all(value, "tile", split_axis=0, concat_axis=0, tiled=True)


def local(
    coarse_solution,
    geometry,
    fine_fields,
    cotangent,
    sample_ids,
    first_weight,
    dilated_weight,
    project_weight,
    down_weight,
    up_weight,
):
    peers = lax.axis_size("tile")
    position = lax.axis_index("tile")
    slots, rows = fine_fields.shape[0], fine_fields.shape[4]
    up = [(i, i + 1) for i in range(peers - 1)]
    down = [(i + 1, i) for i in range(peers - 1)]

    made = constants(rows)
    fine = fine_fields.reshape(slots, 12 * rows, HALF)
    cot = cotangent.reshape(slots, 12 * rows, HALF)

    sent, edge_last, edge_first = run_early(
        peers,
        coarse_solution,
        geometry,
        fine,
        cot,
        jnp.asarray(made["early_x"], BF),
        jnp.asarray(made["early_s"], BF),
    )
    coarse = exchanged(sent)
    from_before = lax.ppermute(edge_last, "tile", up)
    from_after = lax.ppermute(edge_first, "tile", down)
    sums = coarse[:, SENT_INPUT:].astype(F32)
    sums = sums[:, :16] + sums[:, 16:]
    order = lax.broadcasted_iota(jnp.int32, (peers, peers), 0)
    other = lax.broadcasted_iota(jnp.int32, (peers, peers), 1)
    behind = jnp.sum(jnp.where((other > order)[:, :, None, None], sums[None], 0.0), axis=1)
    later = exchanged(behind)

    fixed = [
        jnp.asarray(made["sel_x"], BF),
        jnp.asarray(made["sel_s"], BF),
        jnp.asarray(made["sel_o"], BF),
        jnp.asarray(made["ex"], BF),
        jnp.asarray(made["eu"], BF),
        jnp.asarray(made["ext"], BF),
        jnp.asarray(made["eut"], BF),
        jnp.asarray(made["ef"], BF),
        jnp.asarray(made["eft"], BF),
        jnp.asarray(made["pool_both"], BF),
    ]
    second = dilated_weight
    up_flat = up_weight.reshape(96, 128)
    weights = [
        jnp.pad(first_weight.reshape(27, 128), ((0, 5), (0, 0))).T,
        jnp.transpose(second, (1, 3, 0, 2)).reshape(384, 384),
        jnp.transpose(second, (0, 2, 1, 3)).reshape(384, 384),
        project_weight,
        project_weight.T,
        down_weight.reshape(48, 128).T,
        up_flat.T,
        up_flat,
    ]
    pred_local, last_edge, first_edge, own, sent = run_slots(
        peers,
        sample_ids,
        position.reshape(1).astype(jnp.int32),
        coarse,
        fine,
        cot,
        from_before,
        from_after,
        later,
        fixed,
        weights,
    )

    chunk = GRAD_ROWS // peers
    got = exchanged(sent).astype(F32)
    to_first = lax.ppermute(first_edge, "tile", up)
    to_last = lax.ppermute(last_edge, "tile", down)
    reduced = jnp.sum(got[:, :chunk], axis=0).astype(BF)
    sums = got[:, chunk:]
    ahead = jnp.sum(jnp.where((other < order)[:, :, None, None], sums[None], 0.0), axis=1)
    reduced, to_first, to_last = lax.optimization_barrier((reduced, to_first, to_last))
    back = exchanged(
        jnp.concatenate(
            [
                jnp.broadcast_to(reduced, (peers, chunk, 128)),
                ahead.astype(BF),
            ],
            axis=1,
        )
    )
    prediction, dilated, project, up_grad, down_grad, first = run_final(
        back, pred_local, own, to_first, to_last
    )
    return (
        prediction.reshape(fine_fields.shape),
        first,
        dilated.reshape(dilated_weight.shape),
        project,
        down_grad,
        jnp.swapaxes(up_grad, 1, 2),
    )


def solution(mesh):
    in_specs = (
        P(("groups", "tile"), None, None),
        P(("groups", "tile"), None),
        P("groups", None, None, None, "tile", None),
        P("groups", None, None, None, "tile", None),
        P("groups"),
        P(),
        P(),
        P(),
        P(),
        P(),
    )
    out_specs = (
        P("groups", None, None, None, "tile", None),
        P("groups", None, None, None),
        P("groups", None, None, None),
        P("groups", None),
        P("groups", None, None, None),
        P("groups", None, None, None),
    )
    return jax.shard_map(local, mesh=mesh, in_specs=in_specs, out_specs=out_specs, check_vma=False)
```
